128 devices in a mesh: seq: 4 (over z_lo, core), fsdp: 32 (over y, z_hi, x).
Axes of the slice: x: 4, y: 4, z: 4 (z_hi: 2, z_lo: 2; z = z_hi * 2 + z_lo), core: 2. Of those that a mesh axis runs over, the one named last changes fastest.
Arguments:
- tokens: bfloat16 [32, 1024, 1024], P('fsdp', 'seq'), may hold values from -6 to 6
- triple: bfloat16 [1024, 3072], P('fsdp'), may hold values from -0.25 to 0.25
- triple_bias: bfloat16 [3072], P('fsdp'), may hold values from -1.796875 to 1.796875
- merger: bfloat16 [1024, 1024], P('fsdp'), may hold values from -0.75 to 0.75
- merger_bias: bfloat16 [1024], P('fsdp'), may hold values from -1.796875 to 1.796875
- first_gain: bfloat16 [1024], P('fsdp'), may hold values from 0.25 to 1.75
- first_shift: bfloat16 [1024], P('fsdp'), may hold values from -1.796875 to 1.796875
- expand: bfloat16 [1024, 4096], P('fsdp'), may hold values from -0.1875 to 0.1875
- expand_bias: bfloat16 [4096], P('fsdp'), may hold values from -1.796875 to 1.796875
- shrink: bfloat16 [4096, 1024], P('fsdp'), may hold values from -0.09375 to 0.09375
- shrink_bias: bfloat16 [1024], P('fsdp'), may hold values from -1.796875 to 1.796875
- second_gain: bfloat16 [1024], P('fsdp'), may hold values from 0.25 to 1.75
- second_shift: bfloat16 [1024], P('fsdp'), may hold values from -1.796875 to 1.796875
- cotangent: bfloat16 [32, 1024, 1024], P('fsdp', 'seq'), may hold values from -6 to 6
Outputs:
- encoded: bfloat16 [32, 1024, 1024], P('fsdp', 'seq')
- tokens_grad: bfloat16 [32, 1024, 1024], P('fsdp', 'seq')
- triple_grad: float32 [1024, 3072], P('fsdp')
- triple_bias_grad: float32 [3072], P('fsdp')
- merger_grad: float32 [1024, 1024], P('fsdp')
- merger_bias_grad: float32 [1024], P('fsdp')
- first_gain_grad: float32 [1024], P('fsdp')
- first_shift_grad: float32 [1024], P('fsdp')
- expand_grad: float32 [1024, 4096], P('fsdp')
- expand_bias_grad: float32 [4096], P('fsdp')
- shrink_grad: float32 [4096, 1024], P('fsdp')
- shrink_bias_grad: float32 [1024], P('fsdp')
- second_gain_grad: float32 [1024], P('fsdp')
- second_shift_grad: float32 [1024], P('fsdp')
The draws below stay inside these ranges and needn't reach their ends.
All inputs are finite; a program needn't handle non-finite values.
Results may differ from the reference program's by a relative error of at most 0.025.
Values may be sent and summed in bfloat16 or wider, within the bound.
A program may use at most 192 MiB of HBM per device.

```python
import math
import jax
import jax.numpy as jnp
from jax import lax

D = 1024
HEADS = 16
FF = 4096
SEQS = 32
LENGTH = 1024


def with_spikes(array, key, source, target, blocks, factor):
    def block_of(dim):
        return (jnp.arange(array.shape[dim]) // (array.shape[dim] // blocks)).reshape((-1,) + (1,) * (array.ndim - 1 - dim))

    near = jax.random.permutation(key, blocks)[block_of(target)]
    second = (block_of(target) + blocks // 2) % blocks
    return jnp.where((block_of(source) == near) | (block_of(source) == second), factor * array, array)


def block_scale(key, dims, pieces, least, top_value):
    def one(axis_at, shards_of):
        heights = jax.random.uniform(jax.random.fold_in(jax.random.fold_in(key, 6), axis_at), (shards_of,), jnp.float32, least / len(pieces), top_value / len(pieces))
        return jnp.repeat(jnp.exp(heights), dims[axis_at] // shards_of).reshape((-1,) + (1,) * (len(dims) - axis_at - 1))

    gain = one(*pieces[0])
    for cut in pieces[1:]:
        gain = gain * one(*cut)
    return gain


def scatter_about(stream_key, shape, width, limit, cuts=(), kind=jnp.bfloat16):
    gain = block_scale(stream_key, shape, cuts, -0.22, 0.18) if cuts else 1.0
    result = jax.random.normal(stream_key, shape, jnp.float32) * width * gain
    return jnp.minimum(jnp.maximum(result, -limit), limit).astype(kind)


def bell_draw_with(key, dims, deviation, reach, pieces, heavy, kind=jnp.bfloat16):
    values = deviation * jax.random.normal(key, dims, jnp.float32)
    if pieces:
        values = values * block_scale(key, dims, pieces, -0.22, 0.18)
    return jnp.clip(with_spikes(values, jax.random.fold_in(key, 3), *heavy), -reach, reach).astype(kind)


def setup_inputs(seed: int = 0) -> dict:
    keys = jax.random.split(jax.random.key(seed), 15)
    tokens = bell_draw_with(keys[0], (SEQS, LENGTH, D), 1.0, 6.0, ((0, 32), (1, 4)), (0, 2, 32, 2.75))
    triple = scatter_about(keys[1], (D, 3 * D), (D // 2) ** -0.5, 0.25, ((0, 32),))
    triple_bias = scatter_about(keys[2], (3 * D,), 0.3, 1.796875, ((0, 32),))
    merger = scatter_about(keys[3], (D, D), (D // 16) ** -0.5, 0.75, ((0, 32),))
    merger_bias = scatter_about(keys[4], (D,), 0.3, 1.796875, ((0, 32),))
    first_gain = jnp.clip(1.0 + 0.15 * jax.random.normal(keys[5], (D,), jnp.float32), 0.25, 1.75).astype(jnp.bfloat16)
    first_shift = scatter_about(keys[6], (D,), 0.3, 1.796875, ((0, 32),))
    expand = scatter_about(keys[7], (D, FF), D ** -0.5, 0.1875, ((0, 32),))
    expand_bias = scatter_about(keys[8], (FF,), 0.3, 1.796875, ((0, 32),))
    shrink = scatter_about(keys[9], (FF, D), FF ** -0.5, 0.09375, ((0, 32),))
    shrink_bias = scatter_about(keys[10], (D,), 0.3, 1.796875, ((0, 32),))
    second_gain = jnp.clip(1.0 + 0.15 * jax.random.normal(keys[11], (D,), jnp.float32), 0.25, 1.75).astype(jnp.bfloat16)
    second_shift = scatter_about(keys[12], (D,), 0.3, 1.796875, ((0, 32),))
    cotangent = bell_draw_with(keys[13], (SEQS, LENGTH, D), 1.0, 6.0, ((0, 32), (1, 4)), (0, 2, 32, 2.75))
    return {"tokens": tokens, "triple": triple, "triple_bias": triple_bias, "merger": merger, "merger_bias": merger_bias, "first_gain": first_gain, "first_shift": first_shift, "expand": expand, "expand_bias": expand_bias, "shrink": shrink, "shrink_bias": shrink_bias, "second_gain": second_gain, "second_shift": second_shift, "cotangent": cotangent}


@jax.custom_vjp
def low(v):
    return lax.optimization_barrier(v.astype(jnp.bfloat16)).astype(jnp.float32)

@jax.custom_vjp
def low_back(v):
    return v

def low_keep(v):
    return (low(v), None)

def low_pass(kept, grad):
    return (grad,)

def back_keep(v):
    return (v, None)

def back_low(kept, grad):
    return (low(grad),)
low.defvjp(low_keep, low_pass)
low_back.defvjp(back_keep, back_low)
norm_epsilon = 1e-05
highest = lax.Precision.HIGHEST

def product(left, right):
    return jnp.dot(left, right, precision=highest, preferred_element_type=jnp.float32)

def rotary_tables(positions, head_dim):
    halfway = head_dim // 2
    ladder = jnp.arange(halfway, dtype=jnp.float32)
    inverse = jnp.exp(ladder * (-2.0 * math.log(10000.0) / head_dim))
    angles = positions.astype(jnp.float32)[:, None] * inverse[None, :]
    return (jnp.cos(angles), jnp.sin(angles))

def rotate(heads_block, cosine, sine):
    halfway = heads_block.shape[-1] // 2
    leading = heads_block[..., :halfway]
    trailing = heads_block[..., halfway:]
    cos_wide = cosine[:, None, :]
    sin_wide = sine[:, None, :]
    return jnp.concatenate([leading * cos_wide - trailing * sin_wide, trailing * cos_wide + leading * sin_wide], axis=-1)

def layer_norm(inputs, norm_gain, norm_shift):
    center = lax.optimization_barrier(jnp.mean(inputs, axis=-1, keepdims=True))
    centered = inputs - center
    variance = lax.optimization_barrier(jnp.mean(centered * centered, axis=-1, keepdims=True))
    return centered * lax.rsqrt(variance + norm_epsilon) * norm_gain + norm_shift

def attend(query_rows, keys_all, values_all):
    factor = 1.0 / math.sqrt(D // HEADS)
    scores = low_back(jnp.einsum('qhd,khd->hqk', query_rows, keys_all, precision=highest) * factor)
    peaks = lax.optimization_barrier(jnp.max(scores, axis=-1, keepdims=True))
    powers = jnp.exp(scores - peaks)
    probs = powers / lax.optimization_barrier(jnp.sum(powers, axis=-1, keepdims=True))
    return jnp.einsum('hqk,khd->qhd', low(probs), values_all, precision=highest)

def layer(params, inputs):
    triple, triple_bias, merger, merger_bias, first_gain, first_shift, expand, expand_bias, shrink, shrink_bias, second_gain, second_shift = params
    head_dim = D // HEADS
    positions = jnp.arange(LENGTH, dtype=jnp.int32)
    cosine, sine = rotary_tables(positions, head_dim)
    pre = low_back(product(inputs, triple) + triple_bias)
    split = pre.reshape(LENGTH, 3, HEADS, head_dim)
    queries = low_back(low(rotate(split[:, 0], cosine, sine)))
    keys_all = low_back(low(rotate(split[:, 1], cosine, sine)))
    values_all = low_back(low(split[:, 2]))
    block_rows = min(512, LENGTH)
    blocks = queries.reshape(LENGTH // block_rows, block_rows, HEADS, head_dim)
    context = lax.map(jax.checkpoint(lambda rows_block: attend(rows_block, keys_all, values_all)), blocks)
    context = low_back(low(context.reshape(LENGTH, D)))
    attended = low_back(product(context, merger) + merger_bias)
    hidden = layer_norm(inputs + attended, first_gain, first_shift)
    upward = low_back(product(low(hidden), expand) + expand_bias)
    active = low(jax.nn.gelu(upward, approximate=False))
    feed = low_back(product(active, shrink) + shrink_bias)
    return layer_norm(hidden + feed, second_gain, second_shift)

def reference(tokens, triple, triple_bias, merger, merger_bias, first_gain, first_shift, expand, expand_bias, shrink, shrink_bias, second_gain, second_shift, cotangent):
    params = tuple((weight.astype(jnp.float32) for weight in (triple, triple_bias, merger, merger_bias, first_gain, first_shift, expand, expand_bias, shrink, shrink_bias, second_gain, second_shift)))

    def one_sequence(totals, pair):
        seq_tokens, seq_upstream = pair
        output, pull = jax.vjp(layer, params, seq_tokens.astype(jnp.float32))
        grads, input_grad = pull(seq_upstream.astype(jnp.float32))
        totals = jax.tree.map(lambda left, right: left + right, totals, grads)
        return (totals, (output.astype(jnp.bfloat16), input_grad.astype(jnp.bfloat16)))
    zeros = tuple((jnp.zeros(weight.shape, jnp.float32) for weight in params))
    totals, (encoded, tokens_grad) = lax.scan(one_sequence, zeros, (tokens, cotangent))
    return (encoded, tokens_grad, totals[0], totals[1], totals[2], totals[3], totals[4], totals[5], totals[6], totals[7], totals[8], totals[9], totals[10], totals[11])
```

```python
import functools
import math

import jax
import jax.numpy as jnp
import numpy as np
from jax import lax
from jax.experimental import pallas as pl
from jax.experimental.pallas import tpu as pltpu
from jax.sharding import PartitionSpec as P

HEADS = 16
D = 1024
FF = 4096
LENGTH = 1024
HEAD = 64
bf16 = jnp.bfloat16
f32 = jnp.float32
norm_epsilon = 1e-05
MESH = pl.DeviceIdType.MESH
ANY = pl.BlockSpec(memory_space=pl.ANY)
VMEM = pl.BlockSpec(memory_space=pltpu.VMEM)
SIBLING = [(0, 1), (1, 0), (2, 3), (3, 2)]
ACROSS = [(0, 2), (2, 0), (1, 3), (3, 1)]


class Place:
    def __init__(self):
        seq, fsdp = lax.axis_index("seq"), lax.axis_index("fsdp")
        self.seq, self.fsdp = seq, fsdp
        self.z_lo, self.core = lax.div(seq, 2), lax.rem(seq, 2)
        self.x, rest = lax.rem(fsdp, 4), lax.div(fsdp, 4)
        self.z_hi, self.y = lax.rem(rest, 2), lax.div(rest, 2)

    def at(self, y=None, z_hi=None, x=None, z_lo=None, core=None):
        y = self.y if y is None else y
        z_hi = self.z_hi if z_hi is None else z_hi
        x = self.x if x is None else x
        z_lo = self.z_lo if z_lo is None else z_lo
        core = self.core if core is None else core
        return {"seq": z_lo * 2 + core, "fsdp": (y * 2 + z_hi) * 4 + x}

    def along_x(self, k):
        return lax.rem(self.x + k, 4)

    def along_y(self, k):
        return lax.rem(self.y + k, 4)

    def z_others(self):
        return [
            self.at(z_lo=1 - self.z_lo),
            self.at(z_hi=1 - self.z_hi, z_lo=1 - self.z_lo),
            self.at(z_hi=1 - self.z_hi),
        ]


def meet(peers):
    barrier = pltpu.get_barrier_semaphore()
    for peer in peers:
        pl.semaphore_signal(barrier, inc=1, device_id=peer, device_id_type=MESH)
    pl.semaphore_wait(barrier, len(peers))


class Wires:
    def __init__(self, send, recv):
        self.send, self.recv, self.used, self.open = send, recv, 0, []

    def make(self, source, target, device):
        copy = pltpu.make_async_remote_copy(
            src_ref=source,
            dst_ref=target,
            send_sem=self.send.at[self.used],
            recv_sem=self.recv.at[self.used],
            device_id=device,
            device_id_type=MESH,
        )
        self.used += 1
        return copy

    def go(self, source, target, device):
        copy = self.make(source, target, device)
        copy.start()
        self.open.append(copy)
        return copy

    def drain(self):
        for copy in self.open:
            copy.wait_send()
        self.open = []


def arrive(copies):
    for copy in copies:
        copy.wait_recv()


def gather_first(wires, me, whole):
    half = whole.shape[-1] // 2
    left = whole.at[me.y, :, me.x, :, pl.ds(0, half)]
    right = whole.at[me.y, :, me.x, :, pl.ds(half, half)]
    copies = []
    for k in (1, 3, 2):
        copies.append(wires.go(left, left, me.at(x=me.along_x(k))))
        copies.append(wires.go(right, right, me.at(y=me.along_y(k))))
    return copies


def gather_second(wires, me, whole):
    half = whole.shape[-1] // 2
    left = whole.at[me.y, :, :, :, pl.ds(0, half)]
    right = whole.at[:, :, me.x, :, pl.ds(half, half)]
    copies = []
    for k in (1, 3, 2):
        copies.append(wires.go(left, left, me.at(y=me.along_y(k))))
        copies.append(wires.go(right, right, me.at(x=me.along_x(k))))
    return copies


def gather_kernel(
    triple, expand, shrink, merger, small, tokens, cotangent,
    whole_t, whole_e, whole_s, whole_m, sequence, upstream, small_out,
    small_x, small_y, small_z, sum_x, sum_y, send, recv, local_sems,
):
    me = Place()
    wires = Wires(send, recv)
    sibling = me.at(core=1 - me.core)
    across = me.at(z_lo=1 - me.z_lo)
    partner = me.at(z_hi=1 - me.z_hi, z_lo=1 - me.z_lo)
    peers = [sibling, across, partner]
    peers += [me.at(x=me.along_x(k)) for k in (1, 2, 3)]
    peers += [me.at(y=me.along_y(k)) for k in (1, 2, 3)]
    meet(peers)

    mine_here = me.core == me.z_hi
    slot_t = whole_t.at[me.y, me.z_hi, me.x]
    slot_e = whole_e.at[me.y, me.z_hi, me.x]
    slot_s = whole_s.at[me.y, 0, me.x]
    slot_m = whole_m.at[me.y, 0, me.x]
    own = [
        pltpu.make_async_copy(triple.at[me.z_lo, me.core], slot_t, local_sems.at[0]),
        pltpu.make_async_copy(expand.at[me.core], slot_e, local_sems.at[1]),
        pltpu.make_async_copy(tokens, sequence.at[me.seq], local_sems.at[2]),
        pltpu.make_async_copy(cotangent, upstream.at[me.core], local_sems.at[3]),
    ]
    own_s = pltpu.make_async_copy(shrink, slot_s, local_sems.at[4])
    own_m = pltpu.make_async_copy(merger, slot_m, local_sems.at[5])

    z_t = wires.go(triple.at[1 - me.z_lo, me.core], slot_t, partner)
    x_small = [wires.go(small, small_x.at[k - 1], me.at(x=me.along_x(k))) for k in (1, 2, 3)]
    z_e = wires.go(expand.at[me.core], slot_e, partner)
    tok_across = wires.go(tokens, sequence.at[me.seq], across)
    tok_beside = wires.go(tokens, sequence.at[me.seq], sibling)
    cot_beside = wires.go(cotangent, upstream.at[me.core], sibling)
    z_s = wires.make(shrink, slot_s, partner)
    z_m = wires.make(merger, slot_m, partner)
    for copy in own:
        copy.start()

    @pl.when(mine_here)
    def _():
        z_s.start()
        z_m.start()
        own_s.start()
        own_m.start()

    own[0].wait()
    z_t.wait_recv()
    first_t = gather_first(wires, me, whole_t)
    arrive(x_small)
    sum_x[...] = small[...] + small_x[0] + small_x[1] + small_x[2]
    y_small = [wires.go(sum_x, small_y.at[k - 1], me.at(y=me.along_y(k))) for k in (1, 2, 3)]
    arrive(first_t)
    second_t = gather_second(wires, me, whole_t)
    arrive(y_small)
    sum_y[...] = sum_x[...] + small_y[0] + small_y[1] + small_y[2]
    z_small = wires.go(sum_y, small_z, partner)

    own[1].wait()
    z_e.wait_recv()
    first_e = gather_first(wires, me, whole_e)

    @pl.when(mine_here)
    def _():
        own_s.wait()
        own_m.wait()

    @pl.when(jnp.logical_not(mine_here))
    def _():
        z_s.wait_recv()
        z_m.wait_recv()

    first_s = gather_first(wires, me, whole_s)
    first_m = gather_first(wires, me, whole_m)
    tok_across.wait_recv()
    far = sequence.at[(1 - me.z_lo) * 2 + me.core]
    tok_relay = wires.go(far, far, sibling)
    z_small.wait_recv()
    small_out[...] = sum_y[...] + small_z[...]
    arrive(second_t)
    arrive(first_m)
    second_m = gather_second(wires, me, whole_m)
    arrive(first_e)
    second_e = gather_second(wires, me, whole_e)
    arrive(first_s)
    second_s = gather_second(wires, me, whole_s)
    arrive(second_m)
    arrive(second_e)
    arrive(second_s)
    arrive([tok_beside, cot_beside, tok_relay])
    own[2].wait()
    own[3].wait()
    wires.drain()

    @pl.when(mine_here)
    def _():
        z_s.wait_send()
        z_m.wait_send()


def gather_all(triple, expand, shrink, merger, small, tokens, cotangent):
    shapes = [
        jax.ShapeDtypeStruct((4, 2, 4, 32, 768), bf16),
        jax.ShapeDtypeStruct((4, 2, 4, 32, 2048), bf16),
        jax.ShapeDtypeStruct((4, 1, 4, 128, 1024), bf16),
        jax.ShapeDtypeStruct((4, 1, 4, 32, 1024), bf16),
        jax.ShapeDtypeStruct((4, 256, 1024), bf16),
        jax.ShapeDtypeStruct((2, 256, 1024), bf16),
        jax.ShapeDtypeStruct((16, 1024), f32),
    ]
    return pl.pallas_call(
        gather_kernel,
        out_shape=shapes,
        in_specs=[ANY, ANY, ANY, ANY, VMEM, ANY, ANY],
        out_specs=[ANY] * 6 + [VMEM],
        scratch_shapes=[
            pltpu.VMEM((3, 16, 1024), f32),
            pltpu.VMEM((3, 16, 1024), f32),
            pltpu.VMEM((16, 1024), f32),
            pltpu.VMEM((16, 1024), f32),
            pltpu.VMEM((16, 1024), f32),
            pltpu.SemaphoreType.DMA((64,)),
            pltpu.SemaphoreType.DMA((64,)),
            pltpu.SemaphoreType.DMA((6,)),
        ],
        compiler_params=pltpu.CompilerParams(
            collective_id=0, has_side_effects=True, vmem_limit_bytes=16 << 20
        ),
        name="gather",
    )(triple, expand, shrink, merger, small, tokens, cotangent)


class Reduce:
    def __init__(self, wires, me, grad, hop_l, hop_r, mid_l, mid_r, last_l, last_r, out):
        self.wires, self.me, self.grad, self.out = wires, me, grad, out
        self.hop_l, self.hop_r, self.mid_l, self.mid_r = hop_l, hop_r, mid_l, mid_r
        self.last_l, self.last_r = last_l, last_r
        self.levels, self.half = grad.shape[1], grad.shape[4] // 2

    def first(self):
        me, half = self.me, self.half
        self.one_l, self.one_r = [], []
        for k in (1, 3, 2):
            to_x, to_y = me.along_x(k), me.along_y(k)
            self.one_l.append(
                self.wires.go(
                    self.grad.at[:, :, to_x, :, pl.ds(0, half)], self.hop_l.at[k - 1], me.at(x=to_x)
                )
            )
            self.one_r.append(
                self.wires.go(
                    self.grad.at[to_y, :, :, :, pl.ds(half, half)], self.hop_r.at[k - 1], me.at(y=to_y)
                )
            )

    def second(self):
        me, half, levels = self.me, self.half, self.levels
        self.two_l, self.two_r = [], []
        arrive(self.one_l)

        def left(i, carry):
            y, level = lax.div(i, levels), lax.rem(i, levels)
            total = self.grad[y, level, me.x, :, pl.ds(0, half)].astype(f32)
            for k in range(3):
                total += self.hop_l[k, y, level].astype(f32)
            self.mid_l[y, level] = total.astype(bf16)
            return carry

        lax.fori_loop(0, 4 * levels, left, 0)
        for k in (1, 3, 2):
            to_y = me.along_y(k)
            self.two_l.append(
                self.wires.go(self.mid_l.at[to_y], self.last_l.at[k - 1], me.at(y=to_y))
            )
        arrive(self.one_r)

        def right(i, carry):
            level, x = lax.div(i, 4), lax.rem(i, 4)
            total = self.grad[me.y, level, x, :, pl.ds(half, half)].astype(f32)
            for k in range(3):
                total += self.hop_r[k, level, x].astype(f32)
            self.mid_r[level, x] = total.astype(bf16)
            return carry

        lax.fori_loop(0, 4 * levels, right, 0)
        for k in (1, 3, 2):
            to_x = me.along_x(k)
            self.two_r.append(
                self.wires.go(self.mid_r.at[:, to_x], self.last_r.at[k - 1], me.at(x=to_x))
            )

    def third(self):
        me, half = self.me, self.half
        arrive(self.two_l)
        for level in range(self.levels):
            total = self.mid_l[me.y, level].astype(f32)
            for k in range(3):
                total += self.last_l[k, level].astype(f32)
            self.out[level, :, pl.ds(0, half)] = total.astype(bf16)
        arrive(self.two_r)
        for level in range(self.levels):
            total = self.mid_r[level, me.x].astype(f32)
            for k in range(3):
                total += self.last_r[k, level].astype(f32)
            self.out[level, :, pl.ds(half, half)] = total.astype(bf16)


def reduce_scratch(levels, rows, columns):
    half = columns // 2
    return [
        pltpu.VMEM((3, 4, levels, rows, half), bf16),
        pltpu.VMEM((3, levels, 4, rows, half), bf16),
        pltpu.VMEM((4, levels, rows, half), bf16),
        pltpu.VMEM((levels, 4, rows, half), bf16),
        pltpu.VMEM((3, levels, rows, half), bf16),
        pltpu.VMEM((3, levels, rows, half), bf16),
        pltpu.VMEM((levels, rows, columns), bf16),
    ]


def reduce_kernel(
    grad_s, grad_e, grad_m, grad_t, small,
    out_s, out_e, out_m, out_t, small_out, *rest,
):
    me = Place()
    scratch_s, scratch_e, scratch_m, scratch_t = (rest[7 * i : 7 * i + 7] for i in range(4))
    z_s, z_e, z_m, z_t, small_x, small_y, small_z, small_c, sums, send, recv = rest[28:]
    wires = Wires(send, recv)
    sibling = me.at(core=1 - me.core)
    beside, diagonal, beyond = me.z_others()
    peers = [sibling, beside, diagonal, beyond, me.at(z_lo=1 - me.z_lo, core=1 - me.core)]
    peers += [me.at(x=me.along_x(k)) for k in (1, 2, 3)]
    peers += [me.at(y=me.along_y(k)) for k in (1, 2, 3)]
    meet(peers)
    jobs = [
        Reduce(wires, me, grad, *scratch)
        for grad, scratch in (
            (grad_s, scratch_s), (grad_e, scratch_e), (grad_m, scratch_m), (grad_t, scratch_t)
        )
    ]
    got = [wires.go(small, small_x.at[k - 1], me.at(x=me.along_x(k))) for k in (1, 2, 3)]
    for job in jobs:
        job.first()
    arrive(got)
    sums[0] = small[...] + small_x[0] + small_x[1] + small_x[2]
    got = [wires.go(sums.at[0], small_y.at[k - 1], me.at(y=me.along_y(k))) for k in (1, 2, 3)]
    jobs[0].second()
    arrive(got)
    sums[1] = sums[0] + small_y[0] + small_y[1] + small_y[2]
    got = [wires.go(sums.at[1], small_z.at[k], peer) for k, peer in enumerate((beside, diagonal, beyond))]
    jobs[1].second()
    arrive(got)
    sums[2] = sums[1] + small_z[0] + small_z[1] + small_z[2]
    got = wires.go(sums.at[2], small_c, sibling)
    jobs[2].second()
    jobs[3].second()
    got.wait_recv()
    small_out[...] = sums[2] + small_c[...]

    owner = me.core == me.z_hi
    plane_s, plane_e, plane_m, plane_t = (job.out for job in jobs)
    late = []

    def to_owners(plane, slots):
        copies = [
            wires.make(plane.at[0], slots.at[k], peer)
            for k, peer in enumerate((beside, diagonal, beyond))
        ]

        @pl.when(owner)
        def _():
            copies[0].start()

        @pl.when(jnp.logical_not(owner))
        def _():
            copies[1].start()
            copies[2].start()

        late.append(copies)
        return copies

    def finish_owned(plane, slots, copies, out):
        beside_copy = wires.make(out, out, sibling)

        @pl.when(owner)
        def _():
            arrive(copies)
            total = plane[0].astype(f32)
            for k in range(3):
                total += slots[k].astype(f32)
            out[...] = total.astype(bf16)
            beside_copy.start()

        return beside_copy

    jobs[0].third()
    copies_s = to_owners(plane_s, z_s)
    jobs[1].third()
    other = 1 - me.z_hi
    copies_e = [
        wires.go(plane_e.at[level], z_e.at[k], peer)
        for k, (level, peer) in enumerate(((me.z_hi, beside), (other, diagonal), (other, beyond)))
    ]
    jobs[2].third()
    copies_m = to_owners(plane_m, z_m)
    jobs[3].third()
    copy_t = wires.go(plane_t.at[other], z_t, beyond)
    beside_s = finish_owned(plane_s, z_s, copies_s, out_s)
    arrive(copies_e)
    total = plane_e[me.z_hi].astype(f32)
    for k in range(3):
        total += z_e[k].astype(f32)
    out_e[me.core] = total.astype(bf16)
    beside_e = wires.go(out_e.at[me.core], out_e.at[me.core], sibling)
    beside_m = finish_owned(plane_m, z_m, copies_m, out_m)
    copy_t.wait_recv()
    out_t[me.seq] = (plane_t[me.z_hi].astype(f32) + z_t[...].astype(f32)).astype(bf16)
    spread = [
        wires.go(out_t.at[me.seq], out_t.at[me.seq], peer)
        for peer in (sibling, beside, me.at(z_lo=1 - me.z_lo, core=1 - me.core))
    ]

    @pl.when(jnp.logical_not(owner))
    def _():
        beside_s.wait_recv()
        beside_m.wait_recv()
        for copies in late:
            copies[1].wait_send()
            copies[2].wait_send()

    @pl.when(owner)
    def _():
        beside_s.wait_send()
        beside_m.wait_send()
        for copies in late:
            copies[0].wait_send()

    arrive(spread)
    beside_e.wait_recv()
    wires.drain()


def reduce_all(grad_s, grad_e, grad_m, grad_t, small):
    shapes = [
        jax.ShapeDtypeStruct((128, 1024), bf16),
        jax.ShapeDtypeStruct((2, 32, 2048), bf16),
        jax.ShapeDtypeStruct((32, 1024), bf16),
        jax.ShapeDtypeStruct((4, 32, 768), bf16),
        jax.ShapeDtypeStruct((16, 1024), f32),
    ]
    return pl.pallas_call(
        reduce_kernel,
        out_shape=shapes,
        in_specs=[VMEM] * 5,
        out_specs=[VMEM] * 5,
        scratch_shapes=[
            *reduce_scratch(1, 128, 1024),
            *reduce_scratch(2, 32, 2048),
            *reduce_scratch(1, 32, 1024),
            *reduce_scratch(2, 32, 768),
            pltpu.VMEM((3, 128, 1024), bf16),
            pltpu.VMEM((3, 32, 2048), bf16),
            pltpu.VMEM((3, 32, 1024), bf16),
            pltpu.VMEM((32, 768), bf16),
            pltpu.VMEM((3, 16, 1024), f32),
            pltpu.VMEM((3, 16, 1024), f32),
            pltpu.VMEM((3, 16, 1024), f32),
            pltpu.VMEM((16, 1024), f32),
            pltpu.VMEM((3, 16, 1024), f32),
            pltpu.SemaphoreType.DMA((88,)),
            pltpu.SemaphoreType.DMA((88,)),
        ],
        compiler_params=pltpu.CompilerParams(
            collective_id=1, has_side_effects=True, vmem_limit_bytes=48 << 20
        ),
        name="reduce",
    )(grad_s, grad_e, grad_m, grad_t, small)


def rotary_tables():
    inverse = 10000.0 ** (-2.0 * np.arange(32) / 64)
    angles = np.arange(LENGTH)[:, None] * inverse[None, :]
    return jnp.asarray(np.cos(angles), f32), jnp.asarray(np.sin(angles), f32)


def rotate(block, cosine, sine):
    a, b = block[..., :32], block[..., 32:]
    cosine, sine = cosine[:, None], sine[:, None]
    return jnp.concatenate([a * cosine - b * sine, b * cosine + a * sine], axis=-1)


def normalise(rows):
    centered = rows - jnp.mean(rows, axis=-1, keepdims=True)
    scale = lax.rsqrt(jnp.mean(centered * centered, axis=-1, keepdims=True) + norm_epsilon)
    return centered * scale, scale


def norm_backward(upstream, gain, n, scale):
    u = upstream * gain
    mean = jnp.mean(u, axis=-1, keepdims=True)
    along = jnp.mean(u * n, axis=-1, keepdims=True)
    return scale * (u - mean - n * along)


def swap(x, pairs):
    return lax.ppermute(x, "seq", pairs)


def spread_small(vectors, fsdp):
    rows = []
    for v in vectors:
        n = v.shape[0]
        wide = jnp.tile(v.astype(f32), 32)
        rows.append(jnp.where(lax.iota(jnp.int32, 32 * n) // n == fsdp, wide, 0.0))
    rows.append(jnp.zeros((3 * 1024,), f32))
    return jnp.concatenate(rows).reshape(16, 1024)


def mm(a, b, dims, out=f32):
    return lax.dot_general(a, b, (dims, ((), ())), preferred_element_type=f32).astype(out)


NN = ((1,), (0,))
NT = ((1,), (1,))
TN = ((0,), (0,))


def local(
    tokens, triple, triple_bias, merger, merger_bias, first_gain, first_shift,
    expand, expand_bias, shrink, shrink_bias, second_gain, second_shift, cotangent,
):
    me = Place()
    triple_cut = triple.reshape(32, 3, 2, 2, 2, 128).transpose(2, 4, 0, 1, 3, 5).reshape(2, 2, 32, 768)
    expand_cut = expand.reshape(32, 4, 2, 512).transpose(2, 0, 1, 3).reshape(2, 32, 2048)
    small = spread_small(
        (triple_bias, merger_bias, first_gain, first_shift, expand_bias, shrink_bias, second_gain, second_shift),
        me.fsdp,
    )
    whole_t, whole_e, whole_s, whole_m, sequence, upstream, small = gather_all(
        triple_cut, expand_cut, shrink, merger, small, tokens.reshape(256, D), cotangent.reshape(256, D)
    )
    whole_t = whole_t.reshape(D, 768)
    whole_e = whole_e.reshape(D, 2048)
    whole_s = whole_s.reshape(2048, D)
    whole_m = whole_m.reshape(512, D)
    sequence = sequence.reshape(LENGTH, D)
    upstream = upstream.reshape(512, D).astype(f32)
    bias_t = lax.dynamic_slice(
        small[0:3].reshape(3, 2, 2, 2, 128), (0, me.z_lo, 0, me.core, 0), (3, 1, 2, 1, 128)
    ).reshape(1, 768)
    bias_m, gain_1, shift_1 = small[3:4], small[4:5], small[5:6]
    bias_e = lax.dynamic_slice(small[6:10].reshape(4, 2, 512), (0, me.core, 0), (4, 1, 512)).reshape(1, 2048)
    bias_s, gain_2, shift_2 = small[10:11], small[11:12], small[12:13]

    pre = (mm(sequence, whole_t, NN) + bias_t).reshape(LENGTH, 3, 4, HEAD)
    cosine, sine = rotary_tables()
    q = rotate(pre[:, 0], cosine, sine).astype(bf16).transpose(1, 0, 2)
    k = rotate(pre[:, 1], cosine, sine).astype(bf16).transpose(1, 0, 2)
    v = pre[:, 2].astype(bf16).transpose(1, 0, 2)
    scores = jnp.einsum("hqd,hkd->hqk", q, k, preferred_element_type=f32) * 0.125
    probs = jnp.exp(scores - jnp.max(scores, axis=-1, keepdims=True))
    probs = (probs / jnp.sum(probs, axis=-1, keepdims=True)).astype(bf16)
    context = jnp.einsum("hqk,hkd->qhd", probs, v, preferred_element_type=f32).astype(bf16)
    context = context.reshape(LENGTH, 256)

    chip_rows = me.z_lo * 512
    mine = lax.dynamic_slice(context, (chip_rows, 0), (512, 256))
    theirs = swap(lax.dynamic_slice(context, (512 - chip_rows, 0), (512, 256)), ACROSS)
    first_chip = me.z_lo == 0
    ctx = jnp.concatenate([jnp.where(first_chip, mine, theirs), jnp.where(first_chip, theirs, mine)], axis=1)
    part = mm(ctx, whole_m, NN)
    attended = part + swap(part.astype(bf16), SIBLING).astype(f32) + bias_m
    rows_in = lax.dynamic_slice(sequence, (chip_rows, 0), (512, D)).astype(f32)
    n_1, scale_1 = normalise(rows_in + attended)
    hidden = n_1 * gain_1 + shift_1
    low = hidden.astype(bf16)
    upward = mm(low, whole_e, NN) + bias_e
    gate = 0.5 * (1.0 + lax.erf(upward * math.sqrt(0.5)))
    active = (upward * gate).astype(bf16)
    slope = gate + upward * jnp.exp(-0.5 * upward * upward) * (1.0 / math.sqrt(2.0 * math.pi))
    part = mm(active, whole_s, NN)
    feed = part + swap(part.astype(bf16), SIBLING).astype(f32) + bias_s
    n_2, scale_2 = normalise(hidden + feed)
    own_rows = me.core * 256

    def own(rows):
        return lax.dynamic_slice(rows, (own_rows, 0), (256, rows.shape[1]))

    encoded = own(n_2 * gain_2 + shift_2).astype(bf16)
    gain_2_grad = jnp.sum(own(upstream * n_2), axis=0)
    shift_2_grad = jnp.sum(own(upstream), axis=0)
    second_grad = norm_backward(upstream, gain_2, n_2, scale_2)
    feed_grad = second_grad.astype(bf16)
    bias_s_grad = jnp.sum(own(feed_grad).astype(f32), axis=0)
    grad_s = mm(active, feed_grad, TN, bf16)
    up_grad = (mm(feed_grad, whole_s, NT) * slope).astype(bf16)
    grad_e = mm(low, up_grad, TN, bf16)
    bias_e_grad = jnp.sum(up_grad.astype(f32), axis=0)
    part = mm(up_grad, whole_e, NT)
    hidden_grad = part + swap(part.astype(bf16), SIBLING).astype(f32) + second_grad
    gain_1_grad = jnp.sum(own(hidden_grad * n_1), axis=0)
    shift_1_grad = jnp.sum(own(hidden_grad), axis=0)
    first_grad = norm_backward(hidden_grad, gain_1, n_1, scale_1)
    attended_grad = first_grad.astype(bf16)
    bias_m_grad = jnp.sum(own(attended_grad).astype(f32), axis=0)
    grad_m = mm(ctx, attended_grad, TN, bf16)
    ctx_grad = mm(attended_grad, whole_m, NT, bf16)

    left, right = ctx_grad[:, :256], ctx_grad[:, 256:]
    mine = jnp.where(first_chip, left, right)
    theirs = swap(jnp.where(first_chip, right, left), ACROSS)
    context_grad = jnp.concatenate(
        [jnp.where(first_chip, mine, theirs), jnp.where(first_chip, theirs, mine)], axis=0
    )
    out_grad = context_grad.reshape(LENGTH, 4, HEAD)
    delta = jnp.sum(out_grad.astype(f32) * context.reshape(LENGTH, 4, HEAD).astype(f32), axis=-1)
    prob_grad = jnp.einsum("qhd,hkd->hqk", out_grad, v, preferred_element_type=f32)
    score_grad = (probs.astype(f32) * (prob_grad - delta.T[..., None])).astype(bf16)
    q_grad = jnp.einsum("hqk,hkd->qhd", score_grad, k, preferred_element_type=f32) * 0.125
    k_grad = jnp.einsum("hqk,hqd->khd", score_grad, q, preferred_element_type=f32) * 0.125
    v_grad = jnp.einsum("hqk,qhd->khd", probs, out_grad, preferred_element_type=f32)
    pre_grad = jnp.concatenate(
        [
            rotate(q_grad, cosine, -sine).reshape(LENGTH, 256),
            rotate(k_grad, cosine, -sine).reshape(LENGTH, 256),
            v_grad.reshape(LENGTH, 256),
        ],
        axis=1,
    ).astype(bf16)
    grad_t = mm(sequence, pre_grad, TN, bf16)
    bias_t_grad = jnp.sum(pre_grad.astype(f32), axis=0)
    part = mm(pre_grad, whole_t, NT).reshape(2, 2, 256, D)
    kept = lax.dynamic_index_in_dim(part, me.core, 1, False)
    given = lax.dynamic_index_in_dim(part, 1 - me.core, 1, False).astype(bf16)
    kept = kept + swap(given, SIBLING).astype(f32)
    given = lax.dynamic_index_in_dim(kept, 1 - me.z_lo, 0, False).astype(bf16)
    kept = lax.dynamic_index_in_dim(kept, me.z_lo, 0, False) + swap(given, ACROSS).astype(f32)
    tokens_grad = (kept + own(first_grad)).astype(bf16)

    bias_t_wide = lax.dynamic_update_slice(
        jnp.zeros((3, 2, 2, 2, 128), f32), bias_t_grad.reshape(3, 1, 2, 1, 128), (0, me.z_lo, 0, me.core, 0)
    ).reshape(3072)
    bias_e_wide = lax.dynamic_update_slice(
        jnp.zeros((4, 2, 512), f32), bias_e_grad.reshape(4, 1, 512), (0, me.core, 0)
    ).reshape(4096)
    small_grad = jnp.concatenate(
        [
            bias_t_wide, bias_m_grad, gain_1_grad, shift_1_grad, bias_e_wide, bias_s_grad,
            gain_2_grad, shift_2_grad, jnp.zeros((3072,), f32),
        ]
    ).reshape(16, 1024)
    sum_s, sum_e, sum_m, sum_t, small_sum = reduce_all(
        grad_s.reshape(4, 1, 4, 128, 1024), grad_e.reshape(4, 2, 4, 32, 2048),
        grad_m.reshape(4, 1, 4, 32, 1024), grad_t.reshape(4, 2, 4, 32, 768), small_grad,
    )
    triple_grad = (
        sum_t.reshape(2, 2, 32, 3, 2, 128).transpose(2, 3, 0, 4, 1, 5).reshape(32, 3072).astype(f32)
    )
    expand_grad = sum_e.reshape(2, 32, 4, 512).transpose(1, 2, 0, 3).reshape(32, 4096).astype(f32)
    flat = small_sum.reshape(-1)

    def shard(start, n):
        return lax.dynamic_slice(flat, (start + me.fsdp * n,), (n,))

    return (
        encoded.reshape(1, 256, D),
        tokens_grad.reshape(1, 256, D),
        triple_grad,
        shard(0, 96),
        sum_m.astype(f32),
        shard(3072, 32),
        shard(4096, 32),
        shard(5120, 32),
        expand_grad,
        shard(6144, 128),
        sum_s.astype(f32),
        shard(10240, 32),
        shard(11264, 32),
        shard(12288, 32),
    )


def solution(mesh):
    rows = P("fsdp", "seq", None)
    matrix = P("fsdp", None)
    vector = P("fsdp")
    return jax.shard_map(
        local,
        mesh=mesh,
        in_specs=(
            rows, matrix, vector, matrix, vector, vector, vector, matrix, vector, matrix, vector,
            vector, vector, rows,
        ),
        out_specs=(
            rows, rows, matrix, vector, matrix, vector, vector, vector, matrix, vector, matrix,
            vector, vector, vector,
        ),
        check_vma=False,
    )
```

```python
import functools
import math

import jax
import jax.numpy as jnp
import numpy as np
from jax import lax
from jax.experimental import pallas as pl
from jax.experimental.pallas import tpu as pltpu
from jax.sharding import PartitionSpec as P

HEADS = 16
D = 1024
FF = 4096
LENGTH = 1024
HEAD = 64
bf16 = jnp.bfloat16
f32 = jnp.float32
norm_epsilon = 1e-05
MESH = pl.DeviceIdType.MESH
ANY = pl.BlockSpec(memory_space=pl.ANY)
VMEM = pl.BlockSpec(memory_space=pltpu.VMEM)
SIBLING = [(0, 1), (1, 0), (2, 3), (3, 2)]
ACROSS = [(0, 2), (2, 0), (1, 3), (3, 1)]


class Place:
    def __init__(self):
        seq, fsdp = lax.axis_index("seq"), lax.axis_index("fsdp")
        self.seq, self.fsdp = seq, fsdp
        self.z_lo, self.core = lax.div(seq, 2), lax.rem(seq, 2)
        self.x, rest = lax.rem(fsdp, 4), lax.div(fsdp, 4)
        self.z_hi, self.y = lax.rem(rest, 2), lax.div(rest, 2)

    def at(self, y=None, z_hi=None, x=None, z_lo=None, core=None):
        y = self.y if y is None else y
        z_hi = self.z_hi if z_hi is None else z_hi
        x = self.x if x is None else x
        z_lo = self.z_lo if z_lo is None else z_lo
        core = self.core if core is None else core
        return {"seq": z_lo * 2 + core, "fsdp": (y * 2 + z_hi) * 4 + x}

    def along_x(self, k):
        return lax.rem(self.x + k, 4)

    def along_y(self, k):
        return lax.rem(self.y + k, 4)

    def z_others(self):
        return [
            self.at(z_lo=1 - self.z_lo),
            self.at(z_hi=1 - self.z_hi, z_lo=1 - self.z_lo),
            self.at(z_hi=1 - self.z_hi),
        ]


def meet(peers):
    barrier = pltpu.get_barrier_semaphore()
    for peer in peers:
        pl.semaphore_signal(barrier, inc=1, device_id=peer, device_id_type=MESH)
    pl.semaphore_wait(barrier, len(peers))


class Wires:
    def __init__(self, send, recv):
        self.send, self.recv, self.used, self.open = send, recv, 0, []

    def make(self, source, target, device):
        assert self.used < self.send.shape[0]
        copy = pltpu.make_async_remote_copy(
            src_ref=source,
            dst_ref=target,
            send_sem=self.send.at[self.used],
            recv_sem=self.recv.at[self.used],
            device_id=device,
            device_id_type=MESH,
        )
        self.used += 1
        return copy

    def go(self, source, target, device):
        copy = self.make(source, target, device)
        copy.start()
        self.open.append(copy)
        return copy

    def drain(self):
        for copy in self.open:
            copy.wait_send()
        self.open = []


def arrive(copies):
    for copy in copies:
        copy.wait_recv()


def gather_steps(wires, me, whole):
    half = whole.shape[-1] // 2
    rows = whole.shape[-2] // 2
    low, high, both = pl.ds(0, rows), pl.ds(rows, rows), pl.ds(0, 2 * rows)
    left, right = pl.ds(0, half), pl.ds(half, half)
    on_x = (me.x, lambda i: me.at(x=i))
    on_y = (me.y, lambda i: me.at(y=i))
    hops = (
        (
            (*on_x, lambda i, r: whole.at[me.y, :, i, r, left]),
            (*on_y, lambda i, r: whole.at[i, :, me.x, r, right]),
        ),
        (
            (*on_y, lambda i, r: whole.at[i, :, :, r, left]),
            (*on_x, lambda i, r: whole.at[:, :, i, r, right]),
        ),
    )
    for hop in hops:
        direct = []
        for here, device, piece in hop:
            up, down = lax.rem(here + 1, 4), lax.rem(here + 3, 4)
            direct.append(
                (
                    wires.go(piece(here, both), piece(here, both), device(up)),
                    wires.go(piece(here, both), piece(here, both), device(down)),
                )
            )
        yield
        relayed = []
        for (here, device, piece), (from_down, from_up) in zip(hop, direct):
            up, down = lax.rem(here + 1, 4), lax.rem(here + 3, 4)
            from_down.wait_recv()
            relayed.append(wires.go(piece(down, low), piece(down, low), device(up)))
            from_up.wait_recv()
            relayed.append(wires.go(piece(up, high), piece(up, high), device(down)))
        yield
        arrive(relayed)
    yield


def dot(a, b, dims):
    return lax.dot_general(a, b, (dims, ((), ())), preferred_element_type=f32)


def turn(block, cosine, sine):
    lane = lax.broadcasted_iota(jnp.int32, block.shape, 1)
    other = jnp.where(
        lax.rem(lane, 64) < 32, pltpu.roll(block, 96, 1), pltpu.roll(block, 32, 1)
    )
    return block * cosine + other * sine


def row_norm(rows):
    centered = rows - jnp.mean(rows, axis=-1, keepdims=True)
    scale = lax.rsqrt(jnp.mean(centered * centered, axis=-1, keepdims=True) + norm_epsilon)
    return centered * scale, scale


def row_norm_backward(upstream, gain, n, scale):
    u = upstream * gain
    mean = jnp.mean(u, axis=-1, keepdims=True)
    along = jnp.mean(u * n, axis=-1, keepdims=True)
    return scale * (u - mean - n * along)


class Saves:
    def __init__(self, sems):
        self.sems, self.used, self.open = sems, 0, []

    def go(self, source, target):
        assert self.used < self.sems.shape[0]
        copy = pltpu.make_async_copy(source, target, self.sems.at[self.used])
        self.used += 1
        copy.start()
        self.open.append(copy)
        return copy

    def wait(self, copy):
        copy.wait()
        self.open = [other for other in self.open if other is not copy]

    def drain(self):
        for copy in self.open:
            copy.wait()
        self.open = []


def forward_kernel(
    triple, expand, shrink, merger, small, tokens, cotangent, cosines, sines,
    whole_t, whole_e, whole_s, whole_m, sequence, small_full, encoded, small_grads,
    e_out, o_out, q_out, k_out, v_out, r_out, ctx_out, n_out, scale_out, low_out,
    active_out, slope_out, second_out, feed_out,
    small_x, small_y, small_z, sum_x, sum_y, wt, we, ws, wm, seq, ups,
    e_buf, o_buf, q_buf, k_buf, v_buf, r_buf, ctx, part, give_a, take_a, give_f, take_f,
    n_buf, scale_buf, low_buf, active_buf, slope_buf, second_buf, feed_buf,
    send, recv, local_sems,
):
    me = Place()
    wires, saves = Wires(send, recv), Saves(local_sems)
    sibling = me.at(core=1 - me.core)
    across = me.at(z_lo=1 - me.z_lo)
    partner = me.at(z_hi=1 - me.z_hi, z_lo=1 - me.z_lo)
    peers = [sibling, across, partner]
    peers += [me.at(x=me.along_x(k)) for k in (1, 2, 3)]
    peers += [me.at(y=me.along_y(k)) for k in (1, 2, 3)]
    meet(peers)

    mine_here = me.core == me.z_hi
    slot_t = whole_t.at[me.y, me.z_hi, me.x]
    slot_e = whole_e.at[me.y, me.z_hi, me.x]
    slot_s = whole_s.at[me.y, 0, me.x]
    slot_m = whole_m.at[me.y, 0, me.x]
    z_t = wires.go(triple.at[1 - me.z_lo, me.core], slot_t, partner)
    tok_across = wires.go(tokens, seq.at[me.seq], across)
    x_small = [wires.go(small, small_x.at[k - 1], me.at(x=me.along_x(k))) for k in (1, 2, 3)]
    tok_beside = wires.go(tokens, seq.at[me.seq], sibling)
    z_e = wires.go(expand.at[me.core], slot_e, partner)
    cot_beside = wires.go(cotangent, ups.at[me.core], sibling)
    own_t = saves.go(triple.at[me.z_lo, me.core], slot_t)
    own_tok = saves.go(tokens, seq.at[me.seq])
    own_e = saves.go(expand.at[me.core], slot_e)
    own_cot = saves.go(cotangent, ups.at[me.core])
    z_s = wires.make(shrink, slot_s, partner)
    z_m = wires.make(merger, slot_m, partner)
    own_s = pltpu.make_async_copy(shrink, slot_s, local_sems.at[40])
    own_m = pltpu.make_async_copy(merger, slot_m, local_sems.at[41])

    @pl.when(mine_here)
    def _():
        z_s.start()
        z_m.start()
        own_s.start()
        own_m.start()

    go_t = gather_steps(wires, me, whole_t)
    go_e = gather_steps(wires, me, whole_e)
    go_s = gather_steps(wires, me, whole_s)
    go_m = gather_steps(wires, me, whole_m)
    saves.wait(own_t)
    z_t.wait_recv()
    next(go_t)
    arrive(x_small)
    sum_x[...] = small[...] + small_x[0] + small_x[1] + small_x[2]
    y_small = [wires.go(sum_x, small_y.at[k - 1], me.at(y=me.along_y(k))) for k in (1, 2, 3)]
    next(go_t)
    arrive(y_small)
    sum_y[...] = sum_x[...] + small_y[0] + small_y[1] + small_y[2]
    z_small = wires.go(sum_y, small_z, partner)
    next(go_t)
    saves.wait(own_e)
    z_e.wait_recv()
    next(go_e)

    @pl.when(mine_here)
    def _():
        own_s.wait()
        own_m.wait()

    @pl.when(jnp.logical_not(mine_here))
    def _():
        z_s.wait_recv()
        z_m.wait_recv()

    next(go_m)
    tok_across.wait_recv()
    far = seq.at[(1 - me.z_lo) * 2 + me.core]
    tok_relay = wires.go(far, far, sibling)
    z_small.wait_recv()
    small_full[...] = sum_y[...] + small_z[...]
    next(go_t)
    next(go_e)
    next(go_m)
    next(go_s)
    next(go_t)
    load_t = saves.go(whole_t, wt)
    next(go_e)
    next(go_m)
    next(go_s)
    saves.wait(own_tok)
    arrive([tok_beside, tok_relay])
    saves.wait(load_t)

    def bias(row, start, n):
        return small_full[pl.ds(row, 1), pl.ds(pl.multiple_of(start, 128), n)]

    bias_t = [
        bias(t, me.z_lo * 512 + j * 256 + me.core * 128, 128) for t in range(3) for j in range(2)
    ]
    bias_t = jnp.concatenate(bias_t, axis=1)

    def project(i, carry):
        rows = pl.ds(pl.multiple_of(i * 256, 256), 256)
        pre = dot(seq[i], wt[...].reshape(D, 768), NN) + bias_t
        cosine, sine = cosines[rows, :], sines[rows, :]
        for p in range(2):
            cut = pre[:, p * 128 : p * 128 + 128]
            q_buf[p, rows, :] = (turn(cut, cosine, sine) * 0.125).astype(bf16)
            cut = pre[:, 256 + p * 128 : 384 + p * 128]
            k_buf[p, rows, :] = turn(cut, cosine, sine).astype(bf16)
            v_buf[p, rows, pl.ds(0, 128)] = pre[:, 512 + p * 128 : 640 + p * 128].astype(bf16)
            v_buf[p, rows, pl.ds(128, 128)] = jnp.ones((256, 128), bf16)
        return carry

    lax.fori_loop(0, 4, project, 0)
    saves.go(seq, sequence)
    saves.go(q_buf, q_out)
    saves.go(k_buf, k_out)
    saves.go(v_buf, v_out)
    next(go_s)
    ctx_copies = []
    for p in range(2):

        def attend(i, carry, p=p):
            rows = pl.ds(pl.multiple_of(i * 256, 256), 256)
            lane = lax.broadcasted_iota(jnp.int32, (256, 128), 1)
            found = []
            for h in range(2):
                head = (lane >= 64) if h else (lane < 64)
                q = jnp.where(head, q_buf[p, rows, :], jnp.zeros((), bf16))
                scores = dot(q, k_buf[p], NT)
                peak = jnp.max(scores, axis=1, keepdims=True)
                powers = jnp.exp(scores - peak).astype(bf16)
                e_buf[2 * p + h, rows, :] = powers
                found.append(dot(powers, v_buf[p], NN))
            first = lane < 64
            over = 1.0 / jnp.where(first, found[0][:, 128:], found[1][:, 128:])
            r_buf[p, rows, :] = over
            o_buf[p, rows, :] = (jnp.where(first, found[0][:, :128], found[1][:, :128]) * over).astype(bf16)
            return carry

        lax.fori_loop(0, 4, attend, 0)
        saves.go(e_buf.at[pl.ds(2 * p, 2)], e_out.at[pl.ds(2 * p, 2)])
        theirs = o_buf.at[p, pl.ds(pl.multiple_of((1 - me.z_lo) * 512, 512), 512)]
        ours = o_buf.at[p, pl.ds(pl.multiple_of(me.z_lo * 512, 512), 512)]
        ctx_copies.append(wires.go(theirs, ctx.at[me.z_lo, p], across))
        keep = saves.go(ours, ctx.at[me.z_lo, p])
        if p == 0:
            next(go_e)
            next(go_m)
            keep_0 = keep
    saves.go(r_buf, r_out)
    saves.go(o_buf, o_out)
    next(go_m)
    load_m = saves.go(whole_m, wm)
    next(go_s)
    saves.wait(keep_0)
    saves.wait(keep)
    arrive(ctx_copies)
    saves.wait(load_m)
    ctx_rows = jnp.concatenate([ctx[0, 0], ctx[0, 1], ctx[1, 0], ctx[1, 1]], axis=1)
    merge = []
    for i in range(2):
        rows = pl.ds(i * 256, 256)
        found = dot(ctx_rows[i * 256 : i * 256 + 256], wm[...].reshape(512, D), NN)
        part[rows, :] = found
        give_a[rows, :] = found.astype(bf16)
        merge.append(wires.go(give_a.at[rows], take_a.at[rows], sibling))
    saves.go(ctx, ctx_out)
    next(go_e)
    load_e = saves.go(whole_e, we)
    bias_m, gain_1, shift_1 = bias(3, 0, D), bias(4, 0, D), bias(5, 0, D)

    def first_norm(i, carry):
        rows = pl.ds(pl.multiple_of(i * 64, 64), 64)
        at = pl.ds(pl.multiple_of(lax.rem(i, 4) * 64, 64), 64)
        inputs = seq[me.z_lo * 2 + lax.div(i, 4), at, :].astype(f32)
        total = inputs + part[rows, :] + take_a[rows, :].astype(f32) + bias_m
        n, scale = row_norm(total)
        n_buf[rows, :] = n
        scale_buf[rows, :] = jnp.broadcast_to(scale, (64, 128))
        low_buf[rows, :] = (n * gain_1 + shift_1).astype(bf16)
        return carry

    for i in range(2):
        merge[i].wait_recv()
        lax.fori_loop(4 * i, 4 * i + 4, first_norm, 0)
    saves.go(n_buf, n_out)
    saves.go(scale_buf, scale_out)
    saves.go(low_buf, low_out)
    saves.wait(load_e)

    def widen(i, carry):
        at = pl.ds(pl.multiple_of(i * 256, 256), 256)
        upward = dot(low_buf[...], we[:, :, :, :, at].reshape(D, 256), NN)
        upward += bias(6 + lax.div(i, 2), me.core * 512 + lax.rem(i, 2) * 256, 256)
        gate = 0.5 + 0.5 * lax.erf(upward * math.sqrt(0.5))
        active_buf[:, at] = (upward * gate).astype(bf16)
        bell = jnp.exp(-0.5 * upward * upward) * (1.0 / math.sqrt(2.0 * math.pi))
        slope_buf[:, at] = (gate + upward * bell).astype(bf16)
        return carry

    lax.fori_loop(0, 8, widen, 0)
    saves.go(active_buf, active_out)
    saves.go(slope_buf, slope_out)
    next(go_s)
    load_s = saves.go(whole_s, ws)
    saves.wait(load_s)
    feeds = []
    for i in range(2):
        rows = pl.ds(i * 256, 256)
        found = dot(active_buf[rows, :], ws[...].reshape(2048, D), NN)
        part[rows, :] = found
        give_f[rows, :] = found.astype(bf16)
        feeds.append(wires.go(give_f.at[rows], take_f.at[rows], sibling))
    saves.wait(own_cot)
    cot_beside.wait_recv()
    bias_s, gain_2, shift_2 = bias(10, 0, D), bias(11, 0, D), bias(12, 0, D)
    small_grads[...] = jnp.zeros((16, 1024), f32)

    def second_norm(i, carry):
        rows = pl.ds(pl.multiple_of(i * 64, 64), 64)
        at = pl.ds(pl.multiple_of(lax.rem(i, 4) * 64, 64), 64)
        hidden = n_buf[rows, :] * gain_1 + shift_1
        total = hidden + part[rows, :] + take_f[rows, :].astype(f32) + bias_s
        n, scale = row_norm(total)
        upstream = ups[lax.div(i, 4), at, :].astype(f32)
        grad = row_norm_backward(upstream, gain_2, n, scale)
        second_buf[rows, :] = grad
        feed = grad.astype(bf16)
        feed_buf[rows, :] = feed

        @pl.when(lax.div(i, 4) == me.core)
        def _():
            encoded[at, :] = (n * gain_2 + shift_2).astype(bf16)
            small_grads[10:11, :] += jnp.sum(feed.astype(f32), axis=0, keepdims=True)
            small_grads[11:12, :] += jnp.sum(upstream * n, axis=0, keepdims=True)
            small_grads[12:13, :] += jnp.sum(upstream, axis=0, keepdims=True)

        return carry

    for i in range(2):
        feeds[i].wait_recv()
        lax.fori_loop(4 * i, 4 * i + 4, second_norm, 0)
    saves.go(second_buf, second_out)
    saves.go(feed_buf, feed_out)
    saves.drain()
    wires.drain()

    @pl.when(mine_here)
    def _():
        z_s.wait_send()
        z_m.wait_send()


def forward_all(triple, expand, shrink, merger, small, tokens, cotangent, cosines, sines):
    shape = jax.ShapeDtypeStruct
    shapes = [
        shape((4, 2, 4, 32, 768), bf16),
        shape((4, 2, 4, 32, 2048), bf16),
        shape((4, 1, 4, 128, 1024), bf16),
        shape((4, 1, 4, 32, 1024), bf16),
        shape((4, 256, 1024), bf16),
        shape((16, 1024), f32),
        shape((256, 1024), bf16),
        shape((16, 1024), f32),
        shape((4, 1024, 1024), bf16),
        shape((2, 1024, 128), bf16),
        shape((2, 1024, 128), bf16),
        shape((2, 1024, 128), bf16),
        shape((2, 1024, 256), bf16),
        shape((2, 1024, 128), f32),
        shape((2, 2, 512, 128), bf16),
        shape((512, 1024), f32),
        shape((512, 128), f32),
        shape((512, 1024), bf16),
        shape((512, 2048), bf16),
        shape((512, 2048), bf16),
        shape((512, 1024), f32),
        shape((512, 1024), bf16),
    ]
    scratch = [
        pltpu.VMEM((3, 16, 1024), f32),
        pltpu.VMEM((3, 16, 1024), f32),
        pltpu.VMEM((16, 1024), f32),
        pltpu.VMEM((16, 1024), f32),
        pltpu.VMEM((16, 1024), f32),
        pltpu.VMEM((4, 2, 4, 32, 768), bf16),
        pltpu.VMEM((4, 2, 4, 32, 2048), bf16),
        pltpu.VMEM((4, 1, 4, 128, 1024), bf16),
        pltpu.VMEM((4, 1, 4, 32, 1024), bf16),
        pltpu.VMEM((4, 256, 1024), bf16),
        pltpu.VMEM((2, 256, 1024), bf16),
        pltpu.VMEM((4, 1024, 1024), bf16),
        pltpu.VMEM((2, 1024, 128), bf16),
        pltpu.VMEM((2, 1024, 128), bf16),
        pltpu.VMEM((2, 1024, 128), bf16),
        pltpu.VMEM((2, 1024, 256), bf16),
        pltpu.VMEM((2, 1024, 128), f32),
        pltpu.VMEM((2, 2, 512, 128), bf16),
        pltpu.VMEM((512, 1024), f32),
        pltpu.VMEM((512, 1024), bf16),
        pltpu.VMEM((512, 1024), bf16),
        pltpu.VMEM((512, 1024), bf16),
        pltpu.VMEM((512, 1024), bf16),
        pltpu.VMEM((512, 1024), f32),
        pltpu.VMEM((512, 128), f32),
        pltpu.VMEM((512, 1024), bf16),
        pltpu.VMEM((512, 2048), bf16),
        pltpu.VMEM((512, 2048), bf16),
        pltpu.VMEM((512, 1024), f32),
        pltpu.VMEM((512, 1024), bf16),
        pltpu.SemaphoreType.DMA((96,)),
        pltpu.SemaphoreType.DMA((96,)),
        pltpu.SemaphoreType.DMA((42,)),
    ]
    return pl.pallas_call(
        forward_kernel,
        out_shape=shapes,
        in_specs=[ANY, ANY, ANY, ANY, VMEM, ANY, ANY, VMEM, VMEM],
        out_specs=[ANY] * 5 + [VMEM] * 3 + [ANY] * 14,
        scratch_shapes=scratch,
        compiler_params=pltpu.CompilerParams(
            collective_id=0, has_side_effects=True, vmem_limit_bytes=58 << 20
        ),
        name="forward",
    )(triple, expand, shrink, merger, small, tokens, cotangent, cosines, sines)


NN = ((1,), (0,))
NT = ((1,), (1,))
TN = ((0,), (0,))


class Reduce:
    def __init__(self, wires, me, grad, hop_l, hop_r, mid_l, mid_r, last_l, last_r, out):
        self.wires, self.me, self.grad, self.out = wires, me, grad, out
        self.hop_l, self.hop_r, self.mid_l, self.mid_r = hop_l, hop_r, mid_l, mid_r
        self.last_l, self.last_r = last_l, last_r
        self.levels, self.half = grad.shape[1], grad.shape[4] // 2

    def first(self):
        me, half = self.me, self.half
        self.one_l, self.one_r = [], []
        for k in (1, 3, 2):
            to_x, to_y = me.along_x(k), me.along_y(k)
            self.one_l.append(
                self.wires.go(
                    self.grad.at[:, :, to_x, :, pl.ds(0, half)], self.hop_l.at[k - 1], me.at(x=to_x)
                )
            )
            self.one_r.append(
                self.wires.go(
                    self.grad.at[to_y, :, :, :, pl.ds(half, half)], self.hop_r.at[k - 1], me.at(y=to_y)
                )
            )

    def second(self):
        me, half, levels = self.me, self.half, self.levels
        self.two_l, self.two_r = [], []
        arrive(self.one_l)

        def left(i, carry):
            y, level = lax.div(i, levels), lax.rem(i, levels)
            total = self.grad[y, level, me.x, :, pl.ds(0, half)].astype(f32)
            for k in range(3):
                total += self.hop_l[k, y, level].astype(f32)
            self.mid_l[y, level] = total.astype(bf16)
            return carry

        lax.fori_loop(0, 4 * levels, left, 0)
        for k in (1, 3, 2):
            to_y = me.along_y(k)
            self.two_l.append(
                self.wires.go(self.mid_l.at[to_y], self.last_l.at[k - 1], me.at(y=to_y))
            )
        arrive(self.one_r)

        def right(i, carry):
            level, x = lax.div(i, 4), lax.rem(i, 4)
            total = self.grad[me.y, level, x, :, pl.ds(half, half)].astype(f32)
            for k in range(3):
                total += self.hop_r[k, level, x].astype(f32)
            self.mid_r[level, x] = total.astype(bf16)
            return carry

        lax.fori_loop(0, 4 * levels, right, 0)
        for k in (1, 3, 2):
            to_x = me.along_x(k)
            self.two_r.append(
                self.wires.go(self.mid_r.at[:, to_x], self.last_r.at[k - 1], me.at(x=to_x))
            )

    def third(self):
        me, half = self.me, self.half
        arrive(self.two_l)
        for level in range(self.levels):
            total = self.mid_l[me.y, level].astype(f32)
            for k in range(3):
                total += self.last_l[k, level].astype(f32)
            self.out[level, :, pl.ds(0, half)] = total.astype(bf16)
        arrive(self.two_r)
        for level in range(self.levels):
            total = self.mid_r[level, me.x].astype(f32)
            for k in range(3):
                total += self.last_r[k, level].astype(f32)
            self.out[level, :, pl.ds(half, half)] = total.astype(bf16)


def reduce_scratch(levels, rows, columns):
    half = columns // 2
    return [
        pltpu.VMEM((3, 4, levels, rows, half), bf16),
        pltpu.VMEM((3, levels, 4, rows, half), bf16),
        pltpu.VMEM((4, levels, rows, half), bf16),
        pltpu.VMEM((levels, 4, rows, half), bf16),
        pltpu.VMEM((3, levels, rows, half), bf16),
        pltpu.VMEM((3, levels, rows, half), bf16),
        pltpu.VMEM((levels, rows, columns), bf16),
    ]


def reduce_kernel(
    grad_s, grad_e, grad_m, grad_t, small,
    out_s, out_e, out_m, out_t, small_out, *rest,
):
    me = Place()
    scratch_s, scratch_e, scratch_m, scratch_t = (rest[7 * i : 7 * i + 7] for i in range(4))
    z_s, z_e, z_m, z_t, small_x, small_y, small_z, small_c, sums, send, recv = rest[28:]
    wires = Wires(send, recv)
    sibling = me.at(core=1 - me.core)
    beside, diagonal, beyond = me.z_others()
    peers = [sibling, beside, diagonal, beyond, me.at(z_lo=1 - me.z_lo, core=1 - me.core)]
    peers += [me.at(x=me.along_x(k)) for k in (1, 2, 3)]
    peers += [me.at(y=me.along_y(k)) for k in (1, 2, 3)]
    meet(peers)
    jobs = [
        Reduce(wires, me, grad, *scratch)
        for grad, scratch in (
            (grad_s, scratch_s), (grad_e, scratch_e), (grad_m, scratch_m), (grad_t, scratch_t)
        )
    ]
    got = [wires.go(small, small_x.at[k - 1], me.at(x=me.along_x(k))) for k in (1, 2, 3)]
    for job in jobs:
        job.first()
    arrive(got)
    sums[0] = small[...] + small_x[0] + small_x[1] + small_x[2]
    got = [wires.go(sums.at[0], small_y.at[k - 1], me.at(y=me.along_y(k))) for k in (1, 2, 3)]
    jobs[0].second()
    arrive(got)
    sums[1] = sums[0] + small_y[0] + small_y[1] + small_y[2]
    got = [wires.go(sums.at[1], small_z.at[k], peer) for k, peer in enumerate((beside, diagonal, beyond))]
    jobs[1].second()
    arrive(got)
    sums[2] = sums[1] + small_z[0] + small_z[1] + small_z[2]
    got = wires.go(sums.at[2], small_c, sibling)
    jobs[2].second()
    jobs[3].second()
    got.wait_recv()
    small_out[...] = sums[2] + small_c[...]

    owner = me.core == me.z_hi
    plane_s, plane_e, plane_m, plane_t = (job.out for job in jobs)
    late = []

    def to_owners(plane, slots):
        copies = [
            wires.make(plane.at[0], slots.at[k], peer)
            for k, peer in enumerate((beside, diagonal, beyond))
        ]

        @pl.when(owner)
        def _():
            copies[0].start()

        @pl.when(jnp.logical_not(owner))
        def _():
            copies[1].start()
            copies[2].start()

        late.append(copies)
        return copies

    def finish_owned(plane, slots, copies, out):
        beside_copy = wires.make(out, out, sibling)

        @pl.when(owner)
        def _():
            arrive(copies)
            total = plane[0].astype(f32)
            for k in range(3):
                total += slots[k].astype(f32)
            out[...] = total.astype(bf16)
            beside_copy.start()

        return beside_copy

    jobs[0].third()
    copies_s = to_owners(plane_s, z_s)
    jobs[1].third()
    other = 1 - me.z_hi
    copies_e = [
        wires.go(plane_e.at[level], z_e.at[k], peer)
        for k, (level, peer) in enumerate(((me.z_hi, beside), (other, diagonal), (other, beyond)))
    ]
    jobs[2].third()
    copies_m = to_owners(plane_m, z_m)
    jobs[3].third()
    copy_t = wires.go(plane_t.at[other], z_t, beyond)
    beside_s = finish_owned(plane_s, z_s, copies_s, out_s)
    arrive(copies_e)
    total = plane_e[me.z_hi].astype(f32)
    for k in range(3):
        total += z_e[k].astype(f32)
    out_e[me.core] = total.astype(bf16)
    beside_e = wires.go(out_e.at[me.core], out_e.at[me.core], sibling)
    beside_m = finish_owned(plane_m, z_m, copies_m, out_m)
    copy_t.wait_recv()
    out_t[me.seq] = (plane_t[me.z_hi].astype(f32) + z_t[...].astype(f32)).astype(bf16)
    spread = [
        wires.go(out_t.at[me.seq], out_t.at[me.seq], peer)
        for peer in (sibling, beside, me.at(z_lo=1 - me.z_lo, core=1 - me.core))
    ]

    @pl.when(jnp.logical_not(owner))
    def _():
        beside_s.wait_recv()
        beside_m.wait_recv()
        for copies in late:
            copies[1].wait_send()
            copies[2].wait_send()

    @pl.when(owner)
    def _():
        beside_s.wait_send()
        beside_m.wait_send()
        for copies in late:
            copies[0].wait_send()

    arrive(spread)
    beside_e.wait_recv()
    wires.drain()


def reduce_all(grad_s, grad_e, grad_m, grad_t, small):
    shapes = [
        jax.ShapeDtypeStruct((128, 1024), bf16),
        jax.ShapeDtypeStruct((2, 32, 2048), bf16),
        jax.ShapeDtypeStruct((32, 1024), bf16),
        jax.ShapeDtypeStruct((4, 32, 768), bf16),
        jax.ShapeDtypeStruct((16, 1024), f32),
    ]
    return pl.pallas_call(
        reduce_kernel,
        out_shape=shapes,
        in_specs=[VMEM] * 5,
        out_specs=[VMEM] * 5,
        scratch_shapes=[
            *reduce_scratch(1, 128, 1024),
            *reduce_scratch(2, 32, 2048),
            *reduce_scratch(1, 32, 1024),
            *reduce_scratch(2, 32, 768),
            pltpu.VMEM((3, 128, 1024), bf16),
            pltpu.VMEM((3, 32, 2048), bf16),
            pltpu.VMEM((3, 32, 1024), bf16),
            pltpu.VMEM((32, 768), bf16),
            pltpu.VMEM((3, 16, 1024), f32),
            pltpu.VMEM((3, 16, 1024), f32),
            pltpu.VMEM((3, 16, 1024), f32),
            pltpu.VMEM((16, 1024), f32),
            pltpu.VMEM((3, 16, 1024), f32),
            pltpu.SemaphoreType.DMA((88,)),
            pltpu.SemaphoreType.DMA((88,)),
        ],
        compiler_params=pltpu.CompilerParams(
            collective_id=1, has_side_effects=True, vmem_limit_bytes=48 << 20
        ),
        name="reduce",
    )(grad_s, grad_e, grad_m, grad_t, small)


def rotary_tables():
    inverse = 10000.0 ** (-2.0 * np.arange(32) / 64)
    angles = np.arange(LENGTH)[:, None] * inverse[None, :]
    return jnp.asarray(np.cos(angles), f32), jnp.asarray(np.sin(angles), f32)


def rotate(block, cosine, sine):
    a, b = block[..., :32], block[..., 32:]
    cosine, sine = cosine[:, None], sine[:, None]
    return jnp.concatenate([a * cosine - b * sine, b * cosine + a * sine], axis=-1)


def normalise(rows):
    centered = rows - jnp.mean(rows, axis=-1, keepdims=True)
    scale = lax.rsqrt(jnp.mean(centered * centered, axis=-1, keepdims=True) + norm_epsilon)
    return centered * scale, scale


def norm_backward(upstream, gain, n, scale):
    u = upstream * gain
    mean = jnp.mean(u, axis=-1, keepdims=True)
    along = jnp.mean(u * n, axis=-1, keepdims=True)
    return scale * (u - mean - n * along)


def swap(x, pairs):
    return lax.ppermute(x, "seq", pairs)


def spread_small(vectors, fsdp):
    rows = []
    for v in vectors:
        n = v.shape[0]
        wide = jnp.tile(v.astype(f32), 32)
        rows.append(jnp.where(lax.iota(jnp.int32, 32 * n) // n == fsdp, wide, 0.0))
    rows.append(jnp.zeros((3 * 1024,), f32))
    return jnp.concatenate(rows).reshape(16, 1024)


def mm(a, b, dims, out=f32):
    return lax.dot_general(a, b, (dims, ((), ())), preferred_element_type=f32).astype(out)


NN = ((1,), (0,))
NT = ((1,), (1,))
TN = ((0,), (0,))


def local(
    tokens, triple, triple_bias, merger, merger_bias, first_gain, first_shift,
    expand, expand_bias, shrink, shrink_bias, second_gain, second_shift, cotangent,
):
    me = Place()
    triple_cut = triple.reshape(32, 3, 2, 2, 2, 128).transpose(2, 4, 0, 1, 3, 5).reshape(2, 2, 32, 768)
    expand_cut = expand.reshape(32, 4, 2, 512).transpose(2, 0, 1, 3).reshape(2, 32, 2048)
    small = spread_small(
        (triple_bias, merger_bias, first_gain, first_shift, expand_bias, shrink_bias, second_gain, second_shift),
        me.fsdp,
    )
    inverse = 10000.0 ** (-2.0 * np.arange(32) / 64)
    angles = np.arange(LENGTH)[:, None] * inverse[None, :]
    cosines = jnp.asarray(np.tile(np.cos(angles), (1, 4)), f32)
    sines = jnp.asarray(np.tile(np.concatenate([-np.sin(angles), np.sin(angles)], axis=1), (1, 2)), f32)
    (
        whole_t, whole_e, whole_s, whole_m, sequence, small, encoded, small_part,
        e, o, q, k, v, r, ctx, n_1, scale_1, low, active, slope, second_grad, feed_grad,
    ) = forward_all(
        triple_cut, expand_cut, shrink, merger, small, tokens.reshape(256, D),
        cotangent.reshape(256, D), cosines, sines,
    )
    whole_t = whole_t.reshape(D, 768)
    whole_e = whole_e.reshape(D, 2048)
    whole_s = whole_s.reshape(2048, D)
    whole_m = whole_m.reshape(512, D)
    sequence = sequence.reshape(LENGTH, D)
    gain_1 = small[4:5]
    scale_1 = scale_1[:, :1]
    slope = slope.astype(f32)
    first_chip = me.z_lo == 0
    own_rows = me.core * 256

    def own(rows):
        return lax.dynamic_slice(rows, (own_rows, 0), (256, rows.shape[1]))

    def heads(block):
        return block[..., :128].reshape(2, LENGTH, 2, HEAD).transpose(0, 2, 1, 3).reshape(4, LENGTH, HEAD)

    ctx = ctx.transpose(2, 0, 1, 3).reshape(512, 512)
    probs = (e.astype(f32) * heads(r)[:, :, :1]).astype(bf16)
    context = heads(o).transpose(1, 0, 2).reshape(LENGTH, 256)
    cosine, sine = rotary_tables()
    q, k, v = heads(q) * 8, heads(k), heads(v)
    bias_s_grad, gain_2_grad, shift_2_grad = small_part[10], small_part[11], small_part[12]
    grad_s = mm(active, feed_grad, TN, bf16)
    up_grad = (mm(feed_grad, whole_s, NT) * slope).astype(bf16)
    grad_e = mm(low, up_grad, TN, bf16)
    bias_e_grad = jnp.sum(up_grad.astype(f32), axis=0)
    part = mm(up_grad, whole_e, NT)
    hidden_grad = part + swap(part.astype(bf16), SIBLING).astype(f32) + second_grad
    gain_1_grad = jnp.sum(own(hidden_grad * n_1), axis=0)
    shift_1_grad = jnp.sum(own(hidden_grad), axis=0)
    first_grad = norm_backward(hidden_grad, gain_1, n_1, scale_1)
    attended_grad = first_grad.astype(bf16)
    bias_m_grad = jnp.sum(own(attended_grad).astype(f32), axis=0)
    grad_m = mm(ctx, attended_grad, TN, bf16)
    ctx_grad = mm(attended_grad, whole_m, NT, bf16)

    left, right = ctx_grad[:, :256], ctx_grad[:, 256:]
    mine = jnp.where(first_chip, left, right)
    theirs = swap(jnp.where(first_chip, right, left), ACROSS)
    context_grad = jnp.concatenate(
        [jnp.where(first_chip, mine, theirs), jnp.where(first_chip, theirs, mine)], axis=0
    )
    out_grad = context_grad.reshape(LENGTH, 4, HEAD)
    delta = jnp.sum(out_grad.astype(f32) * context.reshape(LENGTH, 4, HEAD).astype(f32), axis=-1)
    prob_grad = jnp.einsum("qhd,hkd->hqk", out_grad, v, preferred_element_type=f32)
    score_grad = (probs.astype(f32) * (prob_grad - delta.T[..., None])).astype(bf16)
    q_grad = jnp.einsum("hqk,hkd->qhd", score_grad, k, preferred_element_type=f32) * 0.125
    k_grad = jnp.einsum("hqk,hqd->khd", score_grad, q, preferred_element_type=f32) * 0.125
    v_grad = jnp.einsum("hqk,qhd->khd", probs, out_grad, preferred_element_type=f32)
    pre_grad = jnp.concatenate(
        [
            rotate(q_grad, cosine, -sine).reshape(LENGTH, 256),
            rotate(k_grad, cosine, -sine).reshape(LENGTH, 256),
            v_grad.reshape(LENGTH, 256),
        ],
        axis=1,
    ).astype(bf16)
    grad_t = mm(sequence, pre_grad, TN, bf16)
    bias_t_grad = jnp.sum(pre_grad.astype(f32), axis=0)
    part = mm(pre_grad, whole_t, NT).reshape(2, 2, 256, D)
    kept = lax.dynamic_index_in_dim(part, me.core, 1, False)
    given = lax.dynamic_index_in_dim(part, 1 - me.core, 1, False).astype(bf16)
    kept = kept + swap(given, SIBLING).astype(f32)
    given = lax.dynamic_index_in_dim(kept, 1 - me.z_lo, 0, False).astype(bf16)
    kept = lax.dynamic_index_in_dim(kept, me.z_lo, 0, False) + swap(given, ACROSS).astype(f32)
    tokens_grad = (kept + own(first_grad)).astype(bf16)

    bias_t_wide = lax.dynamic_update_slice(
        jnp.zeros((3, 2, 2, 2, 128), f32), bias_t_grad.reshape(3, 1, 2, 1, 128), (0, me.z_lo, 0, me.core, 0)
    ).reshape(3072)
    bias_e_wide = lax.dynamic_update_slice(
        jnp.zeros((4, 2, 512), f32), bias_e_grad.reshape(4, 1, 512), (0, me.core, 0)
    ).reshape(4096)
    small_grad = jnp.concatenate(
        [
            bias_t_wide, bias_m_grad, gain_1_grad, shift_1_grad, bias_e_wide, bias_s_grad,
            gain_2_grad, shift_2_grad, jnp.zeros((3072,), f32),
        ]
    ).reshape(16, 1024)
    sum_s, sum_e, sum_m, sum_t, small_sum = reduce_all(
        grad_s.reshape(4, 1, 4, 128, 1024), grad_e.reshape(4, 2, 4, 32, 2048),
        grad_m.reshape(4, 1, 4, 32, 1024), grad_t.reshape(4, 2, 4, 32, 768), small_grad,
    )
    triple_grad = (
        sum_t.reshape(2, 2, 32, 3, 2, 128).transpose(2, 3, 0, 4, 1, 5).reshape(32, 3072).astype(f32)
    )
    expand_grad = sum_e.reshape(2, 32, 4, 512).transpose(1, 2, 0, 3).reshape(32, 4096).astype(f32)
    flat = small_sum.reshape(-1)

    def shard(start, n):
        return lax.dynamic_slice(flat, (start + me.fsdp * n,), (n,))

    return (
        encoded.reshape(1, 256, D),
        tokens_grad.reshape(1, 256, D),
        triple_grad,
        shard(0, 96),
        sum_m.astype(f32),
        shard(3072, 32),
        shard(4096, 32),
        shard(5120, 32),
        expand_grad,
        shard(6144, 128),
        sum_s.astype(f32),
        shard(10240, 32),
        shard(11264, 32),
        shard(12288, 32),
    )


def solution(mesh):
    rows = P("fsdp", "seq", None)
    matrix = P("fsdp", None)
    vector = P("fsdp")
    return jax.shard_map(
        local,
        mesh=mesh,
        in_specs=(
            rows, matrix, vector, matrix, vector, vector, vector, matrix, vector, matrix, vector,
            vector, vector, rows,
        ),
        out_specs=(
            rows, rows, matrix, vector, matrix, vector, vector, vector, matrix, vector, matrix,
            vector, vector, vector,
        ),
        check_vma=False,
    )
```

```python
import functools
import math

import jax
import jax.numpy as jnp
import numpy as np
from jax import lax
from jax.experimental import pallas as pl
from jax.experimental.pallas import tpu as pltpu
from jax.sharding import PartitionSpec as P

HEADS = 16
D = 1024
FF = 4096
LENGTH = 1024
HEAD = 64
bf16 = jnp.bfloat16
f32 = jnp.float32
norm_epsilon = 1e-05
MESH = pl.DeviceIdType.MESH
ANY = pl.BlockSpec(memory_space=pl.ANY)
VMEM = pl.BlockSpec(memory_space=pltpu.VMEM)
SIBLING = [(0, 1), (1, 0), (2, 3), (3, 2)]
ACROSS = [(0, 2), (2, 0), (1, 3), (3, 1)]


class Place:
    def __init__(self):
        seq, fsdp = lax.axis_index("seq"), lax.axis_index("fsdp")
        self.seq, self.fsdp = seq, fsdp
        self.z_lo, self.core = lax.div(seq, 2), lax.rem(seq, 2)
        self.x, rest = lax.rem(fsdp, 4), lax.div(fsdp, 4)
        self.z_hi, self.y = lax.rem(rest, 2), lax.div(rest, 2)

    def at(self, y=None, z_hi=None, x=None, z_lo=None, core=None):
        y = self.y if y is None else y
        z_hi = self.z_hi if z_hi is None else z_hi
        x = self.x if x is None else x
        z_lo = self.z_lo if z_lo is None else z_lo
        core = self.core if core is None else core
        return {"seq": z_lo * 2 + core, "fsdp": (y * 2 + z_hi) * 4 + x}

    def along_x(self, k):
        return lax.rem(self.x + k, 4)

    def along_y(self, k):
        return lax.rem(self.y + k, 4)

    def z_others(self):
        return [
            self.at(z_lo=1 - self.z_lo),
            self.at(z_hi=1 - self.z_hi, z_lo=1 - self.z_lo),
            self.at(z_hi=1 - self.z_hi),
        ]


def meet(peers):
    barrier = pltpu.get_barrier_semaphore()
    for peer in peers:
        pl.semaphore_signal(barrier, inc=1, device_id=peer, device_id_type=MESH)
    pl.semaphore_wait(barrier, len(peers))


class Wires:
    def __init__(self, send, recv):
        self.send, self.recv, self.used, self.open = send, recv, 0, []

    def make(self, source, target, device):
        assert self.used < self.send.shape[0]
        copy = pltpu.make_async_remote_copy(
            src_ref=source,
            dst_ref=target,
            send_sem=self.send.at[self.used],
            recv_sem=self.recv.at[self.used],
            device_id=device,
            device_id_type=MESH,
        )
        self.used += 1
        return copy

    def go(self, source, target, device):
        copy = self.make(source, target, device)
        copy.start()
        self.open.append(copy)
        return copy

    def drain(self):
        for copy in self.open:
            copy.wait_send()
        self.open = []


def arrive(copies):
    for copy in copies:
        copy.wait_recv()


def gather_steps(wires, me, whole):
    half = whole.shape[-1] // 2
    rows = whole.shape[-2] // 2
    low, high, both = pl.ds(0, rows), pl.ds(rows, rows), pl.ds(0, 2 * rows)
    left, right = pl.ds(0, half), pl.ds(half, half)
    on_x = (me.x, lambda i: me.at(x=i))
    on_y = (me.y, lambda i: me.at(y=i))
    hops = (
        (
            (*on_x, lambda i, r: whole.at[me.y, :, i, r, left]),
            (*on_y, lambda i, r: whole.at[i, :, me.x, r, right]),
        ),
        (
            (*on_y, lambda i, r: whole.at[i, :, :, r, left]),
            (*on_x, lambda i, r: whole.at[:, :, i, r, right]),
        ),
    )
    for hop in hops:
        direct = []
        for here, device, piece in hop:
            up, down = lax.rem(here + 1, 4), lax.rem(here + 3, 4)
            direct.append(
                (
                    wires.go(piece(here, both), piece(here, both), device(up)),
                    wires.go(piece(here, both), piece(here, both), device(down)),
                )
            )
        yield
        relayed = []
        for (here, device, piece), (from_down, from_up) in zip(hop, direct):
            up, down = lax.rem(here + 1, 4), lax.rem(here + 3, 4)
            from_down.wait_recv()
            relayed.append(wires.go(piece(down, low), piece(down, low), device(up)))
            from_up.wait_recv()
            relayed.append(wires.go(piece(up, high), piece(up, high), device(down)))
        yield
        arrive(relayed)
    yield


def dot(a, b, dims):
    return lax.dot_general(a, b, (dims, ((), ())), preferred_element_type=f32)


def turn(block, cosine, sine):
    lane = lax.broadcasted_iota(jnp.int32, block.shape, 1)
    other = jnp.where(
        lax.rem(lane, 64) < 32, pltpu.roll(block, 96, 1), pltpu.roll(block, 32, 1)
    )
    return block * cosine + other * sine


def row_norm(rows):
    centered = rows - jnp.mean(rows, axis=-1, keepdims=True)
    scale = lax.rsqrt(jnp.mean(centered * centered, axis=-1, keepdims=True) + norm_epsilon)
    return centered * scale, scale


def row_norm_backward(upstream, gain, n, scale):
    u = upstream * gain
    mean = jnp.mean(u, axis=-1, keepdims=True)
    along = jnp.mean(u * n, axis=-1, keepdims=True)
    return scale * (u - mean - n * along)


class Saves:
    def __init__(self, sems):
        self.sems, self.used, self.open = sems, 0, []

    def go(self, source, target):
        assert self.used < self.sems.shape[0]
        copy = pltpu.make_async_copy(source, target, self.sems.at[self.used])
        self.used += 1
        copy.start()
        self.open.append(copy)
        return copy

    def wait(self, copy):
        copy.wait()
        self.open = [other for other in self.open if other is not copy]

    def drain(self):
        for copy in self.open:
            copy.wait()
        self.open = []


def forward_kernel(
    triple, expand, shrink, merger, small, tokens, cotangent, cosines, sines,
    whole_t, whole_e, whole_s, whole_m, sequence, small_full, encoded, small_grads,
    e_out, o_out, q_out, k_out, v_out, r_out, ctx_out, n_out, scale_out, low_out,
    active_out, slope_out, second_out, feed_out,
    small_x, small_y, small_z, sum_x, sum_y, wt, we, ws, wm, seq, ups,
    e_buf, o_buf, q_buf, k_buf, v_buf, r_buf, ctx, part, give_a, take_a, give_f, take_f,
    n_buf, scale_buf, low_buf, active_buf, slope_buf, second_buf, feed_buf,
    send, recv, local_sems,
):
    me = Place()
    wires, saves = Wires(send, recv), Saves(local_sems)
    sibling = me.at(core=1 - me.core)
    across = me.at(z_lo=1 - me.z_lo)
    partner = me.at(z_hi=1 - me.z_hi, z_lo=1 - me.z_lo)
    peers = [sibling, across, partner]
    peers += [me.at(x=me.along_x(k)) for k in (1, 2, 3)]
    peers += [me.at(y=me.along_y(k)) for k in (1, 2, 3)]
    meet(peers)

    mine_here = me.core == me.z_hi
    slot_t = whole_t.at[me.y, me.z_hi, me.x]
    slot_e = whole_e.at[me.y, me.z_hi, me.x]
    slot_s = whole_s.at[me.y, 0, me.x]
    slot_m = whole_m.at[me.y, 0, me.x]
    z_t = wires.go(triple.at[1 - me.z_lo, me.core], slot_t, partner)
    tok_across = wires.go(tokens, seq.at[me.seq], across)
    x_small = [wires.go(small, small_x.at[k - 1], me.at(x=me.along_x(k))) for k in (1, 2, 3)]
    tok_beside = wires.go(tokens, seq.at[me.seq], sibling)
    z_e = wires.go(expand.at[me.core], slot_e, partner)
    cot_beside = wires.go(cotangent, ups.at[me.core], sibling)
    own_t = saves.go(triple.at[me.z_lo, me.core], slot_t)
    own_tok = saves.go(tokens, seq.at[me.seq])
    own_e = saves.go(expand.at[me.core], slot_e)
    own_cot = saves.go(cotangent, ups.at[me.core])
    z_s = wires.make(shrink, slot_s, partner)
    z_m = wires.make(merger, slot_m, partner)
    own_s = pltpu.make_async_copy(shrink, slot_s, local_sems.at[40])
    own_m = pltpu.make_async_copy(merger, slot_m, local_sems.at[41])

    @pl.when(mine_here)
    def _():
        z_s.start()
        z_m.start()
        own_s.start()
        own_m.start()

    go_t = gather_steps(wires, me, whole_t)
    go_e = gather_steps(wires, me, whole_e)
    go_s = gather_steps(wires, me, whole_s)
    go_m = gather_steps(wires, me, whole_m)
    saves.wait(own_t)
    z_t.wait_recv()
    next(go_t)
    arrive(x_small)
    sum_x[...] = small[...] + small_x[0] + small_x[1] + small_x[2]
    y_small = [wires.go(sum_x, small_y.at[k - 1], me.at(y=me.along_y(k))) for k in (1, 2, 3)]
    next(go_t)
    arrive(y_small)
    sum_y[...] = sum_x[...] + small_y[0] + small_y[1] + small_y[2]
    z_small = wires.go(sum_y, small_z, partner)
    next(go_t)
    saves.wait(own_e)
    z_e.wait_recv()
    next(go_e)

    @pl.when(mine_here)
    def _():
        own_s.wait()
        own_m.wait()

    @pl.when(jnp.logical_not(mine_here))
    def _():
        z_s.wait_recv()
        z_m.wait_recv()

    next(go_m)
    tok_across.wait_recv()
    far = seq.at[(1 - me.z_lo) * 2 + me.core]
    tok_relay = wires.go(far, far, sibling)
    z_small.wait_recv()
    small_full[...] = sum_y[...] + small_z[...]
    next(go_t)
    next(go_e)
    next(go_m)
    next(go_s)
    next(go_t)
    load_t = saves.go(whole_t, wt)
    next(go_e)
    next(go_m)
    next(go_s)
    saves.wait(own_tok)
    arrive([tok_beside, tok_relay])
    saves.wait(load_t)

    def bias(row, start, n):
        return small_full[pl.ds(row, 1), pl.ds(pl.multiple_of(start, 128), n)]

    bias_t = [
        bias(t, me.z_lo * 512 + j * 256 + me.core * 128, 128) for t in range(3) for j in range(2)
    ]
    bias_t = jnp.concatenate(bias_t, axis=1)

    def project(i, carry):
        rows = pl.ds(pl.multiple_of(i * 256, 256), 256)
        pre = dot(seq[i], wt[...].reshape(D, 768), NN) + bias_t
        cosine, sine = cosines[rows, :], sines[rows, :]
        for p in range(2):
            cut = pre[:, p * 128 : p * 128 + 128]
            q_buf[p, rows, :] = (turn(cut, cosine, sine) * 0.125).astype(bf16)
            cut = pre[:, 256 + p * 128 : 384 + p * 128]
            k_buf[p, rows, :] = turn(cut, cosine, sine).astype(bf16)
            v_buf[p, rows, pl.ds(0, 128)] = pre[:, 512 + p * 128 : 640 + p * 128].astype(bf16)
            v_buf[p, rows, pl.ds(128, 128)] = jnp.ones((256, 128), bf16)
        return carry

    lax.fori_loop(0, 4, project, 0)
    saves.go(seq, sequence)
    saves.go(q_buf, q_out)
    saves.go(k_buf, k_out)
    saves.go(v_buf, v_out)
    next(go_s)
    ctx_copies = []
    for p in range(2):

        def attend(i, carry, p=p):
            rows = pl.ds(pl.multiple_of(i * 256, 256), 256)
            lane = lax.broadcasted_iota(jnp.int32, (256, 128), 1)
            found = []
            for h in range(2):
                head = (lane >= 64) if h else (lane < 64)
                q = jnp.where(head, q_buf[p, rows, :], jnp.zeros((), bf16))
                scores = dot(q, k_buf[p], NT)
                peak = jnp.max(scores, axis=1, keepdims=True)
                powers = jnp.exp(scores - peak).astype(bf16)
                e_buf[2 * p + h, rows, :] = powers
                found.append(dot(powers, v_buf[p], NN))
            first = lane < 64
            over = 1.0 / jnp.where(first, found[0][:, 128:], found[1][:, 128:])
            r_buf[p, rows, :] = over
            o_buf[p, rows, :] = (jnp.where(first, found[0][:, :128], found[1][:, :128]) * over).astype(bf16)
            return carry

        lax.fori_loop(0, 4, attend, 0)
        saves.go(e_buf.at[pl.ds(2 * p, 2)], e_out.at[pl.ds(2 * p, 2)])
        theirs = o_buf.at[p, pl.ds(pl.multiple_of((1 - me.z_lo) * 512, 512), 512)]
        ours = o_buf.at[p, pl.ds(pl.multiple_of(me.z_lo * 512, 512), 512)]
        ctx_copies.append(wires.go(theirs, ctx.at[me.z_lo, p], across))
        keep = saves.go(ours, ctx.at[me.z_lo, p])
        if p == 0:
            next(go_e)
            next(go_m)
            keep_0 = keep
    saves.go(r_buf, r_out)
    saves.go(o_buf, o_out)
    next(go_m)
    load_m = saves.go(whole_m, wm)
    next(go_s)
    saves.wait(keep_0)
    saves.wait(keep)
    arrive(ctx_copies)
    saves.wait(load_m)
    ctx_rows = jnp.concatenate([ctx[0, 0], ctx[0, 1], ctx[1, 0], ctx[1, 1]], axis=1)
    merge = []
    for i in range(2):
        rows = pl.ds(i * 256, 256)
        found = dot(ctx_rows[i * 256 : i * 256 + 256], wm[...].reshape(512, D), NN)
        part[rows, :] = found
        give_a[rows, :] = found.astype(bf16)
        merge.append(wires.go(give_a.at[rows], take_a.at[rows], sibling))
    saves.go(ctx, ctx_out)
    next(go_e)
    load_e = saves.go(whole_e, we)
    bias_m, gain_1, shift_1 = bias(3, 0, D), bias(4, 0, D), bias(5, 0, D)

    def first_norm(i, carry):
        rows = pl.ds(pl.multiple_of(i * 64, 64), 64)
        at = pl.ds(pl.multiple_of(lax.rem(i, 4) * 64, 64), 64)
        inputs = seq[me.z_lo * 2 + lax.div(i, 4), at, :].astype(f32)
        total = inputs + part[rows, :] + take_a[rows, :].astype(f32) + bias_m
        n, scale = row_norm(total)
        n_buf[rows, :] = n
        scale_buf[rows, :] = jnp.broadcast_to(scale, (64, 128))
        low_buf[rows, :] = (n * gain_1 + shift_1).astype(bf16)
        return carry

    for i in range(2):
        merge[i].wait_recv()
        lax.fori_loop(4 * i, 4 * i + 4, first_norm, 0)
    saves.go(n_buf, n_out)
    saves.go(scale_buf, scale_out)
    saves.go(low_buf, low_out)
    saves.wait(load_e)

    def widen(i, carry):
        at = pl.ds(pl.multiple_of(i * 256, 256), 256)
        upward = dot(low_buf[...], we[:, :, :, :, at].reshape(D, 256), NN)
        upward += bias(6 + lax.div(i, 2), me.core * 512 + lax.rem(i, 2) * 256, 256)
        gate = 0.5 + 0.5 * lax.erf(upward * math.sqrt(0.5))
        active_buf[:, at] = (upward * gate).astype(bf16)
        bell = jnp.exp(-0.5 * upward * upward) * (1.0 / math.sqrt(2.0 * math.pi))
        slope_buf[:, at] = (gate + upward * bell).astype(bf16)
        return carry

    lax.fori_loop(0, 8, widen, 0)
    saves.go(active_buf, active_out)
    saves.go(slope_buf, slope_out)
    next(go_s)
    load_s = saves.go(whole_s, ws)
    saves.wait(load_s)
    feeds = []
    for i in range(2):
        rows = pl.ds(i * 256, 256)
        found = dot(active_buf[rows, :], ws[...].reshape(2048, D), NN)
        part[rows, :] = found
        give_f[rows, :] = found.astype(bf16)
        feeds.append(wires.go(give_f.at[rows], take_f.at[rows], sibling))
    saves.wait(own_cot)
    cot_beside.wait_recv()
    bias_s, gain_2, shift_2 = bias(10, 0, D), bias(11, 0, D), bias(12, 0, D)
    small_grads[...] = jnp.zeros((16, 1024), f32)

    def second_norm(i, carry):
        rows = pl.ds(pl.multiple_of(i * 64, 64), 64)
        at = pl.ds(pl.multiple_of(lax.rem(i, 4) * 64, 64), 64)
        hidden = n_buf[rows, :] * gain_1 + shift_1
        total = hidden + part[rows, :] + take_f[rows, :].astype(f32) + bias_s
        n, scale = row_norm(total)
        upstream = ups[lax.div(i, 4), at, :].astype(f32)
        grad = row_norm_backward(upstream, gain_2, n, scale)
        second_buf[rows, :] = grad
        feed = grad.astype(bf16)
        feed_buf[rows, :] = feed

        @pl.when(lax.div(i, 4) == me.core)
        def _():
            encoded[at, :] = (n * gain_2 + shift_2).astype(bf16)
            small_grads[10:11, :] += jnp.sum(feed.astype(f32), axis=0, keepdims=True)
            small_grads[11:12, :] += jnp.sum(upstream * n, axis=0, keepdims=True)
            small_grads[12:13, :] += jnp.sum(upstream, axis=0, keepdims=True)

        return carry

    for i in range(2):
        feeds[i].wait_recv()
        lax.fori_loop(4 * i, 4 * i + 4, second_norm, 0)
    saves.go(second_buf, second_out)
    saves.go(feed_buf, feed_out)
    saves.drain()
    wires.drain()
    assert all(next(steps, "end") == "end" for steps in (go_t, go_e, go_s, go_m))

    @pl.when(mine_here)
    def _():
        z_s.wait_send()
        z_m.wait_send()


def forward_all(triple, expand, shrink, merger, small, tokens, cotangent, cosines, sines):
    shape = jax.ShapeDtypeStruct
    shapes = [
        shape((4, 2, 4, 32, 768), bf16),
        shape((4, 2, 4, 32, 2048), bf16),
        shape((4, 1, 4, 128, 1024), bf16),
        shape((4, 1, 4, 32, 1024), bf16),
        shape((4, 256, 1024), bf16),
        shape((16, 1024), f32),
        shape((256, 1024), bf16),
        shape((16, 1024), f32),
        shape((4, 1024, 1024), bf16),
        shape((2, 1024, 128), bf16),
        shape((2, 1024, 128), bf16),
        shape((2, 1024, 128), bf16),
        shape((2, 1024, 256), bf16),
        shape((2, 1024, 128), f32),
        shape((2, 2, 512, 128), bf16),
        shape((512, 1024), f32),
        shape((512, 128), f32),
        shape((512, 1024), bf16),
        shape((512, 2048), bf16),
        shape((512, 2048), bf16),
        shape((512, 1024), f32),
        shape((512, 1024), bf16),
    ]
    scratch = [
        pltpu.VMEM((3, 16, 1024), f32),
        pltpu.VMEM((3, 16, 1024), f32),
        pltpu.VMEM((16, 1024), f32),
        pltpu.VMEM((16, 1024), f32),
        pltpu.VMEM((16, 1024), f32),
        pltpu.VMEM((4, 2, 4, 32, 768), bf16),
        pltpu.VMEM((4, 2, 4, 32, 2048), bf16),
        pltpu.VMEM((4, 1, 4, 128, 1024), bf16),
        pltpu.VMEM((4, 1, 4, 32, 1024), bf16),
        pltpu.VMEM((4, 256, 1024), bf16),
        pltpu.VMEM((2, 256, 1024), bf16),
        pltpu.VMEM((4, 1024, 1024), bf16),
        pltpu.VMEM((2, 1024, 128), bf16),
        pltpu.VMEM((2, 1024, 128), bf16),
        pltpu.VMEM((2, 1024, 128), bf16),
        pltpu.VMEM((2, 1024, 256), bf16),
        pltpu.VMEM((2, 1024, 128), f32),
        pltpu.VMEM((2, 2, 512, 128), bf16),
        pltpu.VMEM((512, 1024), f32),
        pltpu.VMEM((512, 1024), bf16),
        pltpu.VMEM((512, 1024), bf16),
        pltpu.VMEM((512, 1024), bf16),
        pltpu.VMEM((512, 1024), bf16),
        pltpu.VMEM((512, 1024), f32),
        pltpu.VMEM((512, 128), f32),
        pltpu.VMEM((512, 1024), bf16),
        pltpu.VMEM((512, 2048), bf16),
        pltpu.VMEM((512, 2048), bf16),
        pltpu.VMEM((512, 1024), f32),
        pltpu.VMEM((512, 1024), bf16),
        pltpu.SemaphoreType.DMA((96,)),
        pltpu.SemaphoreType.DMA((96,)),
        pltpu.SemaphoreType.DMA((42,)),
    ]
    return pl.pallas_call(
        forward_kernel,
        out_shape=shapes,
        in_specs=[ANY, ANY, ANY, ANY, VMEM, ANY, ANY, VMEM, VMEM],
        out_specs=[ANY] * 5 + [VMEM] * 3 + [ANY] * 14,
        scratch_shapes=scratch,
        compiler_params=pltpu.CompilerParams(
            collective_id=0, has_side_effects=True, vmem_limit_bytes=58 << 20
        ),
        name="forward",
    )(triple, expand, shrink, merger, small, tokens, cotangent, cosines, sines)


NN = ((1,), (0,))
NT = ((1,), (1,))
TN = ((0,), (0,))


def reduce_steps(wires, me, grad, buffers, out):
    first_l, first_r, mid_l, mid_r, last_l, last_r = buffers
    levels, half, h = grad.shape[1], grad.shape[4] // 2, grad.shape[3] // 2
    left, right = pl.ds(0, half), pl.ds(half, half)
    upper, lower = pl.ds(0, h), pl.ds(h, h)
    on_x = (me.x, lambda i: me.at(x=i))
    on_y = (me.y, lambda i: me.at(y=i))

    def in_mid_l(n, r, value):
        mid_l[lax.div(n, levels), lax.rem(n, levels), r, :] = value

    def in_mid_r(n, r, value):
        mid_r[lax.div(n, 4), lax.rem(n, 4), r, :] = value

    def in_out_l(n, r, value):
        out[n, r, left] = value

    def in_out_r(n, r, value):
        out[n, r, right] = value

    hops = (
        (
            (
                *on_x, 4 * levels, lambda n: (lax.div(n, levels), lax.rem(n, levels)), first_l,
                lambda d, r: grad.at[:, :, d, r, left],
                lambda d, n, r: grad[lax.div(n, levels), lax.rem(n, levels), d, r, left],
                in_mid_l,
            ),
            (
                *on_y, 4 * levels, lambda n: (lax.div(n, 4), lax.rem(n, 4)), first_r,
                lambda d, r: grad.at[d, :, :, r, right],
                lambda d, n, r: grad[d, lax.div(n, 4), lax.rem(n, 4), r, right],
                in_mid_r,
            ),
        ),
        (
            (
                *on_y, levels, lambda n: (n,), last_l,
                lambda d, r: mid_l.at[d, :, r, :],
                lambda d, n, r: mid_l[d, n, r, :],
                in_out_l,
            ),
            (
                *on_x, levels, lambda n: (n,), last_r,
                lambda d, r: mid_r.at[:, d, r, :],
                lambda d, n, r: mid_r[n, d, r, :],
                in_out_r,
            ),
        ),
    )
    for hop in hops:
        sent = []
        for here, device, count, index, (relay, near, far), piece, value, store in hop:
            up, down, corner = lax.rem(here + 1, 4), lax.rem(here + 3, 4), lax.rem(here + 2, 4)
            sent.append(
                (
                    wires.go(piece(corner, upper), relay.at[0], device(up)),
                    wires.go(piece(corner, lower), relay.at[1], device(down)),
                    wires.go(piece(up, lower), near.at[0], device(up)),
                    wires.go(piece(down, upper), near.at[1], device(down)),
                )
            )
        yield
        summed = []
        for (here, device, count, index, (relay, near, far), piece, value, store), copies in zip(hop, sent):
            up, down = lax.rem(here + 1, 4), lax.rem(here + 3, 4)
            arrive(copies[:2])

            def pass_on(n, carry, relay=relay, value=value, index=index, up=up, down=down):
                at = (0, *index(n))
                relay[at] = (relay[at].astype(f32) + value(up, n, upper).astype(f32)).astype(bf16)
                at = (1, *index(n))
                relay[at] = (relay[at].astype(f32) + value(down, n, lower).astype(f32)).astype(bf16)
                return carry

            lax.fori_loop(0, count, pass_on, 0)
            summed.append(wires.go(relay.at[0], far.at[0], device(up)))
            summed.append(wires.go(relay.at[1], far.at[1], device(down)))
        yield
        arrive(summed)
        for (here, device, count, index, (relay, near, far), piece, value, store), copies in zip(hop, sent):
            arrive(copies[2:])

            def finish(n, carry, near=near, far=far, value=value, index=index, store=store, here=here):
                for r, i in ((upper, 0), (lower, 1)):
                    total = value(here, n, r).astype(f32)
                    total += near[(1 - i, *index(n))].astype(f32) + far[(i, *index(n))].astype(f32)
                    store(n, r, total.astype(bf16))
                return carry

            lax.fori_loop(0, count, finish, 0)
    yield


def reduce_scratch(levels, rows, columns):
    half, h = columns // 2, rows // 2

    def trio(*lead):
        return [pltpu.VMEM((2, *lead, h, half), bf16)] * 3

    return [
        *trio(4, levels),
        *trio(levels, 4),
        pltpu.VMEM((4, levels, rows, half), bf16),
        pltpu.VMEM((levels, 4, rows, half), bf16),
        *trio(levels),
        *trio(levels),
        pltpu.VMEM((levels, rows, columns), bf16),
    ]


def reduce_job(wires, me, grad, scratch):
    buffers = (scratch[0:3], scratch[3:6], scratch[6], scratch[7], scratch[8:11], scratch[11:14])
    return reduce_steps(wires, me, grad, buffers, scratch[14])


def backward_kernel(
    whole_t, whole_e, whole_s, whole_m, sequence, small_full, small_part,
    e_in, o_in, q_in, k_in, v_in, r_in, ctx_in, n_in, scale_in, low_in,
    active_in, slope_in, second_in, feed_in, cosines, sines,
    tokens_out, out_s, out_e, out_m, out_t, small_out, *rest,
):
    me = Place()
    scratch_s, scratch_e, scratch_m, scratch_t = (rest[15 * i : 15 * i + 15] for i in range(4))
    (
        z_s, z_e, z_m, z_t, sum_s, sum_e, sum_m, sum_t,
        small_x, small_y, small_z, small_c, sums,
        wt, we, ws, wm, e_buf, o_buf, q_buf, k_buf, v_buf, r_buf, ctx, n_buf, scale_buf,
        low_buf, active_buf, slope_buf, second_buf, feed_buf, part, take_a,
        give_c, dctx, dq_buf, pre_grad, grad_t, take_t, take_x, send, recv, local_sems,
    ) = rest[60:]
    give_a = feed_buf
    acc_k, acc_v = second_buf.at[pl.ds(0, 128)], second_buf.at[pl.ds(128, 128)]
    give_t = [active_buf.at[pl.ds(256 * z, 256), pl.ds(0, D)] for z in range(2)]
    give_x = active_buf.at[pl.ds(0, 256), pl.ds(D, D)]
    wires, saves = Wires(send, recv), Saves(local_sems)
    sibling = me.at(core=1 - me.core)
    beside, diagonal, beyond = me.z_others()
    load_feed = saves.go(feed_in, feed_buf)
    load_s = saves.go(whole_s, ws)
    load_slope = saves.go(slope_in, slope_buf)
    load_active = saves.go(active_in, active_buf)
    load_e = saves.go(whole_e, we)
    load_low = saves.go(low_in, low_buf)
    load_norm = [saves.go(n_in, n_buf), saves.go(scale_in, scale_buf), saves.go(second_in, second_buf)]
    load_m = [saves.go(whole_m, wm), saves.go(ctx_in, ctx)]
    load_heads = [
        saves.go(e_in.at[0], e_buf.at[0]), saves.go(e_in.at[1], e_buf.at[1]), saves.go(o_in, o_buf),
        saves.go(q_in, q_buf), saves.go(k_in, k_buf), saves.go(v_in, v_buf), saves.go(r_in, r_buf),
    ]
    load_t = saves.go(whole_t, wt)
    peers = [sibling, beside, diagonal, beyond, me.at(z_lo=1 - me.z_lo, core=1 - me.core)]
    peers += [me.at(x=me.along_x(k)) for k in (1, 2, 3)]
    peers += [me.at(y=me.along_y(k)) for k in (1, 2, 3)]
    meet(peers)
    go_s = reduce_job(wires, me, ws, scratch_s)
    go_e = reduce_job(wires, me, we, scratch_e)
    go_m = reduce_job(wires, me, wm, scratch_m)
    go_t = reduce_job(wires, me, grad_t, scratch_t)
    plane_s, plane_e, plane_m, plane_t = (s[14] for s in (scratch_s, scratch_e, scratch_m, scratch_t))
    sums[0] = small_part[...]

    for load in (load_feed, load_s, load_slope, load_active):
        saves.wait(load)

    def narrow(i, carry):
        y, pair = lax.div(i, 2), pl.ds(2 * lax.rem(i, 2), 2)
        at = pl.ds(pl.multiple_of(i * 256, 256), 256)
        back = dot(feed_buf[...], ws[y, 0, pair].reshape(256, D), NT)
        up = (back * slope_buf[:, at].astype(f32)).astype(bf16)
        slope_buf[:, at] = up
        where = pl.ds(pl.multiple_of(me.core * 512 + lax.rem(i, 2) * 256, 256), 256)
        sums[0, pl.ds(6 + y, 1), where] = jnp.sum(up.astype(f32), axis=0, keepdims=True)
        found = dot(active_buf[:, at], feed_buf[...], TN)
        ws[y, 0, pair] = found.astype(bf16).reshape(2, 128, D)
        return carry

    lax.fori_loop(0, 8, narrow, 0)
    next(go_s)
    saves.wait(load_e)

    def hidden_part(y, carry):
        at = pl.ds(pl.multiple_of(y * 256, 256), 256)
        found = dot(slope_buf[...], we[y].reshape(256, 2048), NT)
        part[:, at] = found
        give_a[:, at] = found.astype(bf16)
        return carry

    shared = []
    for i in range(2):
        lax.fori_loop(2 * i, 2 * i + 2, hidden_part, 0)
        at = pl.ds(512 * i, 512)
        shared.append(wires.go(give_a.at[:, at], take_a.at[:, at], sibling))
    saves.wait(load_low)

    def expand_part(i, carry):
        y, at = lax.div(i, 4), pl.ds(pl.multiple_of(lax.rem(i, 4) * 512, 512), 512)
        found = dot(low_buf[:, pl.ds(pl.multiple_of(y * 256, 256), 256)], slope_buf[:, at], TN)
        we[y, :, :, :, at] = found.astype(bf16).reshape(2, 4, 32, 512)
        return carry

    lax.fori_loop(0, 16, expand_part, 0)
    next(go_e)
    for load in load_norm:
        saves.wait(load)
    arrive(shared)
    gain_1 = small_full[4:5, :]

    def first_norm(i, carry):
        rows = pl.ds(pl.multiple_of(i * 64, 64), 64)
        upstream = part[rows, :] + take_a[rows, :].astype(f32) + second_buf[rows, :]
        n = n_buf[rows, :]
        grad = row_norm_backward(upstream, gain_1, n, scale_buf[rows, 0:1])
        n_buf[rows, :] = grad
        low = grad.astype(bf16)
        low_buf[rows, :] = low

        @pl.when(lax.div(i, 4) == me.core)
        def _():
            sums[0, 3:4, :] += jnp.sum(low.astype(f32), axis=0, keepdims=True)
            sums[0, 4:5, :] += jnp.sum(upstream * n, axis=0, keepdims=True)
            sums[0, 5:6, :] += jnp.sum(upstream, axis=0, keepdims=True)

        return carry

    lax.fori_loop(0, 8, first_norm, 0)
    for load in load_m:
        saves.wait(load)

    def context_part(group):
        return dot(low_buf[...], wm[pl.ds(2 * group, 2)].reshape(256, D), NT).astype(bf16)

    found = context_part(1 - me.z_lo)
    give_c[0] = found[:, :128]
    give_c[1] = found[:, 128:]
    chip = pl.ds(pl.multiple_of(me.z_lo * 512, 512), 512)
    swapped = wires.go(give_c, dctx.at[:, chip, :], beside)
    found = context_part(me.z_lo)
    dctx[0, chip, :] = found[:, :128]
    dctx[1, chip, :] = found[:, 128:]
    next(go_s)
    for z in range(2):
        for p in range(2):
            found = dot(ctx[z, p], low_buf[...], TN).astype(bf16)
            wm[2 * z + p] = found.reshape(1, 4, 32, D)
    next(go_m)
    for load in load_heads:
        saves.wait(load)
    swapped.wait_recv()

    def head_back(p, h):
        slot = h

        def block(i, carry):
            rows = pl.ds(pl.multiple_of(i * 256, 256), 256)
            lane = lax.broadcasted_iota(jnp.int32, (256, 128), 1)
            head = (lane >= 64) if h else (lane < 64)
            scaled = jnp.where(head, dctx[p, rows, :].astype(f32) * r_buf[p, rows, :], 0.0).astype(bf16)
            delta = jnp.sum(scaled.astype(f32) * o_buf[p, rows, :].astype(f32), axis=1, keepdims=True)
            high = delta.astype(bf16).astype(f32)
            extra = jnp.where(lane == 0, -high, jnp.where(lane == 1, high - delta, 0.0)).astype(bf16)
            given = jnp.concatenate([scaled, extra], axis=1)
            prob_grad = dot(given, v_buf[p], NT)
            powers = e_buf[slot, rows, :]
            score_grad = (powers.astype(f32) * prob_grad).astype(bf16)
            dq = dot(score_grad, k_buf[p], NN)
            if h == 0:
                dq_buf[rows, :] = dq
            else:
                dq = jnp.where(lane < 64, dq_buf[rows, :], dq)
                dq = (dq * 0.125).astype(bf16).astype(f32)
                turned = turn(dq, cosines[rows, :], -sines[rows, :])
                pre_grad[rows, pl.ds(p * 128, 128)] = turned.astype(bf16)
            q = jnp.where(head, q_buf[p, rows, :], jnp.zeros((), bf16))
            acc_k[...] += dot(q, score_grad, TN)
            acc_v[...] += dot(scaled, powers, TN)
            return carry

        lax.fori_loop(0, 4, block, 0)

    def pair_end(p):
        def block(i, carry):
            rows = pl.ds(pl.multiple_of(i * 256, 256), 256)
            dk = acc_k[:, rows].T.astype(bf16).astype(f32)
            turned = turn(dk, cosines[rows, :], -sines[rows, :])
            pre_grad[rows, pl.ds(256 + p * 128, 128)] = turned.astype(bf16)
            pre_grad[rows, pl.ds(512 + p * 128, 128)] = acc_v[:, rows].T.astype(bf16)
            return carry

        lax.fori_loop(0, 4, block, 0)

    def clear():
        acc_k[...] = jnp.zeros((128, D), f32)
        acc_v[...] = jnp.zeros((128, D), f32)

    clear()
    head_back(0, 0)
    load_2 = saves.go(e_in.at[2], e_buf.at[0])
    next(go_e)
    head_back(0, 1)
    load_3 = saves.go(e_in.at[3], e_buf.at[1])
    pair_end(0)
    clear()
    next(go_s)
    next(go_m)
    saves.wait(load_2)
    head_back(1, 0)
    seq = e_buf.at[0]
    load_seq = saves.go(sequence, seq)
    next(go_e)
    saves.wait(load_3)
    head_back(1, 1)
    pair_end(1)
    next(go_s)
    next(go_m)

    def bias_part(i, total):
        rows = pl.ds(pl.multiple_of(i * 128, 128), 128)
        return total + jnp.sum(pre_grad[rows, :].astype(f32), axis=0, keepdims=True)

    total = lax.fori_loop(0, 8, bias_part, jnp.zeros((1, 768), f32))
    for t in range(3):
        for j in range(2):
            at = pl.ds(pl.multiple_of(me.z_lo * 512 + j * 256 + me.core * 128, 128), 128)
            start = t * 256 + j * 128
            sums[0, t : t + 1, at] = total[:, start : start + 128]
    got = [wires.go(sums.at[0], small_x.at[k - 1], me.at(x=me.along_x(k))) for k in (1, 2, 3)]
    saves.wait(load_t)
    saves.wait(load_seq)

    def triple_part(y, carry):
        at = pl.ds(pl.multiple_of(y * 256, 256), 256)
        found = dot(seq[:, at], pre_grad[...], TN)
        grad_t[y] = found.astype(bf16).reshape(2, 4, 32, 768)
        return carry

    lax.fori_loop(0, 4, triple_part, 0)
    next(go_t)

    def tokens_part(z, core):
        rows = pl.ds(pl.multiple_of((2 * z + core) * 256, 256), 256)
        return dot(pre_grad[rows, :], wt[...].reshape(D, 768), NT)

    beside_rows = []
    for z in range(2):
        give_t[z][...] = tokens_part(z, 1 - me.core).astype(bf16)
        beside_rows.append(wires.go(give_t[z], take_t.at[z], sibling))
    next(go_m)
    next(go_e)
    next(go_s)
    owner = me.core == me.z_hi
    late = []

    def to_owners(plane, slots):
        copies = [
            wires.make(plane.at[0], slots.at[k], peer)
            for k, peer in enumerate((beside, diagonal, beyond))
        ]

        @pl.when(owner)
        def _():
            copies[0].start()

        @pl.when(jnp.logical_not(owner))
        def _():
            copies[1].start()
            copies[2].start()

        late.append(copies)
        return copies

    def finish_owned(plane, slots, copies, out):
        beside_copy = wires.make(out, out, sibling)

        @pl.when(owner)
        def _():
            arrive(copies)
            total = plane[0].astype(f32)
            for k in range(3):
                total += slots[k].astype(f32)
            out[...] = total.astype(bf16)
            beside_copy.start()

        return beside_copy

    copies_s = to_owners(plane_s, z_s)
    for z in range(2):
        part[pl.ds(256 * z, 256), :] = tokens_part(z, me.core)
    arrive(got)
    sums[1] = sums[0] + small_x[0] + small_x[1] + small_x[2]
    got = [wires.go(sums.at[1], small_y.at[k - 1], me.at(y=me.along_y(k))) for k in (1, 2, 3)]
    next(go_t)
    arrive(beside_rows)
    other = 1 - me.z_lo
    rows = pl.ds(pl.multiple_of(other * 256, 256), 256)
    give_x[...] = (part[rows, :] + take_t[other].astype(f32)).astype(bf16)
    across_rows = wires.go(give_x, take_x, beside)
    next(go_e)
    flip = 1 - me.z_hi
    copies_e = [
        wires.go(plane_e.at[level], z_e.at[k], peer)
        for k, (level, peer) in enumerate(((me.z_hi, beside), (flip, diagonal), (flip, beyond)))
    ]
    next(go_m)
    copies_m = to_owners(plane_m, z_m)
    next(go_t)
    arrive(got)
    sums[2] = sums[1] + small_y[0] + small_y[1] + small_y[2]
    got = [wires.go(sums.at[2], small_z.at[k], peer) for k, peer in enumerate((beside, diagonal, beyond))]
    beside_s = finish_owned(plane_s, z_s, copies_s, sum_s)
    next(go_t)
    arrive(copies_e)
    total = plane_e[me.z_hi].astype(f32)
    for k in range(3):
        total += z_e[k].astype(f32)
    sum_e[me.core] = total.astype(bf16)
    beside_e = wires.go(sum_e.at[me.core], sum_e.at[me.core], sibling)
    beside_m = finish_owned(plane_m, z_m, copies_m, sum_m)
    arrive(got)
    sums[3] = sums[2] + small_z[0] + small_z[1] + small_z[2]
    got = wires.go(sums.at[3], small_c, sibling)
    next(go_t)
    copy_t = wires.go(plane_t.at[flip], z_t, beyond)
    across_rows.wait_recv()
    rows = pl.ds(pl.multiple_of(me.z_lo * 256, 256), 256)
    own = pl.ds(pl.multiple_of(me.core * 256, 256), 256)
    tokens_out[...] = (
        part[rows, :] + take_t[me.z_lo].astype(f32) + take_x[...].astype(f32) + n_buf[own, :]
    ).astype(bf16)
    got.wait_recv()
    small_out[...] = sums[3] + small_c[...]
    copy_t.wait_recv()
    sum_t[me.seq] = (plane_t[me.z_hi].astype(f32) + z_t[...].astype(f32)).astype(bf16)
    spread = [
        wires.go(sum_t.at[me.seq], sum_t.at[me.seq], peer)
        for peer in (sibling, beside, me.at(z_lo=1 - me.z_lo, core=1 - me.core))
    ]

    @pl.when(jnp.logical_not(owner))
    def _():
        beside_s.wait_recv()
        beside_m.wait_recv()
        for copies in late:
            copies[1].wait_send()
            copies[2].wait_send()

    @pl.when(owner)
    def _():
        beside_s.wait_send()
        beside_m.wait_send()
        for copies in late:
            copies[0].wait_send()

    out_s[...] = sum_s[...].astype(f32)
    out_m[...] = sum_m[...].astype(f32)
    beside_e.wait_recv()
    for c in range(2):
        for y in range(4):
            start = y * 1024 + c * 512
            out_e[:, start : start + 512] = sum_e[c, :, y * 512 : y * 512 + 512].astype(f32)
    arrive(spread)
    for s in range(4):
        for t in range(3):
            for j in range(2):
                start = t * 1024 + (s // 2) * 512 + j * 256 + (s % 2) * 128
                cut = t * 256 + j * 128
                out_t[:, start : start + 128] = sum_t[s, :, cut : cut + 128].astype(f32)
    wires.drain()
    saves.drain()
    assert all(next(steps, "end") == "end" for steps in (go_s, go_e, go_m, go_t))


def backward_all(*operands):
    shape = jax.ShapeDtypeStruct
    shapes = [
        shape((256, 1024), bf16),
        shape((128, 1024), f32),
        shape((32, 4096), f32),
        shape((32, 1024), f32),
        shape((32, 3072), f32),
        shape((16, 1024), f32),
    ]

    def low(*dims):
        return pltpu.VMEM(dims, bf16)

    def wide(*dims):
        return pltpu.VMEM(dims, f32)

    scratch = [
        *reduce_scratch(1, 128, 1024),
        *reduce_scratch(2, 32, 2048),
        *reduce_scratch(1, 32, 1024),
        *reduce_scratch(2, 32, 768),
        low(3, 128, 1024), low(3, 32, 2048), low(3, 32, 1024), low(32, 768),
        low(128, 1024), low(2, 32, 2048), low(32, 1024), low(4, 32, 768),
        wide(3, 16, 1024), wide(3, 16, 1024), wide(3, 16, 1024), wide(16, 1024), wide(4, 16, 1024),
        low(4, 2, 4, 32, 768), low(4, 2, 4, 32, 2048), low(4, 1, 4, 128, 1024), low(4, 1, 4, 32, 1024),
        low(2, 1024, 1024), low(2, 1024, 128), low(2, 1024, 128), low(2, 1024, 128),
        low(2, 1024, 256), wide(2, 1024, 128), low(2, 2, 512, 128), wide(512, 1024), wide(512, 128),
        low(512, 1024), low(512, 2048), low(512, 2048), wide(512, 1024), low(512, 1024),
        wide(512, 1024), low(512, 1024),
        low(2, 512, 128), low(2, 1024, 128), wide(1024, 128),
        low(1024, 768), low(4, 2, 4, 32, 768),
        low(2, 256, 1024), low(256, 1024),
        pltpu.SemaphoreType.DMA((136,)),
        pltpu.SemaphoreType.DMA((136,)),
        pltpu.SemaphoreType.DMA((24,)),
    ]
    return pl.pallas_call(
        backward_kernel,
        out_shape=shapes,
        in_specs=[ANY] * 5 + [VMEM] * 2 + [ANY] * 14 + [VMEM] * 2,
        out_specs=[VMEM] * 6,
        scratch_shapes=scratch,
        compiler_params=pltpu.CompilerParams(
            collective_id=1, has_side_effects=True, vmem_limit_bytes=61 << 20
        ),
        name="backward",
    )(*operands)


def spread_small(vectors, fsdp):
    rows = []
    for v in vectors:
        n = v.shape[0]
        wide = jnp.tile(v.astype(f32), 32)
        rows.append(jnp.where(lax.iota(jnp.int32, 32 * n) // n == fsdp, wide, 0.0))
    rows.append(jnp.zeros((3 * 1024,), f32))
    return jnp.concatenate(rows).reshape(16, 1024)


def local(
    tokens, triple, triple_bias, merger, merger_bias, first_gain, first_shift,
    expand, expand_bias, shrink, shrink_bias, second_gain, second_shift, cotangent,
):
    me = Place()
    triple_cut = triple.reshape(32, 3, 2, 2, 2, 128).transpose(2, 4, 0, 1, 3, 5).reshape(2, 2, 32, 768)
    expand_cut = expand.reshape(32, 4, 2, 512).transpose(2, 0, 1, 3).reshape(2, 32, 2048)
    small = spread_small(
        (triple_bias, merger_bias, first_gain, first_shift, expand_bias, shrink_bias, second_gain, second_shift),
        me.fsdp,
    )
    inverse = 10000.0 ** (-2.0 * np.arange(32) / 64)
    angles = np.arange(LENGTH)[:, None] * inverse[None, :]
    cosines = jnp.asarray(np.tile(np.cos(angles), (1, 4)), f32)
    sines = jnp.asarray(np.tile(np.concatenate([-np.sin(angles), np.sin(angles)], axis=1), (1, 2)), f32)
    (
        whole_t, whole_e, whole_s, whole_m, sequence, small, encoded, small_part, *kept,
    ) = forward_all(
        triple_cut, expand_cut, shrink, merger, small, tokens.reshape(256, D),
        cotangent.reshape(256, D), cosines, sines,
    )
    tokens_grad, shrink_grad, expand_grad, merger_grad, triple_grad, small_sum = backward_all(
        whole_t, whole_e, whole_s, whole_m, sequence.reshape(LENGTH, D), small, small_part, *kept, cosines, sines
    )
    flat = small_sum.reshape(-1)

    def shard(start, n):
        return lax.dynamic_slice(flat, (start + me.fsdp * n,), (n,))

    return (
        encoded.reshape(1, 256, D),
        tokens_grad.reshape(1, 256, D),
        triple_grad,
        shard(0, 96),
        merger_grad,
        shard(3072, 32),
        shard(4096, 32),
        shard(5120, 32),
        expand_grad,
        shard(6144, 128),
        shrink_grad,
        shard(10240, 32),
        shard(11264, 32),
        shard(12288, 32),
    )


def solution(mesh):
    rows = P("fsdp", "seq", None)
    matrix = P("fsdp", None)
    vector = P("fsdp")
    return jax.shard_map(
        local,
        mesh=mesh,
        in_specs=(
            rows, matrix, vector, matrix, vector, vector, vector, matrix, vector, matrix, vector,
            vector, vector, rows,
        ),
        out_specs=(
            rows, rows, matrix, vector, matrix, vector, vector, vector, matrix, vector, matrix,
            vector, vector, vector,
        ),
        check_vma=False,
    )
```

```python
import functools
import math

import jax
import jax.numpy as jnp
import numpy as np
from jax import lax
from jax.experimental import pallas as pl
from jax.experimental.pallas import tpu as pltpu
from jax.sharding import PartitionSpec as P

HEADS = 16
D = 1024
FF = 4096
LENGTH = 1024
HEAD = 64
bf16 = jnp.bfloat16
f32 = jnp.float32
norm_epsilon = 1e-05
MESH = pl.DeviceIdType.MESH
ANY = pl.BlockSpec(memory_space=pl.ANY)
VMEM = pl.BlockSpec(memory_space=pltpu.VMEM)
SIBLING = [(0, 1), (1, 0), (2, 3), (3, 2)]
ACROSS = [(0, 2), (2, 0), (1, 3), (3, 1)]


class Place:
    def __init__(self):
        seq, fsdp = lax.axis_index("seq"), lax.axis_index("fsdp")
        self.seq, self.fsdp = seq, fsdp
        self.z_lo, self.core = lax.div(seq, 2), lax.rem(seq, 2)
        self.x, rest = lax.rem(fsdp, 4), lax.div(fsdp, 4)
        self.z_hi, self.y = lax.rem(rest, 2), lax.div(rest, 2)

    def at(self, y=None, z_hi=None, x=None, z_lo=None, core=None):
        y = self.y if y is None else y
        z_hi = self.z_hi if z_hi is None else z_hi
        x = self.x if x is None else x
        z_lo = self.z_lo if z_lo is None else z_lo
        core = self.core if core is None else core
        return {"seq": z_lo * 2 + core, "fsdp": (y * 2 + z_hi) * 4 + x}

    def along_x(self, k):
        return lax.rem(self.x + k, 4)

    def along_y(self, k):
        return lax.rem(self.y + k, 4)

    def z_others(self):
        return [
            self.at(z_lo=1 - self.z_lo),
            self.at(z_hi=1 - self.z_hi, z_lo=1 - self.z_lo),
            self.at(z_hi=1 - self.z_hi),
        ]


def greet(peers):
    barrier = pltpu.get_barrier_semaphore()
    for peer in peers:
        pl.semaphore_signal(barrier, inc=1, device_id=peer, device_id_type=MESH)


def meet(peers):
    pl.semaphore_wait(pltpu.get_barrier_semaphore(), len(peers))


class Wires:
    def __init__(self, send, recv):
        self.send, self.recv, self.used, self.open = send, recv, 0, []

    def make(self, source, target, device):
        assert self.used < self.send.shape[0]
        copy = pltpu.make_async_remote_copy(
            src_ref=source,
            dst_ref=target,
            send_sem=self.send.at[self.used],
            recv_sem=self.recv.at[self.used],
            device_id=device,
            device_id_type=MESH,
        )
        self.used += 1
        return copy

    def go(self, source, target, device):
        copy = self.make(source, target, device)
        copy.start()
        self.open.append(copy)
        return copy

    def finish(self, copies):
        for copy in copies:
            copy.wait()
        self.open = [copy for copy in self.open if all(copy is not done for done in copies)]

    def drain(self):
        for copy in self.open:
            copy.wait_send()
        self.open = []


def arrive(copies):
    for copy in copies:
        copy.wait_recv()


def gather_steps(wires, me, whole):
    half = whole.shape[-1] // 2
    rows = whole.shape[-2] // 2
    low, high, both = pl.ds(0, rows), pl.ds(rows, rows), pl.ds(0, 2 * rows)
    left, right = pl.ds(0, half), pl.ds(half, half)
    on_x = (me.x, lambda i: me.at(x=i))
    on_y = (me.y, lambda i: me.at(y=i))
    hops = (
        (
            (*on_x, lambda i, r: whole.at[me.y, :, i, r, left]),
            (*on_y, lambda i, r: whole.at[i, :, me.x, r, right]),
        ),
        (
            (*on_y, lambda i, r: whole.at[i, :, :, r, left]),
            (*on_x, lambda i, r: whole.at[:, :, i, r, right]),
        ),
    )
    for hop in hops:
        direct = []
        for here, device, piece in hop:
            up, down = lax.rem(here + 1, 4), lax.rem(here + 3, 4)
            direct.append(
                (
                    wires.go(piece(here, both), piece(here, both), device(up)),
                    wires.go(piece(here, both), piece(here, both), device(down)),
                )
            )
        yield
        relayed = []
        for (here, device, piece), (from_down, from_up) in zip(hop, direct):
            up, down = lax.rem(here + 1, 4), lax.rem(here + 3, 4)
            from_down.wait_recv()
            relayed.append(wires.go(piece(down, low), piece(down, low), device(up)))
            from_up.wait_recv()
            relayed.append(wires.go(piece(up, high), piece(up, high), device(down)))
        yield
        arrive(relayed)
    yield


def dot(a, b, dims):
    return lax.dot_general(a, b, (dims, ((), ())), preferred_element_type=f32)


def turn(block, cosine, sine):
    lane = lax.broadcasted_iota(jnp.int32, block.shape, 1)
    other = jnp.where(
        lax.rem(lane, 64) < 32, pltpu.roll(block, 96, 1), pltpu.roll(block, 32, 1)
    )
    return block * cosine + other * sine


def row_norm(rows):
    centered = rows - jnp.mean(rows, axis=-1, keepdims=True)
    scale = lax.rsqrt(jnp.mean(centered * centered, axis=-1, keepdims=True) + norm_epsilon)
    return centered * scale, scale


def row_norm_backward(upstream, gain, n, scale):
    u = upstream * gain
    mean = jnp.mean(u, axis=-1, keepdims=True)
    along = jnp.mean(u * n, axis=-1, keepdims=True)
    return scale * (u - mean - n * along)


class Saves:
    def __init__(self, sems):
        self.sems, self.used, self.open = sems, 0, []

    def go(self, source, target):
        assert self.used < self.sems.shape[0]
        copy = pltpu.make_async_copy(source, target, self.sems.at[self.used])
        self.used += 1
        copy.start()
        self.open.append(copy)
        return copy

    def wait(self, copy):
        copy.wait()
        self.open = [other for other in self.open if other is not copy]

    def drain(self):
        for copy in self.open:
            copy.wait()
        self.open = []


def place_small(me, vectors, small):
    small[...] = jnp.zeros((16, 1024), f32)
    tile = pl.ds(pl.multiple_of(lax.div(me.fsdp, 4) * 128, 128), 128)
    shifted = pltpu.roll(vectors[...], lax.rem(me.fsdp, 4) * 32, 1)
    for i, row in ((1, 3), (2, 4), (3, 5), (5, 10), (6, 11), (7, 12)):
        small[row : row + 1, tile] = shifted[i : i + 1]
    tile = pl.ds(pl.multiple_of(lax.rem(me.fsdp, 8) * 128, 128), 128)
    for y in range(4):
        small[6 + y : 7 + y, tile] = jnp.where(lax.div(me.fsdp, 8) == y, vectors[4:5, :], 0.0)
    first, ahead = lax.div(me.fsdp * 96, 128), lax.rem(me.fsdp * 96, 128)
    shifted = pltpu.roll(vectors[...], ahead, 1)[0:1]
    behind = lax.broadcasted_iota(jnp.int32, (1, 128), 1) >= ahead
    for at, part in ((first, jnp.where(behind, shifted, 0.0)), (first + 1, jnp.where(behind, 0.0, shifted))):
        tile = pl.ds(pl.multiple_of(lax.rem(at, 8) * 128, 128), 128)
        for y in range(3):
            small[y : y + 1, tile] += jnp.where(lax.div(at, 8) == y, part, 0.0)


def forward_kernel(
    triple, expand, shrink, merger, vectors, tokens, cotangent, cosines, sines,
    whole_t, whole_e, whole_s, whole_m, sequence, small_full, encoded, small_grads,
    e_out, o_out, q_out, k_out, v_out, r_out, ctx_out, n_out, scale_out, low_out,
    active_out, slope_out, second_out, feed_out,
    small, small_x, small_y, small_z, sum_x, sum_y, wt, we, ws, wm, seq, ups,
    e_buf, o_buf, q_buf, k_buf, v_buf, r_buf, ctx, part, give_a, take_a, give_f, take_f,
    n_buf, scale_buf, low_buf, active_buf, slope_buf, second_buf, feed_buf,
    send, recv, local_sems,
):
    me = Place()
    wires, saves = Wires(send, recv), Saves(local_sems)
    sibling = me.at(core=1 - me.core)
    across = me.at(z_lo=1 - me.z_lo)
    partner = me.at(z_hi=1 - me.z_hi, z_lo=1 - me.z_lo)
    peers = [sibling, across, partner]
    peers += [me.at(x=me.along_x(k)) for k in (1, 2, 3)]
    peers += [me.at(y=me.along_y(k)) for k in (1, 2, 3)]
    greet(peers)
    place_small(me, vectors, small)
    meet(peers)

    mine_here = me.core == me.z_hi
    slot_t = wt.at[me.y, me.z_hi, me.x]
    slot_e = we.at[me.y, me.z_hi, me.x]
    slot_s = ws.at[me.y, 0, me.x]
    slot_m = wm.at[me.y, 0, me.x]
    def triple_cuts(z_lo):
        for t in range(3):
            for j in range(2):
                start = pl.multiple_of(t * 1024 + z_lo * 512 + j * 256 + me.core * 128, 128)
                yield triple.at[:, pl.ds(start, 128)], slot_t.at[:, pl.ds((j * 3 + t) * 128, 128)]

    def expand_cuts():
        for i in range(4):
            start = pl.multiple_of(i * 1024 + me.core * 512, 512)
            yield expand.at[:, pl.ds(start, 512)], slot_e.at[:, pl.ds(i * 512, 512)]

    z_t = [wires.go(a, b, partner) for a, b in triple_cuts(1 - me.z_lo)]
    tok_across = wires.go(tokens, seq.at[me.seq], across)
    x_small = [wires.go(small, small_x.at[k - 1], me.at(x=me.along_x(k))) for k in (1, 2, 3)]
    tok_beside = wires.go(tokens, seq.at[me.seq], sibling)
    z_e = [wires.go(a, b, partner) for a, b in expand_cuts()]
    cot_beside = wires.go(cotangent, ups.at[me.core], sibling)
    own_t = [saves.go(a, b) for a, b in triple_cuts(me.z_lo)]
    own_tok = saves.go(tokens, seq.at[me.seq])
    own_e = [saves.go(a, b) for a, b in expand_cuts()]
    own_cot = saves.go(cotangent, ups.at[me.core])
    z_s = wires.make(shrink, slot_s, partner)
    z_m = wires.make(merger, slot_m, partner)
    own_s = pltpu.make_async_copy(shrink, slot_s, local_sems.at[46])
    own_m = pltpu.make_async_copy(merger, slot_m, local_sems.at[47])

    @pl.when(mine_here)
    def _():
        z_s.start()
        z_m.start()
        own_s.start()
        own_m.start()

    go_t = gather_steps(wires, me, wt)
    go_e = gather_steps(wires, me, we)
    go_s = gather_steps(wires, me, ws)
    go_m = gather_steps(wires, me, wm)
    for copy in own_t:
        saves.wait(copy)
    arrive(z_t)
    next(go_t)
    for copy in own_e:
        saves.wait(copy)
    arrive(z_e)
    next(go_e)
    arrive(x_small)
    sum_x[...] = small[...] + small_x[0] + small_x[1] + small_x[2]
    y_small = [wires.go(sum_x, small_y.at[k - 1], me.at(y=me.along_y(k))) for k in (1, 2, 3)]
    next(go_t)

    @pl.when(mine_here)
    def _():
        own_s.wait()
        own_m.wait()

    @pl.when(jnp.logical_not(mine_here))
    def _():
        z_s.wait_recv()
        z_m.wait_recv()

    next(go_s)
    next(go_m)
    next(go_t)
    next(go_e)
    arrive(y_small)
    sum_y[...] = sum_x[...] + small_y[0] + small_y[1] + small_y[2]
    z_small = wires.go(sum_y, small_z, partner)
    next(go_s)
    next(go_m)
    next(go_e)
    next(go_t)
    next(go_m)
    next(go_s)
    z_small.wait_recv()
    small_full[...] = sum_y[...] + small_z[...]
    tok_across.wait_recv()
    far = seq.at[(1 - me.z_lo) * 2 + me.core]
    tok_relay = wires.go(far, far, sibling)
    next(go_t)
    saves.go(wt, whole_t)
    saves.wait(own_tok)
    arrive([tok_beside, tok_relay])

    def bias(row, start, n):
        return small_full[pl.ds(row, 1), pl.ds(pl.multiple_of(start, 128), n)]

    bias_t = [
        bias(t, me.z_lo * 512 + j * 256 + me.core * 128, 128) for j in range(2) for t in range(3)
    ]
    bias_t = jnp.concatenate(bias_t, axis=1)

    def project(i, carry):
        rows = pl.ds(pl.multiple_of(i * 512, 512), 512)
        pre = dot(seq[pl.ds(2 * i, 2)].reshape(512, D), wt[...].reshape(D, 768), NN) + bias_t
        cosine, sine = cosines[rows, :], sines[rows, :]
        for p in range(2):
            cut = pre[:, p * 384 : p * 384 + 128]
            q_buf[p, rows, :] = (turn(cut, cosine, sine) * 0.125).astype(bf16)
            cut = pre[:, p * 384 + 128 : p * 384 + 256]
            k_buf[p, rows, :] = turn(cut, cosine, sine).astype(bf16)
            v_buf[p, rows, pl.ds(0, 128)] = pre[:, p * 384 + 256 : p * 384 + 384].astype(bf16)
            v_buf[p, rows, pl.ds(128, 128)] = jnp.ones((512, 128), bf16)
        return carry

    lax.fori_loop(0, 2, project, 0)
    saves.go(seq, sequence)
    saves.go(q_buf, q_out)
    saves.go(k_buf, k_out)
    saves.go(v_buf, v_out)
    ctx_copies = []
    keeps = []
    for p in range(2):

        def attend(i, carry, p=p):
            rows = pl.ds(pl.multiple_of(i * 512, 512), 512)
            lane = lax.broadcasted_iota(jnp.int32, (512, 128), 1)
            found = []
            for h in range(2):
                head = (lane >= 64) if h else (lane < 64)
                q = jnp.where(head, q_buf[p, rows, :], jnp.zeros((), bf16))
                scores = dot(q, k_buf[p], NT)
                peak = jnp.max(scores, axis=1, keepdims=True)
                powers = jnp.exp(scores - peak).astype(bf16)
                e_buf[2 * p + h, rows, :] = powers
                found.append(dot(powers, v_buf[p], NN))
            first = lane < 64
            over = 1.0 / jnp.where(first, found[0][:, 128:], found[1][:, 128:])
            r_buf[p, rows, :] = over
            o_buf[p, rows, :] = (jnp.where(first, found[0][:, :128], found[1][:, :128]) * over).astype(bf16)
            return carry

        lax.fori_loop(0, 2, attend, 0)
        saves.go(e_buf.at[pl.ds(2 * p, 2)], e_out.at[pl.ds(2 * p, 2)])
        theirs = o_buf.at[p, pl.ds(pl.multiple_of((1 - me.z_lo) * 512, 512), 512)]
        ours = o_buf.at[p, pl.ds(pl.multiple_of(me.z_lo * 512, 512), 512)]
        ctx_copies.append(wires.go(theirs, ctx.at[me.z_lo, p], across))
        keeps.append(saves.go(ours, ctx.at[me.z_lo, p]))
        if p == 0:
            next(go_e)
            next(go_m)
    saves.go(r_buf, r_out)
    saves.go(o_buf, o_out)
    next(go_m)
    saves.go(wm, whole_m)
    next(go_s)
    for keep in keeps:
        saves.wait(keep)
    arrive(ctx_copies)
    ctx_rows = jnp.concatenate([ctx[0, 0], ctx[0, 1], ctx[1, 0], ctx[1, 1]], axis=1)
    merge = []
    for i in range(2):
        rows = pl.ds(i * 256, 256)
        found = dot(ctx_rows[i * 256 : i * 256 + 256], wm[...].reshape(512, D), NN)
        part[rows, :] = found
        give_a[rows, :] = found.astype(bf16)
        merge.append(wires.go(give_a.at[rows], take_a.at[rows], sibling))
    saves.go(ctx, ctx_out)
    next(go_e)
    saves.go(we, whole_e)
    bias_m, gain_1, shift_1 = bias(3, 0, D), bias(4, 0, D), bias(5, 0, D)

    def first_norm(i, carry):
        rows = pl.ds(pl.multiple_of(i * 64, 64), 64)
        at = pl.ds(pl.multiple_of(lax.rem(i, 4) * 64, 64), 64)
        inputs = seq[me.z_lo * 2 + lax.div(i, 4), at, :].astype(f32)
        total = inputs + part[rows, :] + take_a[rows, :].astype(f32) + bias_m
        n, scale = row_norm(total)
        n_buf[rows, :] = n
        scale_buf[rows, :] = jnp.broadcast_to(scale, (64, 128))
        low_buf[rows, :] = (n * gain_1 + shift_1).astype(bf16)
        return carry

    for i in range(2):
        merge[i].wait_recv()
        lax.fori_loop(4 * i, 4 * i + 4, first_norm, 0)
    saves.go(n_buf, n_out)
    saves.go(scale_buf, scale_out)
    saves.go(low_buf, low_out)

    def widen(i, carry):
        at = pl.ds(pl.multiple_of(i * 1024, 1024), 1024)
        upward = dot(low_buf[...], we[:, :, :, :, at].reshape(D, 1024), NN)
        biases = [bias(6 + 2 * i + y, me.core * 512, 512) for y in range(2)]
        upward += jnp.concatenate(biases, axis=1)
        gate = 0.5 + 0.5 * lax.erf(upward * math.sqrt(0.5))
        active_buf[:, at] = (upward * gate).astype(bf16)
        bell = jnp.exp(-0.5 * upward * upward) * (1.0 / math.sqrt(2.0 * math.pi))
        slope_buf[:, at] = (gate + upward * bell).astype(bf16)
        return carry

    lax.fori_loop(0, 1, widen, 0)
    next(go_s)
    saves.go(ws, whole_s)
    lax.fori_loop(1, 2, widen, 0)
    saves.go(active_buf, active_out)
    saves.go(slope_buf, slope_out)
    feeds = []
    for i in range(2):
        rows = pl.ds(i * 256, 256)
        found = dot(active_buf[rows, :], ws[...].reshape(2048, D), NN)
        part[rows, :] = found
        give_f[rows, :] = found.astype(bf16)
        feeds.append(wires.go(give_f.at[rows], take_f.at[rows], sibling))
    saves.wait(own_cot)
    cot_beside.wait_recv()
    bias_s, gain_2, shift_2 = bias(10, 0, D), bias(11, 0, D), bias(12, 0, D)
    small_grads[...] = jnp.zeros((16, 1024), f32)

    def second_norm(i, carry):
        rows = pl.ds(pl.multiple_of(i * 64, 64), 64)
        at = pl.ds(pl.multiple_of(lax.rem(i, 4) * 64, 64), 64)
        hidden = n_buf[rows, :] * gain_1 + shift_1
        total = hidden + part[rows, :] + take_f[rows, :].astype(f32) + bias_s
        n, scale = row_norm(total)
        upstream = ups[lax.div(i, 4), at, :].astype(f32)
        grad = row_norm_backward(upstream, gain_2, n, scale)
        second_buf[rows, :] = grad
        feed = grad.astype(bf16)
        feed_buf[rows, :] = feed

        @pl.when(lax.div(i, 4) == me.core)
        def _():
            encoded[at, :] = (n * gain_2 + shift_2).astype(bf16)
            small_grads[10:11, :] += jnp.sum(feed.astype(f32), axis=0, keepdims=True)
            small_grads[11:12, :] += jnp.sum(upstream * n, axis=0, keepdims=True)
            small_grads[12:13, :] += jnp.sum(upstream, axis=0, keepdims=True)

        return carry

    for i in range(2):
        feeds[i].wait_recv()
        lax.fori_loop(4 * i, 4 * i + 4, second_norm, 0)
    saves.go(second_buf, second_out)
    saves.go(feed_buf, feed_out)
    saves.drain()
    wires.drain()
    assert all(next(steps, "end") == "end" for steps in (go_t, go_e, go_s, go_m))

    @pl.when(mine_here)
    def _():
        z_s.wait_send()
        z_m.wait_send()


def forward_all(triple, expand, shrink, merger, vectors, tokens, cotangent, cosines, sines):
    shape = jax.ShapeDtypeStruct
    shapes = [
        shape((4, 2, 4, 32, 768), bf16),
        shape((4, 2, 4, 32, 2048), bf16),
        shape((4, 1, 4, 128, 1024), bf16),
        shape((4, 1, 4, 32, 1024), bf16),
        shape((4, 256, 1024), bf16),
        shape((16, 1024), f32),
        shape((256, 1024), bf16),
        shape((16, 1024), f32),
        shape((4, 1024, 1024), bf16),
        shape((2, 1024, 128), bf16),
        shape((2, 1024, 128), bf16),
        shape((2, 1024, 128), bf16),
        shape((2, 1024, 256), bf16),
        shape((2, 1024, 128), f32),
        shape((2, 2, 512, 128), bf16),
        shape((512, 1024), f32),
        shape((512, 128), f32),
        shape((512, 1024), bf16),
        shape((512, 2048), bf16),
        shape((512, 2048), bf16),
        shape((512, 1024), f32),
        shape((512, 1024), bf16),
    ]
    scratch = [
        pltpu.VMEM((16, 1024), f32),
        pltpu.VMEM((3, 16, 1024), f32),
        pltpu.VMEM((3, 16, 1024), f32),
        pltpu.VMEM((16, 1024), f32),
        pltpu.VMEM((16, 1024), f32),
        pltpu.VMEM((16, 1024), f32),
        pltpu.VMEM((4, 2, 4, 32, 768), bf16),
        pltpu.VMEM((4, 2, 4, 32, 2048), bf16),
        pltpu.VMEM((4, 1, 4, 128, 1024), bf16),
        pltpu.VMEM((4, 1, 4, 32, 1024), bf16),
        pltpu.VMEM((4, 256, 1024), bf16),
        pltpu.VMEM((2, 256, 1024), bf16),
        pltpu.VMEM((4, 1024, 1024), bf16),
        pltpu.VMEM((2, 1024, 128), bf16),
        pltpu.VMEM((2, 1024, 128), bf16),
        pltpu.VMEM((2, 1024, 128), bf16),
        pltpu.VMEM((2, 1024, 256), bf16),
        pltpu.VMEM((2, 1024, 128), f32),
        pltpu.VMEM((2, 2, 512, 128), bf16),
        pltpu.VMEM((512, 1024), f32),
        pltpu.VMEM((512, 1024), bf16),
        pltpu.VMEM((512, 1024), bf16),
        pltpu.VMEM((512, 1024), bf16),
        pltpu.VMEM((512, 1024), bf16),
        pltpu.VMEM((512, 1024), f32),
        pltpu.VMEM((512, 128), f32),
        pltpu.VMEM((512, 1024), bf16),
        pltpu.VMEM((512, 2048), bf16),
        pltpu.VMEM((512, 2048), bf16),
        pltpu.VMEM((512, 1024), f32),
        pltpu.VMEM((512, 1024), bf16),
        pltpu.SemaphoreType.DMA((104,)),
        pltpu.SemaphoreType.DMA((104,)),
        pltpu.SemaphoreType.DMA((48,)),
    ]
    return pl.pallas_call(
        forward_kernel,
        out_shape=shapes,
        in_specs=[ANY, ANY, ANY, ANY, VMEM, ANY, ANY, VMEM, VMEM],
        out_specs=[ANY] * 5 + [VMEM] * 3 + [ANY] * 14,
        scratch_shapes=scratch,
        compiler_params=pltpu.CompilerParams(
            collective_id=0, has_side_effects=True, vmem_limit_bytes=58 << 20
        ),
        name="forward",
    )(triple, expand, shrink, merger, vectors, tokens, cotangent, cosines, sines)


NN = ((1,), (0,))
NT = ((1,), (1,))
TN = ((0,), (0,))


def reduce_steps(wires, me, grad, buffers, out):
    first_l, first_r, mid_l, mid_r, last_l, last_r = buffers
    levels, half, h = grad.shape[1], grad.shape[4] // 2, grad.shape[3] // 2
    left, right = pl.ds(0, half), pl.ds(half, half)
    upper, lower = pl.ds(0, h), pl.ds(h, h)
    on_x = (me.x, lambda i: me.at(x=i))
    on_y = (me.y, lambda i: me.at(y=i))

    def in_mid_l(n, r, value):
        mid_l[lax.div(n, levels), lax.rem(n, levels), r, :] = value

    def in_mid_r(n, r, value):
        mid_r[lax.div(n, 4), lax.rem(n, 4), r, :] = value

    def in_out_l(n, r, value):
        out[n, r, left] = value

    def in_out_r(n, r, value):
        out[n, r, right] = value

    hops = (
        (
            (
                *on_x, 4 * levels, lambda n: (lax.div(n, levels), lax.rem(n, levels)), first_l,
                lambda d, r: grad.at[:, :, d, r, left],
                lambda d, n, r: grad[lax.div(n, levels), lax.rem(n, levels), d, r, left],
                in_mid_l,
            ),
            (
                *on_y, 4 * levels, lambda n: (lax.div(n, 4), lax.rem(n, 4)), first_r,
                lambda d, r: grad.at[d, :, :, r, right],
                lambda d, n, r: grad[d, lax.div(n, 4), lax.rem(n, 4), r, right],
                in_mid_r,
            ),
        ),
        (
            (
                *on_y, levels, lambda n: (n,), last_l,
                lambda d, r: mid_l.at[d, :, r, :],
                lambda d, n, r: mid_l[d, n, r, :],
                in_out_l,
            ),
            (
                *on_x, levels, lambda n: (n,), last_r,
                lambda d, r: mid_r.at[:, d, r, :],
                lambda d, n, r: mid_r[n, d, r, :],
                in_out_r,
            ),
        ),
    )
    for hop in hops:
        sent = []
        for here, device, count, index, (relay, near, far), piece, value, store in hop:
            up, down, corner = lax.rem(here + 1, 4), lax.rem(here + 3, 4), lax.rem(here + 2, 4)
            sent.append(
                (
                    wires.go(piece(corner, upper), relay.at[0], device(up)),
                    wires.go(piece(corner, lower), relay.at[1], device(down)),
                    wires.go(piece(up, lower), near.at[0], device(up)),
                    wires.go(piece(down, upper), near.at[1], device(down)),
                )
            )
        yield
        summed = []
        for (here, device, count, index, (relay, near, far), piece, value, store), copies in zip(hop, sent):
            up, down = lax.rem(here + 1, 4), lax.rem(here + 3, 4)
            arrive(copies[:2])

            def pass_on(n, carry, relay=relay, value=value, index=index, up=up, down=down):
                at = (0, *index(n))
                relay[at] = (relay[at].astype(f32) + value(up, n, upper).astype(f32)).astype(bf16)
                at = (1, *index(n))
                relay[at] = (relay[at].astype(f32) + value(down, n, lower).astype(f32)).astype(bf16)
                return carry

            lax.fori_loop(0, count, pass_on, 0)
            summed.append(wires.go(relay.at[0], far.at[0], device(up)))
            summed.append(wires.go(relay.at[1], far.at[1], device(down)))
        yield
        arrive(summed)
        for (here, device, count, index, (relay, near, far), piece, value, store), copies in zip(hop, sent):
            arrive(copies[2:])

            def finish(n, carry, near=near, far=far, value=value, index=index, store=store, here=here):
                for r, i in ((upper, 0), (lower, 1)):
                    total = value(here, n, r).astype(f32)
                    total += near[(1 - i, *index(n))].astype(f32) + far[(i, *index(n))].astype(f32)
                    store(n, r, total.astype(bf16))
                return carry

            lax.fori_loop(0, count, finish, 0)
    yield


def reduce_scratch(levels, rows, columns):
    half, h = columns // 2, rows // 2

    def trio(*lead):
        return [pltpu.VMEM((2, *lead, h, half), bf16)] * 3

    return [
        *trio(4, levels),
        *trio(levels, 4),
        pltpu.VMEM((4, levels, rows, half), bf16),
        pltpu.VMEM((levels, 4, rows, half), bf16),
        *trio(levels),
        *trio(levels),
        pltpu.VMEM((levels, rows, columns), bf16),
    ]


def reduce_job(wires, me, grad, scratch):
    buffers = (scratch[0:3], scratch[3:6], scratch[6], scratch[7], scratch[8:11], scratch[11:14])
    return reduce_steps(wires, me, grad, buffers, scratch[14])


def triple_steps(wires, me, grad, first_l, first_r, mid_l, mid_r, last_l, last_r, out, shares):
    upper, lower = pl.ds(0, 16), pl.ds(16, 16)
    one = []
    for k in (2, 1, 3):
        x, y = me.along_x(k), me.along_y(k)
        one.append(wires.go(grad.at[:, :, x, upper, :], first_l.at[k - 1], me.at(x=x)))
        one.append(wires.go(grad.at[y, :, :, lower, :], first_r.at[k - 1], me.at(y=y)))
    yield
    arrive(one)

    def total(n, carry):
        y, z = lax.div(n, 2), lax.rem(n, 2)
        left = grad[y, z, me.x, upper, :].astype(f32)
        right = grad[me.y, z, y, lower, :].astype(f32)
        for k in range(3):
            left += first_l[k, y, z].astype(f32)
            right += first_r[k, z, y].astype(f32)
        mid_l[y, z] = left.astype(bf16)
        mid_r[z, y] = right.astype(bf16)
        return carry

    lax.fori_loop(0, 8, total, 0)
    two = []
    for k in range(1, 8):
        z = 1 - me.z_hi if k % 2 else me.z_hi
        x, y = me.along_x(k // 2), me.along_y(k // 2)
        two.append(wires.go(mid_l.at[y, z], last_l.at[k - 1], me.at(y=y, z_hi=z)))
        two.append(wires.go(mid_r.at[z, x], last_r.at[k - 1], me.at(x=x, z_hi=z)))
    yield
    arrive(two)
    left = mid_l[me.y, me.z_hi].astype(f32)
    right = mid_r[me.z_hi, me.x].astype(f32)
    for k in range(7):
        left += last_l[k].astype(f32)
        right += last_r[k].astype(f32)
    out[me.seq, upper, :] = left.astype(bf16)
    out[me.seq, lower, :] = right.astype(bf16)
    spread = [wires.go(out.at[me.seq], out.at[me.seq], peer) for peer in shares]
    yield
    arrive(spread)
    yield


def triple_scratch():
    return [
        pltpu.VMEM((4, 2, 4, 32, 384), bf16),
        pltpu.VMEM((3, 4, 2, 16, 384), bf16),
        pltpu.VMEM((3, 2, 4, 16, 384), bf16),
        pltpu.VMEM((4, 2, 16, 384), bf16),
        pltpu.VMEM((2, 4, 16, 384), bf16),
        pltpu.VMEM((7, 16, 384), bf16),
        pltpu.VMEM((7, 16, 384), bf16),
    ]


def small_steps(wires, me, sums, by_x, by_y, by_z, by_core, out):
    got = [wires.go(sums.at[0], by_x.at[k - 1], me.at(x=me.along_x(k))) for k in (1, 2, 3)]
    yield
    arrive(got)
    sums[1] = sums[0] + by_x[0] + by_x[1] + by_x[2]
    got = [wires.go(sums.at[1], by_y.at[k - 1], me.at(y=me.along_y(k))) for k in (1, 2, 3)]
    yield
    arrive(got)
    sums[2] = sums[1] + by_y[0] + by_y[1] + by_y[2]
    got = [wires.go(sums.at[2], by_z.at[k], peer) for k, peer in enumerate(me.z_others())]
    yield
    arrive(got)
    sums[3] = sums[2] + by_z[0] + by_z[1] + by_z[2]
    got = wires.go(sums.at[3], by_core, me.at(core=1 - me.core))
    yield
    got.wait_recv()
    out[...] = sums[3] + by_core[...]
    yield


def small_scratch(rows):
    return [
        pltpu.VMEM((4, rows, 1024), f32),
        pltpu.VMEM((3, rows, 1024), f32),
        pltpu.VMEM((3, rows, 1024), f32),
        pltpu.VMEM((3, rows, 1024), f32),
        pltpu.VMEM((rows, 1024), f32),
    ]


def backward_kernel(
    whole_t, whole_e, whole_s, whole_m, sequence, small_full, small_part,
    e_in, o_in, q_in, k_in, v_in, r_in, ctx_in, n_in, scale_in, low_in,
    active_in, slope_in, second_in, feed_in, cosines, sines,
    tokens_out, sum_s, sum_e, sum_m, sum_t, small_out, bias_out, *rest,
):
    me = Place()
    scratch_s, scratch_e, scratch_m = (rest[15 * i : 15 * i + 15] for i in range(3))
    scratch_t = (rest[45:52], rest[52:59])
    scratch_small, scratch_bias = rest[59:64], rest[64:69]
    sums, biases = scratch_small[0], scratch_bias[0]
    (
        z_s, z_e, z_m,
        wt, we, ws, wm, e_buf, o_buf, q_buf, k_buf, v_buf, r_buf, ctx, n_buf, scale_buf,
        low_buf, active_buf, slope_buf, second_buf, feed_buf, part, take_a,
        give_c, dctx, dq_buf, pre_grad, take_t, take_x, send, recv, local_sems,
    ) = rest[69:]
    give_a = feed_buf
    acc_k, acc_v = second_buf.at[pl.ds(0, 128)], second_buf.at[pl.ds(128, 128)]
    give_t = [active_buf.at[pl.ds(256 * z, 256), pl.ds(0, D)] for z in range(2)]
    give_x = active_buf.at[pl.ds(0, 256), pl.ds(D, D)]
    wires, saves = Wires(send, recv), Saves(local_sems)
    sibling = me.at(core=1 - me.core)
    beside, diagonal, beyond = me.z_others()
    load_first = [
        saves.go(feed_in, feed_buf), saves.go(whole_s, ws), saves.go(slope_in, slope_buf),
        saves.go(active_in, active_buf),
    ]
    crossing = me.at(z_lo=1 - me.z_lo, core=1 - me.core)
    peers = [sibling, beside, diagonal, beyond, crossing]
    for z in (me.z_hi, 1 - me.z_hi):
        peers += [me.at(x=me.along_x(k), z_hi=z) for k in (1, 2, 3)]
        peers += [me.at(y=me.along_y(k), z_hi=z) for k in (1, 2, 3)]
    greet(peers)
    go_s = reduce_job(wires, me, ws, scratch_s)
    go_e = reduce_job(wires, me, we, scratch_e)
    go_m = reduce_job(wires, me, wm, scratch_m)
    plane_s, plane_e, plane_m = (s[14] for s in (scratch_s, scratch_e, scratch_m))
    go_small = small_steps(wires, me, *scratch_small, small_out)
    go_bias = small_steps(wires, me, *scratch_bias, bias_out)
    biases[0] = jnp.zeros((8, 1024), f32)
    go_t = [
        triple_steps(wires, me, *scratch_t[p], sum_t.at[p], (sibling, beside, crossing))
        for p in range(2)
    ]
    sums[0] = small_part[...]

    for load in load_first:
        saves.wait(load)
    load_e, load_low = saves.go(whole_e, we), saves.go(low_in, low_buf)
    load_norm = [saves.go(n_in, n_buf), saves.go(scale_in, scale_buf), saves.go(second_in, second_buf)]
    load_m = [saves.go(whole_m, wm), saves.go(ctx_in, ctx)]

    def narrow(y, carry):
        at = pl.ds(pl.multiple_of(y * 512, 512), 512)
        back = dot(feed_buf[...], ws[y].reshape(512, D), NT)
        up = (back * slope_buf[:, at].astype(f32)).astype(bf16)
        slope_buf[:, at] = up
        where = pl.ds(pl.multiple_of(me.core * 512, 512), 512)
        sums[0, pl.ds(6 + y, 1), where] = jnp.sum(up.astype(f32), axis=0, keepdims=True)
        ws[y] = dot(active_buf[:, at], feed_buf[...], TN).astype(bf16).reshape(1, 4, 128, D)
        return carry

    lax.fori_loop(0, 4, narrow, 0)
    load_seq = [
        saves.go(sequence.at[pl.ds(512 * i, 512)], active_buf.at[:, pl.ds(D * i, D)]) for i in range(2)
    ]
    meet(peers)
    next(go_s)
    saves.wait(load_e)

    def hidden_part(i, carry):
        at = pl.ds(pl.multiple_of(i * 512, 512), 512)
        found = dot(slope_buf[...], we[pl.ds(2 * i, 2)].reshape(512, 2048), NT)
        part[:, at] = found
        give_a[:, at] = found.astype(bf16)
        return carry

    shared = []
    for i in range(2):
        lax.fori_loop(i, i + 1, hidden_part, 0)
        at = pl.ds(512 * i, 512)
        shared.append(wires.go(give_a.at[:, at], take_a.at[:, at], sibling))
    saves.wait(load_low)
    load_heads = [
        saves.go(e_in.at[0], e_buf.at[0]), saves.go(e_in.at[1], e_buf.at[1]), saves.go(o_in, o_buf),
        saves.go(q_in, q_buf), saves.go(k_in, k_buf), saves.go(v_in, v_buf), saves.go(r_in, r_buf),
    ]
    load_t = saves.go(whole_t, wt)

    def expand_part(y, carry):
        low = low_buf[:, pl.ds(pl.multiple_of(y * 256, 256), 256)]
        we[y] = dot(low, slope_buf[...], TN).astype(bf16).reshape(2, 4, 32, 2048)
        return carry

    lax.fori_loop(0, 2, expand_part, 0)
    for load in load_norm:
        saves.wait(load)
    wires.finish(shared)
    turned_buf = give_a
    gain_1 = small_full[4:5, :]

    def first_norm(i, carry):
        rows = pl.ds(pl.multiple_of(i * 64, 64), 64)
        upstream = part[rows, :] + take_a[rows, :].astype(f32) + second_buf[rows, :]
        n = n_buf[rows, :]
        grad = row_norm_backward(upstream, gain_1, n, scale_buf[rows, 0:1])
        n_buf[rows, :] = grad
        low = grad.astype(bf16)
        turned_buf[rows, :] = low

        @pl.when(lax.div(i, 4) == me.core)
        def _():
            sums[0, 3:4, :] += jnp.sum(low.astype(f32), axis=0, keepdims=True)
            sums[0, 4:5, :] += jnp.sum(upstream * n, axis=0, keepdims=True)
            sums[0, 5:6, :] += jnp.sum(upstream, axis=0, keepdims=True)

        return carry

    lax.fori_loop(0, 8, first_norm, 0)
    next(go_small)
    for load in load_m:
        saves.wait(load)

    def context_part(group):
        return dot(turned_buf[...], wm[pl.ds(2 * group, 2)].reshape(256, D), NT).astype(bf16)

    found = context_part(1 - me.z_lo)
    give_c[0] = found[:, :128]
    give_c[1] = found[:, 128:]
    chip = pl.ds(pl.multiple_of(me.z_lo * 512, 512), 512)
    swapped = wires.go(give_c, dctx.at[:, chip, :], beside)
    found = context_part(me.z_lo)
    dctx[0, chip, :] = found[:, :128]
    dctx[1, chip, :] = found[:, 128:]
    lax.fori_loop(2, 4, expand_part, 0)
    next(go_s)
    next(go_e)
    for z in range(2):
        for p in range(2):
            found = dot(ctx[z, p], turned_buf[...], TN).astype(bf16)
            wm[2 * z + p] = found.reshape(1, 4, 32, D)
    next(go_m)
    for load in load_heads:
        saves.wait(load)
    swapped.wait_recv()

    def head_back(p, h):
        slot = h

        def block(i, carry):
            rows = pl.ds(pl.multiple_of(i * 512, 512), 512)
            lane = lax.broadcasted_iota(jnp.int32, (512, 128), 1)
            head = (lane >= 64) if h else (lane < 64)
            scaled = jnp.where(head, dctx[p, rows, :].astype(f32) * r_buf[p, rows, :], 0.0).astype(bf16)
            delta = jnp.sum(scaled.astype(f32) * o_buf[p, rows, :].astype(f32), axis=1, keepdims=True)
            high = delta.astype(bf16).astype(f32)
            extra = jnp.where(lane == 0, -high, jnp.where(lane == 1, high - delta, 0.0)).astype(bf16)
            given = jnp.concatenate([scaled, extra], axis=1)
            prob_grad = dot(given, v_buf[p], NT)
            powers = e_buf[slot, rows, :]
            score_grad = (powers.astype(f32) * prob_grad).astype(bf16)
            dq = dot(score_grad, k_buf[p], NN)
            if h == 0:
                dq_buf[rows, :] = dq
            else:
                dq = jnp.where(lane < 64, dq_buf[rows, :], dq)
                dq = (dq * 0.125).astype(bf16).astype(f32)
                turned = turn(dq, cosines[rows, :], -sines[rows, :])
                pre_grad[p, rows, pl.ds(0, 128)] = turned.astype(bf16)
            q = jnp.where(head, q_buf[p, rows, :], jnp.zeros((), bf16))
            acc_k[...] += dot(q, score_grad, TN)
            acc_v[...] += dot(scaled, powers, TN)
            return carry

        lax.fori_loop(0, 2, block, 0)

    def pair_end(p):
        def block(i, carry):
            rows = pl.ds(pl.multiple_of(i * 256, 256), 256)
            dk = acc_k[:, rows].T.astype(bf16).astype(f32)
            turned = turn(dk, cosines[rows, :], -sines[rows, :])
            pre_grad[p, rows, pl.ds(128, 128)] = turned.astype(bf16)
            pre_grad[p, rows, pl.ds(256, 128)] = acc_v[:, rows].T.astype(bf16)
            return carry

        lax.fori_loop(0, 4, block, 0)
        found = dot(active_buf[:, 0:D], pre_grad[p, 0:512, :], TN)
        found += dot(active_buf[:, D:], pre_grad[p, 512:, :], TN)
        scratch_t[p][0][...] = found.astype(bf16).reshape(4, 2, 4, 32, 384)
        next(go_t[p])

    def bias_part(p):
        def block(i, total):
            rows = pl.ds(pl.multiple_of(i * 256, 256), 256)
            return total + jnp.sum(pre_grad[p, rows, :].astype(f32), axis=0, keepdims=True)

        total = lax.fori_loop(0, 4, block, jnp.zeros((1, 384), f32))
        at = pl.ds(pl.multiple_of(me.z_lo * 512 + p * 256 + me.core * 128, 128), 128)
        for t in range(3):
            biases[0, t : t + 1, at] = total[:, t * 128 : t * 128 + 128]

    def clear():
        acc_k[...] = jnp.zeros((128, D), f32)
        acc_v[...] = jnp.zeros((128, D), f32)

    clear()
    head_back(0, 0)
    load_2 = saves.go(e_in.at[2], e_buf.at[0])
    next(go_e)
    next(go_small)
    head_back(0, 1)
    load_3 = saves.go(e_in.at[3], e_buf.at[1])
    next(go_s)
    for load in load_seq:
        saves.wait(load)
    pair_end(0)
    clear()
    next(go_m)
    next(go_small)
    saves.wait(load_2)
    head_back(1, 0)
    next(go_t[0])
    next(go_m)
    next(go_e)
    next(go_s)
    next(go_small)
    saves.wait(load_3)
    head_back(1, 1)
    pair_end(1)
    saves.wait(load_t)

    def tokens_part(z, core):
        rows = pl.ds(pl.multiple_of((2 * z + core) * 256, 256), 256)
        found = dot(pre_grad[0, rows, :], wt[:, :, :, :, 0:384].reshape(D, 384), NT)
        return found + dot(pre_grad[1, rows, :], wt[:, :, :, :, 384:768].reshape(D, 384), NT)

    beside_rows = []
    for i, z in enumerate((1 - me.z_lo, me.z_lo)):
        give_t[i][...] = tokens_part(z, 1 - me.core).astype(bf16)
        beside_rows.append(wires.go(give_t[i], take_t.at[i], sibling))
        if i == 0:
            far_rows = tokens_part(z, me.core)
            beside_rows[0].wait_recv()
            give_x[...] = (far_rows + take_t[0].astype(f32)).astype(bf16)
            across_rows = wires.go(give_x, take_x, beside)
    bias_part(0)
    bias_part(1)
    next(go_bias)
    part[0:256, :] = tokens_part(me.z_lo, me.core)
    next(go_t[0])
    next(go_s)
    next(go_m)
    next(go_e)
    owner = me.core == me.z_hi
    late = []

    def to_owners(plane, slots):
        copies = [
            wires.make(plane.at[0], slots.at[k], peer)
            for k, peer in enumerate((beside, diagonal, beyond))
        ]

        @pl.when(owner)
        def _():
            copies[0].start()

        @pl.when(jnp.logical_not(owner))
        def _():
            copies[1].start()
            copies[2].start()

        late.append(copies)
        return copies

    def finish_owned(plane, slots, copies, out):
        beside_copy = wires.make(out, out, sibling)

        @pl.when(owner)
        def _():
            arrive(copies)
            total = plane[0].astype(f32)
            for k in range(3):
                total += slots[k].astype(f32)
            out[...] = total.astype(bf16)
            beside_copy.start()

        return beside_copy

    copies_s = to_owners(plane_s, z_s)
    next(go_t[1])
    next(go_bias)
    next(go_e)
    flip = 1 - me.z_hi
    copies_e = [
        wires.go(plane_e.at[level], z_e.at[k], peer)
        for k, (level, peer) in enumerate(((me.z_hi, beside), (flip, diagonal), (flip, beyond)))
    ]
    next(go_m)
    copies_m = to_owners(plane_m, z_m)
    next(go_bias)
    next(go_t[1])
    next(go_small)
    beside_s = finish_owned(plane_s, z_s, copies_s, sum_s)
    arrive(copies_e)
    total = plane_e[me.z_hi].astype(f32)
    for k in range(3):
        total += z_e[k].astype(f32)
    sum_e[me.core] = total.astype(bf16)
    beside_e = wires.go(sum_e.at[me.core], sum_e.at[me.core], sibling)
    beside_m = finish_owned(plane_m, z_m, copies_m, sum_m)
    next(go_bias)
    arrive([across_rows, beside_rows[1]])
    own = pl.ds(pl.multiple_of(me.core * 256, 256), 256)
    tokens_out[...] = (
        part[0:256, :] + take_t[1].astype(f32) + take_x[...].astype(f32) + n_buf[own, :]
    ).astype(bf16)
    next(go_t[0])
    next(go_t[1])
    next(go_bias)

    @pl.when(jnp.logical_not(owner))
    def _():
        beside_s.wait_recv()
        beside_m.wait_recv()
        for copies in late:
            copies[1].wait_send()
            copies[2].wait_send()

    @pl.when(owner)
    def _():
        beside_s.wait_send()
        beside_m.wait_send()
        for copies in late:
            copies[0].wait_send()

    beside_e.wait_recv()
    wires.drain()
    saves.drain()
    assert all(next(steps, "end") == "end" for steps in (go_s, go_e, go_m, *go_t, go_small, go_bias))


def backward_all(*operands):
    shape = jax.ShapeDtypeStruct
    shapes = [
        shape((256, 1024), bf16),
        shape((128, 1024), bf16),
        shape((2, 32, 2048), bf16),
        shape((32, 1024), bf16),
        shape((2, 4, 32, 384), bf16),
        shape((16, 1024), f32),
        shape((8, 1024), f32),
    ]

    def low(*dims):
        return pltpu.VMEM(dims, bf16)

    def wide(*dims):
        return pltpu.VMEM(dims, f32)

    scratch = [
        *reduce_scratch(1, 128, 1024),
        *reduce_scratch(2, 32, 2048),
        *reduce_scratch(1, 32, 1024),
        *triple_scratch(),
        *triple_scratch(),
        *small_scratch(16),
        *small_scratch(8),
        low(3, 128, 1024), low(3, 32, 2048), low(3, 32, 1024),
        low(4, 2, 4, 32, 768), low(4, 2, 4, 32, 2048), low(4, 1, 4, 128, 1024), low(4, 1, 4, 32, 1024),
        low(2, 1024, 1024), low(2, 1024, 128), low(2, 1024, 128), low(2, 1024, 128),
        low(2, 1024, 256), wide(2, 1024, 128), low(2, 2, 512, 128), wide(512, 1024), wide(512, 128),
        low(512, 1024), low(512, 2048), low(512, 2048), wide(512, 1024), low(512, 1024),
        wide(512, 1024), low(512, 1024),
        low(2, 512, 128), low(2, 1024, 128), wide(1024, 128),
        low(2, 1024, 384),
        low(2, 256, 1024), low(256, 1024),
        pltpu.SemaphoreType.DMA((160,)),
        pltpu.SemaphoreType.DMA((160,)),
        pltpu.SemaphoreType.DMA((24,)),
    ]
    return pl.pallas_call(
        backward_kernel,
        out_shape=shapes,
        in_specs=[ANY] * 5 + [VMEM] * 2 + [ANY] * 14 + [VMEM] * 2,
        out_specs=[VMEM] * 7,
        scratch_shapes=scratch,
        compiler_params=pltpu.CompilerParams(
            collective_id=1, has_side_effects=True, vmem_limit_bytes=61 << 20
        ),
        name="backward",
    )(*operands)


def finish_kernel(tokens, encoded, sum_s, sum_e, sum_m, sum_t, *rest):
    tokens_out, encoded_out, out_s, out_e, out_m, out_t = rest
    tokens_out[...] = tokens[...]
    encoded_out[...] = encoded[...]
    out_s[...] = sum_s[...].astype(f32)
    out_m[...] = sum_m[...].astype(f32)
    for c in range(2):
        for y in range(4):
            start = y * 1024 + c * 512
            out_e[:, start : start + 512] = sum_e[c, :, y * 512 : y * 512 + 512].astype(f32)
    for s in range(4):
        for t in range(3):
            for j in range(2):
                start = t * 1024 + (s // 2) * 512 + j * 256 + (s % 2) * 128
                out_t[:, start : start + 128] = sum_t[j, s, :, t * 128 : t * 128 + 128].astype(f32)


def finish_all(*operands):
    shape = jax.ShapeDtypeStruct
    shapes = [
        shape((256, 1024), bf16),
        shape((256, 1024), bf16),
        shape((128, 1024), f32),
        shape((32, 4096), f32),
        shape((32, 1024), f32),
        shape((32, 3072), f32),
    ]
    return pl.pallas_call(
        finish_kernel,
        out_shape=shapes,
        in_specs=[VMEM] * 6,
        out_specs=[VMEM] * 6,
        compiler_params=pltpu.CompilerParams(vmem_limit_bytes=60 << 20),
        name="finish",
    )(*operands)


def local(
    tokens, triple, triple_bias, merger, merger_bias, first_gain, first_shift,
    expand, expand_bias, shrink, shrink_bias, second_gain, second_shift, cotangent,
):
    me = Place()
    vectors = (
        triple_bias, merger_bias, first_gain, first_shift, expand_bias, shrink_bias, second_gain, second_shift,
    )
    vectors = jnp.stack([jnp.pad(v, (0, 128 - v.shape[0])) for v in vectors]).astype(f32)
    inverse = 10000.0 ** (-2.0 * np.arange(32) / 64)
    angles = np.arange(LENGTH)[:, None] * inverse[None, :]
    cosines = jnp.asarray(np.tile(np.cos(angles), (1, 4)), f32)
    sines = jnp.asarray(np.tile(np.concatenate([-np.sin(angles), np.sin(angles)], axis=1), (1, 2)), f32)
    (
        whole_t, whole_e, whole_s, whole_m, sequence, small, encoded, small_part, *kept,
    ) = forward_all(
        triple, expand, shrink, merger, vectors, tokens.reshape(256, D),
        cotangent.reshape(256, D), cosines, sines,
    )
    tokens_grad, sum_s, sum_e, sum_m, sum_t, small_sum, bias_sum = backward_all(
        whole_t, whole_e, whole_s, whole_m, sequence.reshape(LENGTH, D), small, small_part, *kept, cosines, sines
    )
    tokens_grad, encoded, shrink_grad, expand_grad, merger_grad, triple_grad = finish_all(
        tokens_grad, encoded, sum_s, sum_e, sum_m, sum_t
    )
    flat = small_sum.reshape(-1)

    def shard(start, n):
        return lax.dynamic_slice(flat, (start + me.fsdp * n,), (n,))

    return (
        encoded.reshape(1, 256, D),
        tokens_grad.reshape(1, 256, D),
        triple_grad,
        lax.dynamic_slice(bias_sum.reshape(-1), (me.fsdp * 96,), (96,)),
        merger_grad,
        shard(3072, 32),
        shard(4096, 32),
        shard(5120, 32),
        expand_grad,
        shard(6144, 128),
        shrink_grad,
        shard(10240, 32),
        shard(11264, 32),
        shard(12288, 32),
    )


def solution(mesh):
    rows = P("fsdp", "seq", None)
    matrix = P("fsdp", None)
    vector = P("fsdp")
    return jax.shard_map(
        local,
        mesh=mesh,
        in_specs=(
            rows, matrix, vector, matrix, vector, vector, vector, matrix, vector, matrix, vector,
            vector, vector, rows,
        ),
        out_specs=(
            rows, rows, matrix, vector, matrix, vector, vector, vector, matrix, vector, matrix,
            vector, vector, vector,
        ),
        check_vma=False,
    )
```

```python
import functools
import math

import jax
import jax.numpy as jnp
import numpy as np
from jax import lax
from jax.experimental import pallas as pl
from jax.experimental.pallas import tpu as pltpu
from jax.sharding import PartitionSpec as P

HEADS = 16
D = 1024
FF = 4096
LENGTH = 1024
HEAD = 64
bf16 = jnp.bfloat16
f32 = jnp.float32
norm_epsilon = 1e-05
MESH = pl.DeviceIdType.MESH
ANY = pl.BlockSpec(memory_space=pl.ANY)
VMEM = pl.BlockSpec(memory_space=pltpu.VMEM)
SIBLING = [(0, 1), (1, 0), (2, 3), (3, 2)]
ACROSS = [(0, 2), (2, 0), (1, 3), (3, 1)]


class Place:
    def __init__(self):
        seq, fsdp = lax.axis_index("seq"), lax.axis_index("fsdp")
        self.seq, self.fsdp = seq, fsdp
        self.z_lo, self.core = lax.div(seq, 2), lax.rem(seq, 2)
        self.x, rest = lax.rem(fsdp, 4), lax.div(fsdp, 4)
        self.z_hi, self.y = lax.rem(rest, 2), lax.div(rest, 2)

    def at(self, y=None, z_hi=None, x=None, z_lo=None, core=None):
        y = self.y if y is None else y
        z_hi = self.z_hi if z_hi is None else z_hi
        x = self.x if x is None else x
        z_lo = self.z_lo if z_lo is None else z_lo
        core = self.core if core is None else core
        return {"seq": z_lo * 2 + core, "fsdp": (y * 2 + z_hi) * 4 + x}

    def along_x(self, k):
        return lax.rem(self.x + k, 4)

    def along_y(self, k):
        return lax.rem(self.y + k, 4)

    def z_others(self):
        return [
            self.at(z_lo=1 - self.z_lo),
            self.at(z_hi=1 - self.z_hi, z_lo=1 - self.z_lo),
            self.at(z_hi=1 - self.z_hi),
        ]


def greet(peers):
    barrier = pltpu.get_barrier_semaphore()
    for peer in peers:
        pl.semaphore_signal(barrier, inc=1, device_id=peer, device_id_type=MESH)


def meet(peers):
    pl.semaphore_wait(pltpu.get_barrier_semaphore(), len(peers))


class Wires:
    def __init__(self, send, recv):
        self.send, self.recv, self.used, self.open = send, recv, 0, []

    def make(self, source, target, device):
        assert self.used < self.send.shape[0]
        copy = pltpu.make_async_remote_copy(
            src_ref=source,
            dst_ref=target,
            send_sem=self.send.at[self.used],
            recv_sem=self.recv.at[self.used],
            device_id=device,
            device_id_type=MESH,
        )
        self.used += 1
        return copy

    def go(self, source, target, device):
        copy = self.make(source, target, device)
        copy.start()
        self.open.append(copy)
        return copy

    def finish(self, copies):
        for copy in copies:
            copy.wait()
        self.open = [copy for copy in self.open if all(copy is not done for done in copies)]

    def drain(self):
        for copy in self.open:
            copy.wait_send()
        self.open = []


def arrive(copies):
    for copy in copies:
        copy.wait_recv()


def gather_steps(wires, me, whole):
    half = whole.shape[-1] // 2
    rows = whole.shape[-2] // 2
    low, high, both = pl.ds(0, rows), pl.ds(rows, rows), pl.ds(0, 2 * rows)
    left, right = pl.ds(0, half), pl.ds(half, half)
    on_x = (me.x, lambda i: me.at(x=i))
    on_y = (me.y, lambda i: me.at(y=i))
    hops = (
        (
            (*on_x, lambda i, r: whole.at[me.y, :, i, r, left]),
            (*on_y, lambda i, r: whole.at[i, :, me.x, r, right]),
        ),
        (
            (*on_y, lambda i, r: whole.at[i, :, :, r, left]),
            (*on_x, lambda i, r: whole.at[:, :, i, r, right]),
        ),
    )
    for hop in hops:
        direct = []
        for here, device, piece in hop:
            up, down = lax.rem(here + 1, 4), lax.rem(here + 3, 4)
            direct.append(
                (
                    wires.go(piece(here, both), piece(here, both), device(up)),
                    wires.go(piece(here, both), piece(here, both), device(down)),
                )
            )
        yield
        relayed = []
        for (here, device, piece), (from_down, from_up) in zip(hop, direct):
            up, down = lax.rem(here + 1, 4), lax.rem(here + 3, 4)
            from_down.wait_recv()
            relayed.append(wires.go(piece(down, low), piece(down, low), device(up)))
            from_up.wait_recv()
            relayed.append(wires.go(piece(up, high), piece(up, high), device(down)))
        yield
        arrive(relayed)
    yield


def dot(a, b, dims):
    return lax.dot_general(a, b, (dims, ((), ())), preferred_element_type=f32)


def turn(block, cosine, sine):
    lane = lax.broadcasted_iota(jnp.int32, block.shape, 1)
    other = jnp.where(
        lax.rem(lane, 64) < 32, pltpu.roll(block, 96, 1), pltpu.roll(block, 32, 1)
    )
    return block * cosine + other * sine


def row_norm(rows):
    centered = rows - jnp.mean(rows, axis=-1, keepdims=True)
    scale = lax.rsqrt(jnp.mean(centered * centered, axis=-1, keepdims=True) + norm_epsilon)
    return centered * scale, scale


def row_norm_backward(upstream, gain, n, scale):
    u = upstream * gain
    mean = jnp.mean(u, axis=-1, keepdims=True)
    along = jnp.mean(u * n, axis=-1, keepdims=True)
    return scale * (u - mean - n * along)


class Saves:
    def __init__(self, sems):
        self.sems, self.used, self.open = sems, 0, []

    def go(self, source, target):
        assert self.used < self.sems.shape[0]
        copy = pltpu.make_async_copy(source, target, self.sems.at[self.used])
        self.used += 1
        copy.start()
        self.open.append(copy)
        return copy

    def wait(self, copy):
        copy.wait()
        self.open = [other for other in self.open if other is not copy]

    def drain(self):
        for copy in self.open:
            copy.wait()
        self.open = []


def place_small(me, vectors, small):
    small[...] = jnp.zeros((16, 1024), f32)
    tile = pl.ds(pl.multiple_of(lax.div(me.fsdp, 4) * 128, 128), 128)
    shifted = pltpu.roll(vectors[...], lax.rem(me.fsdp, 4) * 32, 1)
    for i, row in ((1, 3), (2, 4), (3, 5), (5, 10), (6, 11), (7, 12)):
        small[row : row + 1, tile] = shifted[i : i + 1]
    tile = pl.ds(pl.multiple_of(lax.rem(me.fsdp, 8) * 128, 128), 128)
    for y in range(4):
        small[6 + y : 7 + y, tile] = jnp.where(lax.div(me.fsdp, 8) == y, vectors[4:5, :], 0.0)
    first, ahead = lax.div(me.fsdp * 96, 128), lax.rem(me.fsdp * 96, 128)
    shifted = pltpu.roll(vectors[...], ahead, 1)[0:1]
    behind = lax.broadcasted_iota(jnp.int32, (1, 128), 1) >= ahead
    for at, part in ((first, jnp.where(behind, shifted, 0.0)), (first + 1, jnp.where(behind, 0.0, shifted))):
        tile = pl.ds(pl.multiple_of(lax.rem(at, 8) * 128, 128), 128)
        for y in range(3):
            small[y : y + 1, tile] += jnp.where(lax.div(at, 8) == y, part, 0.0)


def forward_kernel(
    triple, expand, shrink, merger, vectors, tokens, cotangent, cosines, sines,
    whole_t, whole_e, whole_s, whole_m, sequence, small_full, encoded, small_grads,
    e_out, o_out, q_out, k_out, v_out, r_out, ctx_out, n_out, scale_out, low_out,
    active_out, slope_out, second_out, feed_out,
    small, small_x, small_y, small_z, sum_x, sum_y, wt, we, ws, wm, seq, ups,
    e_buf, o_buf, q_buf, k_buf, v_buf, r_buf, ctx, part, give_a, take_a, give_f, take_f,
    n_buf, scale_buf, low_buf, active_buf, slope_buf, second_buf, feed_buf,
    send, recv, local_sems,
):
    me = Place()
    wires, saves = Wires(send, recv), Saves(local_sems)
    sibling = me.at(core=1 - me.core)
    across = me.at(z_lo=1 - me.z_lo)
    partner = me.at(z_hi=1 - me.z_hi, z_lo=1 - me.z_lo)
    peers = [sibling, across, partner]
    peers += [me.at(x=me.along_x(k)) for k in (1, 2, 3)]
    peers += [me.at(y=me.along_y(k)) for k in (1, 2, 3)]
    greet(peers)
    place_small(me, vectors, small)
    meet(peers)

    mine_here = me.core == me.z_hi
    slot_t = wt.at[me.y, me.z_hi, me.x]
    slot_e = we.at[me.y, me.z_hi, me.x]
    slot_s = ws.at[me.y, 0, me.x]
    slot_m = wm.at[me.y, 0, me.x]
    def triple_cuts(z_lo):
        for t in range(3):
            for j in range(2):
                start = pl.multiple_of(t * 1024 + z_lo * 512 + j * 256 + me.core * 128, 128)
                yield triple.at[:, pl.ds(start, 128)], slot_t.at[:, pl.ds((j * 3 + t) * 128, 128)]

    def expand_cuts():
        for i in range(4):
            start = pl.multiple_of(i * 1024 + me.core * 512, 512)
            yield expand.at[:, pl.ds(start, 512)], slot_e.at[:, pl.ds(i * 512, 512)]

    z_t = [wires.go(a, b, partner) for a, b in triple_cuts(1 - me.z_lo)]
    tok_across = wires.go(tokens, seq.at[me.seq], across)
    x_small = [wires.go(small, small_x.at[k - 1], me.at(x=me.along_x(k))) for k in (1, 2, 3)]
    tok_beside = wires.go(tokens, seq.at[me.seq], sibling)
    z_e = [wires.go(a, b, partner) for a, b in expand_cuts()]
    cot_beside = wires.go(cotangent, ups.at[me.core], sibling)
    own_t = [saves.go(a, b) for a, b in triple_cuts(me.z_lo)]
    own_tok = saves.go(tokens, seq.at[me.seq])
    own_e = [saves.go(a, b) for a, b in expand_cuts()]
    own_cot = saves.go(cotangent, ups.at[me.core])
    z_s = wires.make(shrink, slot_s, partner)
    z_m = wires.make(merger, slot_m, partner)
    own_s = pltpu.make_async_copy(shrink, slot_s, local_sems.at[46])
    own_m = pltpu.make_async_copy(merger, slot_m, local_sems.at[47])

    @pl.when(mine_here)
    def _():
        z_s.start()
        z_m.start()
        own_s.start()
        own_m.start()

    go_t = gather_steps(wires, me, wt)
    go_e = gather_steps(wires, me, we)
    go_s = gather_steps(wires, me, ws)
    go_m = gather_steps(wires, me, wm)
    for copy in own_t:
        saves.wait(copy)
    arrive(z_t)
    next(go_t)
    for copy in own_e:
        saves.wait(copy)
    arrive(z_e)
    next(go_e)
    arrive(x_small)
    sum_x[...] = small[...] + small_x[0] + small_x[1] + small_x[2]
    y_small = [wires.go(sum_x, small_y.at[k - 1], me.at(y=me.along_y(k))) for k in (1, 2, 3)]
    next(go_t)

    @pl.when(mine_here)
    def _():
        own_s.wait()
        own_m.wait()

    @pl.when(jnp.logical_not(mine_here))
    def _():
        z_s.wait_recv()
        z_m.wait_recv()

    next(go_s)
    next(go_m)
    next(go_t)
    next(go_e)
    arrive(y_small)
    sum_y[...] = sum_x[...] + small_y[0] + small_y[1] + small_y[2]
    z_small = wires.go(sum_y, small_z, partner)
    next(go_s)
    next(go_m)
    next(go_e)
    next(go_t)
    next(go_m)
    next(go_s)
    z_small.wait_recv()
    small_full[...] = sum_y[...] + small_z[...]
    tok_across.wait_recv()
    far = seq.at[(1 - me.z_lo) * 2 + me.core]
    tok_relay = wires.go(far, far, sibling)
    next(go_t)
    saves.go(wt, whole_t)
    saves.wait(own_tok)
    arrive([tok_beside, tok_relay])

    def bias(row, start, n):
        return small_full[pl.ds(row, 1), pl.ds(pl.multiple_of(start, 128), n)]

    bias_t = [
        bias(t, me.z_lo * 512 + j * 256 + me.core * 128, 128) for j in range(2) for t in range(3)
    ]
    bias_t = jnp.concatenate(bias_t, axis=1)

    def project(i, carry):
        rows = pl.ds(pl.multiple_of(i * 512, 512), 512)
        pre = dot(seq[pl.ds(2 * i, 2)].reshape(512, D), wt[...].reshape(D, 768), NN) + bias_t
        cosine, sine = cosines[rows, :], sines[rows, :]
        for p in range(2):
            cut = pre[:, p * 384 : p * 384 + 128]
            q_buf[p, rows, :] = (turn(cut, cosine, sine) * 0.125).astype(bf16)
            cut = pre[:, p * 384 + 128 : p * 384 + 256]
            k_buf[p, rows, :] = turn(cut, cosine, sine).astype(bf16)
            v_buf[p, rows, pl.ds(0, 128)] = pre[:, p * 384 + 256 : p * 384 + 384].astype(bf16)
            v_buf[p, rows, pl.ds(128, 128)] = jnp.ones((512, 128), bf16)
        return carry

    lax.fori_loop(0, 2, project, 0)
    saves.go(seq, sequence)
    saves.go(q_buf, q_out)
    saves.go(k_buf, k_out)
    saves.go(v_buf, v_out)
    ctx_copies = []
    keeps = []
    for p in range(2):

        def attend(i, carry, p=p):
            rows = pl.ds(pl.multiple_of(i * 512, 512), 512)
            lane = lax.broadcasted_iota(jnp.int32, (512, 128), 1)
            found = []
            for h in range(2):
                head = (lane >= 64) if h else (lane < 64)
                q = jnp.where(head, q_buf[p, rows, :], jnp.zeros((), bf16))
                scores = dot(q, k_buf[p], NT)
                peak = jnp.max(scores, axis=1, keepdims=True)
                powers = jnp.exp(scores - peak).astype(bf16)
                e_buf[2 * p + h, rows, :] = powers
                found.append(dot(powers, v_buf[p], NN))
            first = lane < 64
            over = 1.0 / jnp.where(first, found[0][:, 128:], found[1][:, 128:])
            r_buf[p, rows, :] = over
            o_buf[p, rows, :] = (jnp.where(first, found[0][:, :128], found[1][:, :128]) * over).astype(bf16)
            return carry

        lax.fori_loop(0, 2, attend, 0)
        saves.go(e_buf.at[pl.ds(2 * p, 2)], e_out.at[pl.ds(2 * p, 2)])
        theirs = o_buf.at[p, pl.ds(pl.multiple_of((1 - me.z_lo) * 512, 512), 512)]
        ours = o_buf.at[p, pl.ds(pl.multiple_of(me.z_lo * 512, 512), 512)]
        ctx_copies.append(wires.go(theirs, ctx.at[me.z_lo, p], across))
        keeps.append(saves.go(ours, ctx.at[me.z_lo, p]))
        if p == 0:
            next(go_e)
            next(go_m)
    saves.go(r_buf, r_out)
    saves.go(o_buf, o_out)
    next(go_m)
    saves.go(wm, whole_m)
    for keep in keeps:
        saves.wait(keep)
    arrive(ctx_copies)
    ctx_rows = jnp.concatenate([ctx[0, 0], ctx[0, 1], ctx[1, 0], ctx[1, 1]], axis=1)
    merge = []
    for i in range(2):
        rows = pl.ds(i * 256, 256)
        found = dot(ctx_rows[i * 256 : i * 256 + 256], wm[...].reshape(512, D), NN)
        part[rows, :] = found
        give_a[rows, :] = found.astype(bf16)
        merge.append(wires.go(give_a.at[rows], take_a.at[rows], sibling))
    saves.go(ctx, ctx_out)
    next(go_s)
    next(go_e)
    saves.go(we, whole_e)
    bias_m, gain_1, shift_1 = bias(3, 0, D), bias(4, 0, D), bias(5, 0, D)

    def first_norm(i, carry):
        rows = pl.ds(pl.multiple_of(i * 64, 64), 64)
        at = pl.ds(pl.multiple_of(lax.rem(i, 4) * 64, 64), 64)
        inputs = seq[me.z_lo * 2 + lax.div(i, 4), at, :].astype(f32)
        total = inputs + part[rows, :] + take_a[rows, :].astype(f32) + bias_m
        n, scale = row_norm(total)
        n_buf[rows, :] = n
        scale_buf[rows, :] = jnp.broadcast_to(scale, (64, 128))
        low_buf[rows, :] = (n * gain_1 + shift_1).astype(bf16)
        return carry

    for i in range(2):
        merge[i].wait_recv()
        lax.fori_loop(4 * i, 4 * i + 4, first_norm, 0)
    saves.go(n_buf, n_out)
    saves.go(scale_buf, scale_out)
    saves.go(low_buf, low_out)

    def widen(i, carry):
        at = pl.ds(pl.multiple_of(i * 1024, 1024), 1024)
        upward = dot(low_buf[...], we[:, :, :, :, at].reshape(D, 1024), NN)
        biases = [bias(6 + 2 * i + y, me.core * 512, 512) for y in range(2)]
        upward += jnp.concatenate(biases, axis=1)
        gate = 0.5 + 0.5 * lax.erf(upward * math.sqrt(0.5))
        active_buf[:, at] = (upward * gate).astype(bf16)
        bell = jnp.exp(-0.5 * upward * upward) * (1.0 / math.sqrt(2.0 * math.pi))
        slope_buf[:, at] = (gate + upward * bell).astype(bf16)
        return carry

    lax.fori_loop(0, 1, widen, 0)
    next(go_s)
    saves.go(ws, whole_s)
    lax.fori_loop(1, 2, widen, 0)
    saves.go(active_buf, active_out)
    saves.go(slope_buf, slope_out)
    feeds = []
    for i in range(2):
        rows = pl.ds(i * 256, 256)
        found = dot(active_buf[rows, :], ws[...].reshape(2048, D), NN)
        part[rows, :] = found
        give_f[rows, :] = found.astype(bf16)
        feeds.append(wires.go(give_f.at[rows], take_f.at[rows], sibling))
    saves.wait(own_cot)
    cot_beside.wait_recv()
    bias_s, gain_2, shift_2 = bias(10, 0, D), bias(11, 0, D), bias(12, 0, D)
    small_grads[...] = jnp.zeros((16, 1024), f32)

    def second_norm(i, carry):
        rows = pl.ds(pl.multiple_of(i * 64, 64), 64)
        at = pl.ds(pl.multiple_of(lax.rem(i, 4) * 64, 64), 64)
        hidden = n_buf[rows, :] * gain_1 + shift_1
        total = hidden + part[rows, :] + take_f[rows, :].astype(f32) + bias_s
        n, scale = row_norm(total)
        upstream = ups[lax.div(i, 4), at, :].astype(f32)
        grad = row_norm_backward(upstream, gain_2, n, scale)
        second_buf[rows, :] = grad
        feed = grad.astype(bf16)
        feed_buf[rows, :] = feed

        @pl.when(lax.div(i, 4) == me.core)
        def _():
            encoded[at, :] = (n * gain_2 + shift_2).astype(bf16)
            small_grads[10:11, :] += jnp.sum(feed.astype(f32), axis=0, keepdims=True)
            small_grads[11:12, :] += jnp.sum(upstream * n, axis=0, keepdims=True)
            small_grads[12:13, :] += jnp.sum(upstream, axis=0, keepdims=True)

        return carry

    for i in range(2):
        feeds[i].wait_recv()
        lax.fori_loop(4 * i, 4 * i + 4, second_norm, 0)
    saves.go(second_buf, second_out)
    saves.go(feed_buf, feed_out)
    saves.drain()
    wires.drain()
    assert all(next(steps, "end") == "end" for steps in (go_t, go_e, go_s, go_m))

    @pl.when(mine_here)
    def _():
        z_s.wait_send()
        z_m.wait_send()


def forward_all(triple, expand, shrink, merger, vectors, tokens, cotangent, cosines, sines):
    shape = jax.ShapeDtypeStruct
    shapes = [
        shape((4, 2, 4, 32, 768), bf16),
        shape((4, 2, 4, 32, 2048), bf16),
        shape((4, 1, 4, 128, 1024), bf16),
        shape((4, 1, 4, 32, 1024), bf16),
        shape((4, 256, 1024), bf16),
        shape((16, 1024), f32),
        shape((256, 1024), bf16),
        shape((16, 1024), f32),
        shape((4, 1024, 1024), bf16),
        shape((2, 1024, 128), bf16),
        shape((2, 1024, 128), bf16),
        shape((2, 1024, 128), bf16),
        shape((2, 1024, 256), bf16),
        shape((2, 1024, 128), f32),
        shape((2, 2, 512, 128), bf16),
        shape((512, 1024), f32),
        shape((512, 128), f32),
        shape((512, 1024), bf16),
        shape((512, 2048), bf16),
        shape((512, 2048), bf16),
        shape((512, 1024), f32),
        shape((512, 1024), bf16),
    ]
    scratch = [
        pltpu.VMEM((16, 1024), f32),
        pltpu.VMEM((3, 16, 1024), f32),
        pltpu.VMEM((3, 16, 1024), f32),
        pltpu.VMEM((16, 1024), f32),
        pltpu.VMEM((16, 1024), f32),
        pltpu.VMEM((16, 1024), f32),
        pltpu.VMEM((4, 2, 4, 32, 768), bf16),
        pltpu.VMEM((4, 2, 4, 32, 2048), bf16),
        pltpu.VMEM((4, 1, 4, 128, 1024), bf16),
        pltpu.VMEM((4, 1, 4, 32, 1024), bf16),
        pltpu.VMEM((4, 256, 1024), bf16),
        pltpu.VMEM((2, 256, 1024), bf16),
        pltpu.VMEM((4, 1024, 1024), bf16),
        pltpu.VMEM((2, 1024, 128), bf16),
        pltpu.VMEM((2, 1024, 128), bf16),
        pltpu.VMEM((2, 1024, 128), bf16),
        pltpu.VMEM((2, 1024, 256), bf16),
        pltpu.VMEM((2, 1024, 128), f32),
        pltpu.VMEM((2, 2, 512, 128), bf16),
        pltpu.VMEM((512, 1024), f32),
        pltpu.VMEM((512, 1024), bf16),
        pltpu.VMEM((512, 1024), bf16),
        pltpu.VMEM((512, 1024), bf16),
        pltpu.VMEM((512, 1024), bf16),
        pltpu.VMEM((512, 1024), f32),
        pltpu.VMEM((512, 128), f32),
        pltpu.VMEM((512, 1024), bf16),
        pltpu.VMEM((512, 2048), bf16),
        pltpu.VMEM((512, 2048), bf16),
        pltpu.VMEM((512, 1024), f32),
        pltpu.VMEM((512, 1024), bf16),
        pltpu.SemaphoreType.DMA((104,)),
        pltpu.SemaphoreType.DMA((104,)),
        pltpu.SemaphoreType.DMA((48,)),
    ]
    return pl.pallas_call(
        forward_kernel,
        out_shape=shapes,
        in_specs=[ANY, ANY, ANY, ANY, VMEM, ANY, ANY, VMEM, VMEM],
        out_specs=[ANY] * 5 + [VMEM] * 3 + [ANY] * 14,
        scratch_shapes=scratch,
        compiler_params=pltpu.CompilerParams(
            collective_id=0, has_side_effects=True, vmem_limit_bytes=58 << 20
        ),
        name="forward",
    )(triple, expand, shrink, merger, vectors, tokens, cotangent, cosines, sines)


NN = ((1,), (0,))
NT = ((1,), (1,))
TN = ((0,), (0,))


def reduce_steps(wires, me, grad, buffers, out):
    first_l, first_r, mid_l, mid_r, last_l, last_r = buffers
    levels, half, h = grad.shape[1], grad.shape[4] // 2, grad.shape[3] // 2
    left, right = pl.ds(0, half), pl.ds(half, half)
    upper, lower = pl.ds(0, h), pl.ds(h, h)
    on_x = (me.x, lambda i: me.at(x=i))
    on_y = (me.y, lambda i: me.at(y=i))

    def in_mid_l(n, r, value):
        mid_l[lax.div(n, levels), lax.rem(n, levels), r, :] = value

    def in_mid_r(n, r, value):
        mid_r[lax.div(n, 4), lax.rem(n, 4), r, :] = value

    def in_out_l(n, r, value):
        out[n, r, left] = value

    def in_out_r(n, r, value):
        out[n, r, right] = value

    hops = (
        (
            (
                *on_x, 4 * levels, lambda n: (lax.div(n, levels), lax.rem(n, levels)), first_l,
                lambda d, r: grad.at[:, :, d, r, left],
                lambda d, n, r: grad[lax.div(n, levels), lax.rem(n, levels), d, r, left],
                in_mid_l,
            ),
            (
                *on_y, 4 * levels, lambda n: (lax.div(n, 4), lax.rem(n, 4)), first_r,
                lambda d, r: grad.at[d, :, :, r, right],
                lambda d, n, r: grad[d, lax.div(n, 4), lax.rem(n, 4), r, right],
                in_mid_r,
            ),
        ),
        (
            (
                *on_y, levels, lambda n: (n,), last_l,
                lambda d, r: mid_l.at[d, :, r, :],
                lambda d, n, r: mid_l[d, n, r, :],
                in_out_l,
            ),
            (
                *on_x, levels, lambda n: (n,), last_r,
                lambda d, r: mid_r.at[:, d, r, :],
                lambda d, n, r: mid_r[n, d, r, :],
                in_out_r,
            ),
        ),
    )
    for hop in hops:
        sent = []
        for here, device, count, index, (relay, near, far), piece, value, store in hop:
            up, down, corner = lax.rem(here + 1, 4), lax.rem(here + 3, 4), lax.rem(here + 2, 4)
            sent.append(
                (
                    wires.go(piece(corner, upper), relay.at[0], device(up)),
                    wires.go(piece(corner, lower), relay.at[1], device(down)),
                    wires.go(piece(up, lower), near.at[0], device(up)),
                    wires.go(piece(down, upper), near.at[1], device(down)),
                )
            )
        yield
        summed = []
        for (here, device, count, index, (relay, near, far), piece, value, store), copies in zip(hop, sent):
            up, down = lax.rem(here + 1, 4), lax.rem(here + 3, 4)
            arrive(copies[:2])

            def pass_on(n, carry, relay=relay, value=value, index=index, up=up, down=down):
                at = (0, *index(n))
                relay[at] = (relay[at].astype(f32) + value(up, n, upper).astype(f32)).astype(bf16)
                at = (1, *index(n))
                relay[at] = (relay[at].astype(f32) + value(down, n, lower).astype(f32)).astype(bf16)
                return carry

            lax.fori_loop(0, count, pass_on, 0)
            summed.append(wires.go(relay.at[0], far.at[0], device(up)))
            summed.append(wires.go(relay.at[1], far.at[1], device(down)))
        yield
        arrive(summed)
        for (here, device, count, index, (relay, near, far), piece, value, store), copies in zip(hop, sent):
            arrive(copies[2:])

            def finish(n, carry, near=near, far=far, value=value, index=index, store=store, here=here):
                for r, i in ((upper, 0), (lower, 1)):
                    total = value(here, n, r).astype(f32)
                    total += near[(1 - i, *index(n))].astype(f32) + far[(i, *index(n))].astype(f32)
                    store(n, r, total.astype(bf16))
                return carry

            lax.fori_loop(0, count, finish, 0)
    yield


def reduce_scratch(levels, rows, columns):
    half, h = columns // 2, rows // 2

    def trio(*lead):
        return [pltpu.VMEM((2, *lead, h, half), bf16)] * 3

    return [
        *trio(4, levels),
        *trio(levels, 4),
        pltpu.VMEM((4, levels, rows, half), bf16),
        pltpu.VMEM((levels, 4, rows, half), bf16),
        *trio(levels),
        *trio(levels),
        pltpu.VMEM((levels, rows, columns), bf16),
    ]


def reduce_job(wires, me, grad, scratch):
    buffers = (scratch[0:3], scratch[3:6], scratch[6], scratch[7], scratch[8:11], scratch[11:14])
    return reduce_steps(wires, me, grad, buffers, scratch[14])


def triple_steps(wires, me, grad, first_l, first_r, mid_l, mid_r, last_l, last_r, out, shares):
    upper, lower = pl.ds(0, 16), pl.ds(16, 16)
    one = []
    for k in (2, 1, 3):
        x, y = me.along_x(k), me.along_y(k)
        one.append(wires.go(grad.at[:, :, x, upper, :], first_l.at[k - 1], me.at(x=x)))
        one.append(wires.go(grad.at[y, :, :, lower, :], first_r.at[k - 1], me.at(y=y)))
    yield
    arrive(one)

    def total(n, carry):
        y, z = lax.div(n, 2), lax.rem(n, 2)
        left = grad[y, z, me.x, upper, :].astype(f32)
        right = grad[me.y, z, y, lower, :].astype(f32)
        for k in range(3):
            left += first_l[k, y, z].astype(f32)
            right += first_r[k, z, y].astype(f32)
        mid_l[y, z] = left.astype(bf16)
        mid_r[z, y] = right.astype(bf16)
        return carry

    lax.fori_loop(0, 8, total, 0)
    two = []
    for k in range(1, 8):
        z = 1 - me.z_hi if k % 2 else me.z_hi
        x, y = me.along_x(k // 2), me.along_y(k // 2)
        two.append(wires.go(mid_l.at[y, z], last_l.at[k - 1], me.at(y=y, z_hi=z)))
        two.append(wires.go(mid_r.at[z, x], last_r.at[k - 1], me.at(x=x, z_hi=z)))
    yield
    arrive(two)
    left = mid_l[me.y, me.z_hi].astype(f32)
    right = mid_r[me.z_hi, me.x].astype(f32)
    for k in range(7):
        left += last_l[k].astype(f32)
        right += last_r[k].astype(f32)
    out[me.seq, upper, :] = left.astype(bf16)
    out[me.seq, lower, :] = right.astype(bf16)
    spread = [wires.go(out.at[me.seq], out.at[me.seq], peer) for peer in shares]
    yield
    arrive(spread)
    yield


def triple_scratch():
    return [
        pltpu.VMEM((4, 2, 4, 32, 384), bf16),
        pltpu.VMEM((3, 4, 2, 16, 384), bf16),
        pltpu.VMEM((3, 2, 4, 16, 384), bf16),
        pltpu.VMEM((4, 2, 16, 384), bf16),
        pltpu.VMEM((2, 4, 16, 384), bf16),
        pltpu.VMEM((7, 16, 384), bf16),
        pltpu.VMEM((7, 16, 384), bf16),
    ]


def small_steps(wires, me, sums, by_x, by_y, by_z, by_core, out):
    got = [wires.go(sums.at[0], by_x.at[k - 1], me.at(x=me.along_x(k))) for k in (1, 2, 3)]
    yield
    arrive(got)
    sums[1] = sums[0] + by_x[0] + by_x[1] + by_x[2]
    got = [wires.go(sums.at[1], by_y.at[k - 1], me.at(y=me.along_y(k))) for k in (1, 2, 3)]
    yield
    arrive(got)
    sums[2] = sums[1] + by_y[0] + by_y[1] + by_y[2]
    got = [wires.go(sums.at[2], by_z.at[k], peer) for k, peer in enumerate(me.z_others())]
    yield
    arrive(got)
    sums[3] = sums[2] + by_z[0] + by_z[1] + by_z[2]
    got = wires.go(sums.at[3], by_core, me.at(core=1 - me.core))
    yield
    got.wait_recv()
    out[...] = sums[3] + by_core[...]
    yield


def small_scratch(rows):
    return [
        pltpu.VMEM((4, rows, 1024), f32),
        pltpu.VMEM((3, rows, 1024), f32),
        pltpu.VMEM((3, rows, 1024), f32),
        pltpu.VMEM((3, rows, 1024), f32),
        pltpu.VMEM((rows, 1024), f32),
    ]


def backward_kernel(
    whole_t, whole_e, whole_s, whole_m, sequence, small_full, small_part,
    e_in, o_in, q_in, k_in, v_in, r_in, ctx_in, n_in, scale_in, low_in,
    active_in, slope_in, second_in, feed_in, cosines, sines,
    tokens_out, sum_s, sum_e, sum_m, sum_t, small_out, bias_out, *rest,
):
    me = Place()
    scratch_s, scratch_e, scratch_m = (rest[15 * i : 15 * i + 15] for i in range(3))
    scratch_t = (rest[45:52], rest[52:59])
    scratch_small, scratch_bias = rest[59:64], rest[64:69]
    sums, biases = scratch_small[0], scratch_bias[0]
    (
        z_s, z_e, z_m,
        wt, we, ws, wm, e_buf, o_buf, q_buf, k_buf, v_buf, r_buf, ctx, n_buf, scale_buf,
        low_buf, active_buf, slope_buf, second_buf, feed_buf, part, take_a,
        give_c, dctx, dq_buf, pre_grad, take_t, take_x, send, recv, local_sems,
    ) = rest[69:]
    give_a = feed_buf
    acc_k, acc_v = second_buf.at[pl.ds(0, 128)], second_buf.at[pl.ds(128, 128)]
    give_t = [active_buf.at[pl.ds(256 * z, 256), pl.ds(0, D)] for z in range(2)]
    give_x = active_buf.at[pl.ds(0, 256), pl.ds(D, D)]
    wires, saves = Wires(send, recv), Saves(local_sems)
    sibling = me.at(core=1 - me.core)
    beside, diagonal, beyond = me.z_others()
    load_first = [
        saves.go(feed_in, feed_buf), saves.go(whole_s, ws), saves.go(slope_in, slope_buf),
        saves.go(active_in, active_buf),
    ]
    crossing = me.at(z_lo=1 - me.z_lo, core=1 - me.core)
    peers = [sibling, beside, diagonal, beyond, crossing]
    for z in (me.z_hi, 1 - me.z_hi):
        peers += [me.at(x=me.along_x(k), z_hi=z) for k in (1, 2, 3)]
        peers += [me.at(y=me.along_y(k), z_hi=z) for k in (1, 2, 3)]
    greet(peers)
    go_s = reduce_job(wires, me, ws, scratch_s)
    go_e = reduce_job(wires, me, we, scratch_e)
    go_m = reduce_job(wires, me, wm, scratch_m)
    plane_s, plane_e, plane_m = (s[14] for s in (scratch_s, scratch_e, scratch_m))
    go_small = small_steps(wires, me, *scratch_small, small_out)
    go_bias = small_steps(wires, me, *scratch_bias, bias_out)
    biases[0] = jnp.zeros((8, 1024), f32)
    go_t = [
        triple_steps(wires, me, *scratch_t[p], sum_t.at[p], (sibling, beside, crossing))
        for p in range(2)
    ]
    sums[0] = small_part[...]

    for load in load_first:
        saves.wait(load)
    load_e, load_low = saves.go(whole_e, we), saves.go(low_in, low_buf)
    load_norm = [saves.go(n_in, n_buf), saves.go(scale_in, scale_buf), saves.go(second_in, second_buf)]
    load_m = [saves.go(whole_m, wm), saves.go(ctx_in, ctx)]

    def narrow(y, carry):
        at = pl.ds(pl.multiple_of(y * 512, 512), 512)
        back = dot(feed_buf[...], ws[y].reshape(512, D), NT)
        up = (back * slope_buf[:, at].astype(f32)).astype(bf16)
        slope_buf[:, at] = up
        where = pl.ds(pl.multiple_of(me.core * 512, 512), 512)
        sums[0, pl.ds(6 + y, 1), where] = jnp.sum(up.astype(f32), axis=0, keepdims=True)
        ws[y] = dot(active_buf[:, at], feed_buf[...], TN).astype(bf16).reshape(1, 4, 128, D)
        return carry

    lax.fori_loop(0, 4, narrow, 0)
    load_seq = [
        saves.go(sequence.at[pl.ds(512 * i, 512)], active_buf.at[:, pl.ds(D * i, D)]) for i in range(2)
    ]
    meet(peers)
    next(go_s)
    saves.wait(load_e)

    def hidden_part(i, carry):
        at = pl.ds(pl.multiple_of(i * 512, 512), 512)
        found = dot(slope_buf[...], we[pl.ds(2 * i, 2)].reshape(512, 2048), NT)
        part[:, at] = found
        give_a[:, at] = found.astype(bf16)
        return carry

    shared = []
    for i in range(2):
        lax.fori_loop(i, i + 1, hidden_part, 0)
        at = pl.ds(512 * i, 512)
        shared.append(wires.go(give_a.at[:, at], take_a.at[:, at], sibling))
    saves.wait(load_low)
    load_heads = [
        saves.go(e_in.at[0], e_buf.at[0]), saves.go(e_in.at[1], e_buf.at[1]), saves.go(o_in, o_buf),
        saves.go(q_in, q_buf), saves.go(k_in, k_buf), saves.go(v_in, v_buf), saves.go(r_in, r_buf),
    ]
    load_t = saves.go(whole_t, wt)

    def expand_part(y, carry):
        low = low_buf[:, pl.ds(pl.multiple_of(y * 256, 256), 256)]
        we[y] = dot(low, slope_buf[...], TN).astype(bf16).reshape(2, 4, 32, 2048)
        return carry

    lax.fori_loop(0, 2, expand_part, 0)
    for load in load_norm:
        saves.wait(load)
    wires.finish(shared)
    turned_buf = give_a
    gain_1 = small_full[4:5, :]

    def first_norm(i, carry):
        rows = pl.ds(pl.multiple_of(i * 64, 64), 64)
        upstream = part[rows, :] + take_a[rows, :].astype(f32) + second_buf[rows, :]
        n = n_buf[rows, :]
        grad = row_norm_backward(upstream, gain_1, n, scale_buf[rows, 0:1])
        n_buf[rows, :] = grad
        low = grad.astype(bf16)
        turned_buf[rows, :] = low

        @pl.when(lax.div(i, 4) == me.core)
        def _():
            sums[0, 3:4, :] += jnp.sum(low.astype(f32), axis=0, keepdims=True)
            sums[0, 4:5, :] += jnp.sum(upstream * n, axis=0, keepdims=True)
            sums[0, 5:6, :] += jnp.sum(upstream, axis=0, keepdims=True)

        return carry

    lax.fori_loop(0, 8, first_norm, 0)
    next(go_small)
    for load in load_m:
        saves.wait(load)

    def context_part(group):
        return dot(turned_buf[...], wm[pl.ds(2 * group, 2)].reshape(256, D), NT).astype(bf16)

    found = context_part(1 - me.z_lo)
    give_c[0] = found[:, :128]
    give_c[1] = found[:, 128:]
    chip = pl.ds(pl.multiple_of(me.z_lo * 512, 512), 512)
    swapped = wires.go(give_c, dctx.at[:, chip, :], beside)
    found = context_part(me.z_lo)
    dctx[0, chip, :] = found[:, :128]
    dctx[1, chip, :] = found[:, 128:]
    lax.fori_loop(2, 4, expand_part, 0)
    next(go_s)
    next(go_e)
    for z in range(2):
        for p in range(2):
            found = dot(ctx[z, p], turned_buf[...], TN).astype(bf16)
            wm[2 * z + p] = found.reshape(1, 4, 32, D)
    next(go_m)
    for load in load_heads:
        saves.wait(load)
    swapped.wait_recv()

    def head_back(p, h):
        slot = h

        def block(i, carry):
            rows = pl.ds(pl.multiple_of(i * 512, 512), 512)
            lane = lax.broadcasted_iota(jnp.int32, (512, 128), 1)
            head = (lane >= 64) if h else (lane < 64)
            scaled = jnp.where(head, dctx[p, rows, :].astype(f32) * r_buf[p, rows, :], 0.0).astype(bf16)
            delta = jnp.sum(scaled.astype(f32) * o_buf[p, rows, :].astype(f32), axis=1, keepdims=True)
            high = delta.astype(bf16).astype(f32)
            extra = jnp.where(lane == 0, -high, jnp.where(lane == 1, high - delta, 0.0)).astype(bf16)
            given = jnp.concatenate([scaled, extra], axis=1)
            prob_grad = dot(given, v_buf[p], NT)
            powers = e_buf[slot, rows, :]
            score_grad = (powers.astype(f32) * prob_grad).astype(bf16)
            dq = dot(score_grad, k_buf[p], NN)
            if h == 0:
                dq_buf[rows, :] = dq
            else:
                dq = jnp.where(lane < 64, dq_buf[rows, :], dq)
                dq = (dq * 0.125).astype(bf16).astype(f32)
                turned = turn(dq, cosines[rows, :], -sines[rows, :])
                pre_grad[p, rows, pl.ds(0, 128)] = turned.astype(bf16)
            q = jnp.where(head, q_buf[p, rows, :], jnp.zeros((), bf16))
            acc_k[...] += dot(q, score_grad, TN)
            acc_v[...] += dot(scaled, powers, TN)
            return carry

        lax.fori_loop(0, 2, block, 0)

    def pair_end(p):
        def block(i, carry):
            rows = pl.ds(pl.multiple_of(i * 256, 256), 256)
            dk = acc_k[:, rows].T.astype(bf16).astype(f32)
            turned = turn(dk, cosines[rows, :], -sines[rows, :])
            pre_grad[p, rows, pl.ds(128, 128)] = turned.astype(bf16)
            pre_grad[p, rows, pl.ds(256, 128)] = acc_v[:, rows].T.astype(bf16)
            return carry

        lax.fori_loop(0, 4, block, 0)
        found = dot(active_buf[:, 0:D], pre_grad[p, 0:512, :], TN)
        found += dot(active_buf[:, D:], pre_grad[p, 512:, :], TN)
        scratch_t[p][0][...] = found.astype(bf16).reshape(4, 2, 4, 32, 384)
        next(go_t[p])

    def bias_part(p):
        def block(i, total):
            rows = pl.ds(pl.multiple_of(i * 256, 256), 256)
            return total + jnp.sum(pre_grad[p, rows, :].astype(f32), axis=0, keepdims=True)

        total = lax.fori_loop(0, 4, block, jnp.zeros((1, 384), f32))
        at = pl.ds(pl.multiple_of(me.z_lo * 512 + p * 256 + me.core * 128, 128), 128)
        for t in range(3):
            biases[0, t : t + 1, at] = total[:, t * 128 : t * 128 + 128]

    def clear():
        acc_k[...] = jnp.zeros((128, D), f32)
        acc_v[...] = jnp.zeros((128, D), f32)

    clear()
    head_back(0, 0)
    load_2 = saves.go(e_in.at[2], e_buf.at[0])
    next(go_small)
    head_back(0, 1)
    load_3 = saves.go(e_in.at[3], e_buf.at[1])
    next(go_e)
    for load in load_seq:
        saves.wait(load)
    pair_end(0)
    clear()
    next(go_small)
    saves.wait(load_2)
    head_back(1, 0)
    next(go_s)
    next(go_m)
    saves.wait(load_3)
    head_back(1, 1)
    pair_end(1)
    saves.wait(load_t)

    def tokens_part(z, core):
        rows = pl.ds(pl.multiple_of((2 * z + core) * 256, 256), 256)
        found = dot(pre_grad[0, rows, :], wt[:, :, :, :, 0:384].reshape(D, 384), NT)
        return found + dot(pre_grad[1, rows, :], wt[:, :, :, :, 384:768].reshape(D, 384), NT)

    beside_rows = []
    for i, z in enumerate((1 - me.z_lo, me.z_lo)):
        give_t[i][...] = tokens_part(z, 1 - me.core).astype(bf16)
        beside_rows.append(wires.go(give_t[i], take_t.at[i], sibling))
        if i == 0:
            far_rows = tokens_part(z, me.core)
            beside_rows[0].wait_recv()
            give_x[...] = (far_rows + take_t[0].astype(f32)).astype(bf16)
            across_rows = wires.go(give_x, take_x, beside)
    bias_part(0)
    bias_part(1)
    next(go_bias)
    part[0:256, :] = tokens_part(me.z_lo, me.core)
    next(go_t[0])
    next(go_e)
    next(go_s)
    next(go_m)
    next(go_t[1])
    next(go_small)
    next(go_bias)
    next(go_t[0])
    next(go_s)
    owner = me.core == me.z_hi
    late = []

    def to_owners(plane, slots):
        copies = [
            wires.make(plane.at[0], slots.at[k], peer)
            for k, peer in enumerate((beside, diagonal, beyond))
        ]

        @pl.when(owner)
        def _():
            copies[0].start()

        @pl.when(jnp.logical_not(owner))
        def _():
            copies[1].start()
            copies[2].start()

        late.append(copies)
        return copies

    def finish_owned(plane, slots, copies, out):
        beside_copy = wires.make(out, out, sibling)

        @pl.when(owner)
        def _():
            arrive(copies)
            total = plane[0].astype(f32)
            for k in range(3):
                total += slots[k].astype(f32)
            out[...] = total.astype(bf16)
            beside_copy.start()

        return beside_copy

    copies_s = to_owners(plane_s, z_s)
    next(go_e)
    next(go_m)
    next(go_t[1])
    next(go_small)
    next(go_bias)
    next(go_e)
    flip = 1 - me.z_hi
    copies_e = [
        wires.go(plane_e.at[level], z_e.at[k], peer)
        for k, (level, peer) in enumerate(((me.z_hi, beside), (flip, diagonal), (flip, beyond)))
    ]
    next(go_m)
    copies_m = to_owners(plane_m, z_m)
    beside_s = finish_owned(plane_s, z_s, copies_s, sum_s)
    arrive(copies_e)
    total = plane_e[me.z_hi].astype(f32)
    for k in range(3):
        total += z_e[k].astype(f32)
    sum_e[me.core] = total.astype(bf16)
    beside_e = wires.go(sum_e.at[me.core], sum_e.at[me.core], sibling)
    beside_m = finish_owned(plane_m, z_m, copies_m, sum_m)
    next(go_bias)
    arrive([across_rows, beside_rows[1]])
    own = pl.ds(pl.multiple_of(me.core * 256, 256), 256)
    tokens_out[...] = (
        part[0:256, :] + take_t[1].astype(f32) + take_x[...].astype(f32) + n_buf[own, :]
    ).astype(bf16)
    next(go_t[0])
    next(go_t[1])
    next(go_bias)

    @pl.when(jnp.logical_not(owner))
    def _():
        beside_s.wait_recv()
        beside_m.wait_recv()
        for copies in late:
            copies[1].wait_send()
            copies[2].wait_send()

    @pl.when(owner)
    def _():
        beside_s.wait_send()
        beside_m.wait_send()
        for copies in late:
            copies[0].wait_send()

    beside_e.wait_recv()
    wires.drain()
    saves.drain()
    assert all(next(steps, "end") == "end" for steps in (go_s, go_e, go_m, *go_t, go_small, go_bias))


def backward_all(*operands):
    shape = jax.ShapeDtypeStruct
    shapes = [
        shape((256, 1024), bf16),
        shape((128, 1024), bf16),
        shape((2, 32, 2048), bf16),
        shape((32, 1024), bf16),
        shape((2, 4, 32, 384), bf16),
        shape((16, 1024), f32),
        shape((8, 1024), f32),
    ]

    def low(*dims):
        return pltpu.VMEM(dims, bf16)

    def wide(*dims):
        return pltpu.VMEM(dims, f32)

    scratch = [
        *reduce_scratch(1, 128, 1024),
        *reduce_scratch(2, 32, 2048),
        *reduce_scratch(1, 32, 1024),
        *triple_scratch(),
        *triple_scratch(),
        *small_scratch(16),
        *small_scratch(8),
        low(3, 128, 1024), low(3, 32, 2048), low(3, 32, 1024),
        low(4, 2, 4, 32, 768), low(4, 2, 4, 32, 2048), low(4, 1, 4, 128, 1024), low(4, 1, 4, 32, 1024),
        low(2, 1024, 1024), low(2, 1024, 128), low(2, 1024, 128), low(2, 1024, 128),
        low(2, 1024, 256), wide(2, 1024, 128), low(2, 2, 512, 128), wide(512, 1024), wide(512, 128),
        low(512, 1024), low(512, 2048), low(512, 2048), wide(512, 1024), low(512, 1024),
        wide(512, 1024), low(512, 1024),
        low(2, 512, 128), low(2, 1024, 128), wide(1024, 128),
        low(2, 1024, 384),
        low(2, 256, 1024), low(256, 1024),
        pltpu.SemaphoreType.DMA((160,)),
        pltpu.SemaphoreType.DMA((160,)),
        pltpu.SemaphoreType.DMA((24,)),
    ]
    return pl.pallas_call(
        backward_kernel,
        out_shape=shapes,
        in_specs=[ANY] * 5 + [VMEM] * 2 + [ANY] * 14 + [VMEM] * 2,
        out_specs=[VMEM] * 7,
        scratch_shapes=scratch,
        compiler_params=pltpu.CompilerParams(
            collective_id=1, has_side_effects=True, vmem_limit_bytes=61 << 20
        ),
        name="backward",
    )(*operands)


def finish_kernel(tokens, encoded, sum_s, sum_e, sum_m, sum_t, *rest):
    tokens_out, encoded_out, out_s, out_e, out_m, out_t = rest
    tokens_out[...] = tokens[...]
    encoded_out[...] = encoded[...]
    out_s[...] = sum_s[...].astype(f32)
    out_m[...] = sum_m[...].astype(f32)
    for c in range(2):
        for y in range(4):
            start = y * 1024 + c * 512
            out_e[:, start : start + 512] = sum_e[c, :, y * 512 : y * 512 + 512].astype(f32)
    for s in range(4):
        for t in range(3):
            for j in range(2):
                start = t * 1024 + (s // 2) * 512 + j * 256 + (s % 2) * 128
                out_t[:, start : start + 128] = sum_t[j, s, :, t * 128 : t * 128 + 128].astype(f32)


def finish_all(*operands):
    shape = jax.ShapeDtypeStruct
    shapes = [
        shape((256, 1024), bf16),
        shape((256, 1024), bf16),
        shape((128, 1024), f32),
        shape((32, 4096), f32),
        shape((32, 1024), f32),
        shape((32, 3072), f32),
    ]
    return pl.pallas_call(
        finish_kernel,
        out_shape=shapes,
        in_specs=[VMEM] * 6,
        out_specs=[VMEM] * 6,
        compiler_params=pltpu.CompilerParams(vmem_limit_bytes=60 << 20),
        name="finish",
    )(*operands)


def local(
    tokens, triple, triple_bias, merger, merger_bias, first_gain, first_shift,
    expand, expand_bias, shrink, shrink_bias, second_gain, second_shift, cotangent,
):
    me = Place()
    vectors = (
        triple_bias, merger_bias, first_gain, first_shift, expand_bias, shrink_bias, second_gain, second_shift,
    )
    gaps = [jnp.zeros((128 - v.shape[0],), f32) for v in vectors]
    vectors = jnp.concatenate([x for v, gap in zip(vectors, gaps) for x in (v.astype(f32), gap) if x.shape[0]])
    vectors = vectors.reshape(8, 128)
    inverse = 10000.0 ** (-2.0 * np.arange(32) / 64)
    angles = np.arange(LENGTH)[:, None] * inverse[None, :]
    cosines = jnp.asarray(np.tile(np.cos(angles), (1, 4)), f32)
    sines = jnp.asarray(np.tile(np.concatenate([-np.sin(angles), np.sin(angles)], axis=1), (1, 2)), f32)
    (
        whole_t, whole_e, whole_s, whole_m, sequence, small, encoded, small_part, *kept,
    ) = forward_all(
        triple, expand, shrink, merger, vectors, tokens.reshape(256, D),
        cotangent.reshape(256, D), cosines, sines,
    )
    tokens_grad, sum_s, sum_e, sum_m, sum_t, small_sum, bias_sum = backward_all(
        whole_t, whole_e, whole_s, whole_m, sequence.reshape(LENGTH, D), small, small_part, *kept, cosines, sines
    )
    tokens_grad, encoded, shrink_grad, expand_grad, merger_grad, triple_grad = finish_all(
        tokens_grad, encoded, sum_s, sum_e, sum_m, sum_t
    )
    flat = small_sum.reshape(-1)

    def shard(start, n):
        return lax.dynamic_slice(flat, (start + me.fsdp * n,), (n,))

    return (
        encoded.reshape(1, 256, D),
        tokens_grad.reshape(1, 256, D),
        triple_grad,
        lax.dynamic_slice(bias_sum.reshape(-1), (me.fsdp * 96,), (96,)),
        merger_grad,
        shard(3072, 32),
        shard(4096, 32),
        shard(5120, 32),
        expand_grad,
        shard(6144, 128),
        shrink_grad,
        shard(10240, 32),
        shard(11264, 32),
        shard(12288, 32),
    )


def solution(mesh):
    rows = P("fsdp", "seq", None)
    matrix = P("fsdp", None)
    vector = P("fsdp")
    return jax.shard_map(
        local,
        mesh=mesh,
        in_specs=(
            rows, matrix, vector, matrix, vector, vector, vector, matrix, vector, matrix, vector,
            vector, vector, rows,
        ),
        out_specs=(
            rows, rows, matrix, vector, matrix, vector, vector, vector, matrix, vector, matrix,
            vector, vector, vector,
        ),
        check_vma=False,
    )
```
